256 devices in a mesh: label: 128 (over x, y_lo, z, core), dp: 2 (over y_hi).
Axes of the slice: x: 4, y: 4 (y_hi: 2, y_lo: 2; y = y_hi * 2 + y_lo), z: 8, core: 2. Of those that a mesh axis runs over, the one named last changes fastest.
Arguments:
- queries: bfloat16 [4096, 512], P(('label', 'dp')), may hold values from -9 to 9
- positives: int32 [4096, 8], P(('label', 'dp')), may hold values from -1 to 131071, as said below
- weights: float32 [131072, 512], P('label'), may hold values from -4 to 4
- first_moment: float32 [131072, 512], P('label'), may hold values from -1.8 to 1.8
- second_moment: float32 [131072, 512], P('label'), may hold values from 0.05 to 1
Outputs:
- new_weights: float32 [131072, 512], P('label')
- new_first: float32 [131072, 512], P('label')
- new_second: float32 [131072, 512], P('label')
- query_grads: float32 [2, 4096, 512], P(None, ('label', 'dp'))
The draws below stay inside these ranges and needn't reach their ends.
Inputs may be any that keep to these rules, and one draw needn't show every extreme that they name: `positives`: each row lists its query's positive label ids (one to 8) first and -1 in the unused slots after them; ids may repeat within a row.
All inputs are finite; a program needn't handle non-finite values.
Results may differ from the reference program's by a relative error of at most 0.0023.
Values may be sent and summed in bfloat16 or wider, within the bound.
No kernel may reach another device: no remote copies, remote signals or barrier semaphores. Data moves between devices by JAX's collectives and lax.ppermute only.
A program may use at most 128 MiB of HBM per device.

```python
import math
import jax
import jax.numpy as jnp
from jax import lax

D = 512
LAB_DEV = 1024
STEPS = 2
MAXPOS = 8
LABELS = 131072
QUERIES = 4096


def shared_direction(key):
    signs = jax.random.rademacher(jax.random.fold_in(key, 101), (D,), dtype=jnp.float32)
    return signs * D ** (-0.5)


def draw_queries(key, part):
    direction = shared_direction(key)
    key = jax.random.fold_in(key, 3)
    noise = jnp.clip(jax.random.normal(key, (QUERIES, D), jnp.float32), -5.0, 5.0)
    return (noise + 4.0 * direction[None, :]).astype(jnp.bfloat16)


def draw_weights(key, part):
    direction = shared_direction(key)
    key = jax.random.fold_in(key, 5)
    noise = jnp.clip(jax.random.normal(key, (LABELS, D), jnp.float32), -5.0, 5.0)
    return (noise * (4.0 * D ** (-0.5)) - 2.0 * direction[None, :]).astype(jnp.float32)


def draw_positives(key, part):
    key = jax.random.fold_in(key, 7)
    key_ids, key_counts = jax.random.split(key)
    label_ids = jax.random.randint(key_ids, (QUERIES, MAXPOS), 0, LABELS)
    counts = jax.random.randint(key_counts, (QUERIES, 1), 1, MAXPOS + 1)
    first_row = jnp.arange(QUERIES)[:, None] == 0
    counts = jnp.where(first_row, 1, counts)
    slots = jnp.arange(MAXPOS)[None, :]
    return jnp.where(slots < counts, label_ids, -1).astype(jnp.int32)


def shard_levels(key, dims, cuts, low, high):
    gain = 1.0
    for axis_at, blocks in cuts:
        draws = jax.random.uniform(jax.random.fold_in(jax.random.fold_in(key, 6), axis_at), (blocks,), jnp.float32, low / len(cuts), high / len(cuts))
        gain = gain * jnp.repeat(jnp.exp(draws), dims[axis_at] // blocks).reshape((-1,) + (1,) * (len(dims) - 1 - axis_at))
    return gain


def bell_draw(key, extent, width, reach, cuts=(), kind=jnp.bfloat16):
    result = jax.random.normal(key, extent, jnp.float32) * width
    if len(cuts) > 0:
        result = shard_levels(key, extent, cuts, -0.22, 0.18) * result
    return jnp.clip(result, min=-reach, max=reach).astype(kind)


def setup_inputs(seed: int = 0) -> dict:
    streams_of = jax.random.split(jax.random.key(seed), 6)
    return {
        "queries": draw_queries(jax.random.fold_in(streams_of[5], 71), 0),
        "positives": draw_positives(jax.random.fold_in(streams_of[5], 71), 0),
        "weights": draw_weights(jax.random.fold_in(streams_of[5], 71), 0),
        "first_moment": bell_draw(streams_of[3], (LABELS, D), 0.3, 1.8, ((0, 128),), jnp.float32),
        "second_moment": jnp.clip(jnp.exp(math.log(1.0) - 2.9957323 * jax.random.uniform(streams_of[4], (LABELS, D), jnp.float32) ** shard_levels(streams_of[4], (LABELS, D), ((0, 128),), -0.2, 0.2)), 0.05, 1.0),
    }


beta_one = 0.9
beta_two = 0.95
rate = 0.02
decay = 0.1
epsilon = 1e-08
past_steps = 1000

def contract_last(left, right):
    return lax.dot_general(left, right, (((1,), (1,)), ((), ())), preferred_element_type=jnp.float32)

def contract_first(left, right):
    return lax.dot_general(left, right, (((0,), (0,)), ((), ())), preferred_element_type=jnp.float32)

def residuals(rows, pos_rows, wb, label_ids):
    logits = contract_last(rows, wb)
    hits = jnp.any(pos_rows[:, :, None] == label_ids[None, None, :], axis=1)
    return (jax.nn.sigmoid(logits) - hits.astype(jnp.float32)).astype(jnp.bfloat16)

def adamw(weight, first, second, grad, count):
    first = beta_one * first + (1.0 - beta_one) * grad
    second = beta_two * second + (1.0 - beta_two) * grad * grad
    first_hat = first / (1.0 - beta_one ** count)
    second_hat = second / (1.0 - beta_two ** count)
    weight = weight - rate * (first_hat / (jnp.sqrt(second_hat) + epsilon) + decay * weight)
    return (weight, first, second)

def reference(queries, positives, weights, first_moment, second_moment):
    weight, first, second = (weights, first_moment, second_moment)
    results = []
    for step in range(STEPS):
        blocks = weight.astype(jnp.bfloat16).reshape(LABELS // LAB_DEV, LAB_DEV, D)

        def one_block(acc, item):
            index, wb = item
            label_ids = index * LAB_DEV + jnp.arange(LAB_DEV, dtype=jnp.int32)
            resid = residuals(queries, positives, wb, label_ids)
            acc = acc + jnp.dot(resid, wb, preferred_element_type=jnp.float32)
            return (acc, contract_first(resid, queries))
        start = jnp.zeros((QUERIES, D), jnp.float32)
        indices = jnp.arange(LABELS // LAB_DEV, dtype=jnp.int32)
        query_grad, grads = lax.scan(one_block, start, (indices, blocks))
        results.append(query_grad)
        weight, first, second = adamw(weight, first, second, grads.reshape(LABELS, D), past_steps + step + 1)
    return (weight, first, second, jnp.stack(results))
```

```python
import jax
import jax.numpy as jnp
from jax import lax
from jax.experimental import pallas as pl
from jax.experimental.pallas import tpu as pltpu
from jax.sharding import Mesh, PartitionSpec as P

STEPS = 2

beta_one = 0.9
beta_two = 0.95
rate = 0.02
decay = 0.1
epsilon = 1e-08
past_steps = 1000

f32 = jnp.float32
bf16 = jnp.bfloat16
i32 = jnp.int32

NX, NLO, NZ, NCORE, NHI = 4, 2, 8, 2, 2
NY = NLO * NHI
D = 512
ROWS = 16
LINE = NZ * ROWS
HALF = LINE // 2
PAD = 80
NQ = NX * NY * LINE
BLOCK = 256
NBLOCK = NQ // BLOCK
LAB = 1024
TILE = 256
SLOTS = 8
VMEM = 40 * 2**20


def spec(shape=None, index=None, space=pltpu.VMEM):
    if shape is None:
        return pl.BlockSpec(memory_space=space)
    return pl.BlockSpec(shape, index, memory_space=space)


SMEM = pltpu.SMEM


def params():
    return pltpu.CompilerParams(vmem_limit_bytes=VMEM)


def descending(rows):
    rows = list(rows)
    for a, b in (
        (0, 1), (2, 3), (4, 5), (6, 7), (0, 2), (1, 3), (4, 6), (5, 7), (1, 2), (5, 6),
        (0, 4), (1, 5), (2, 6), (3, 7), (2, 4), (3, 5), (1, 2), (3, 4), (5, 6),
    ):
        rows[a], rows[b] = jnp.maximum(rows[a], rows[b]), jnp.minimum(rows[a], rows[b])
    return rows


def assemble_kernel(meta, *refs):
    left, right, (q_ref, pos_ref, most_ref) = refs[:4], refs[4:8], refs[8:]
    base = meta[1]

    def fill(shift):
        for c in range(NY):
            dy = (c + shift) % NY
            most = []
            for dx in range(NX):
                at = c * NX * LINE + dx * LINE
                q_ref[at : at + HALF, :] = left[dy][dx, :HALF, :]
                q_ref[at + HALF : at + LINE, :] = right[dx][dy]
                coded = left[dy][dx, HALF:PAD, : 3 * LINE].astype(f32)[:SLOTS]
                ids = coded[:, :LINE] + 256.0 * coded[:, LINE : 2 * LINE] + 65536.0 * coded[:, 2 * LINE :]
                local = ids.astype(i32) - base
                local = jnp.where((local >= 0) & (local < NCORE * LAB), local, -1)
                rows = descending([local[j : j + 1, :] for j in range(SLOTS)])
                for j in range(SLOTS):
                    pos_ref[j : j + 1, at : at + LINE] = rows[j]
                most.append(sum((row >= 0).astype(f32) for row in rows))
            for pair in range(2):
                both = jnp.maximum(most[2 * pair], most[2 * pair + 1])
                most_ref[2 * c + pair] = jnp.max(both).astype(i32)

    pl.when(meta[0] == 0)(lambda: fill(0))
    pl.when(meta[0] == 1)(lambda: fill(NLO))


def assemble(meta, left, right):
    return pl.pallas_call(
        assemble_kernel,
        out_shape=(
            jax.ShapeDtypeStruct((NQ, D), bf16),
            jax.ShapeDtypeStruct((SLOTS, NQ), i32),
            jax.ShapeDtypeStruct((NBLOCK,), i32),
        ),
        in_specs=[spec(space=SMEM)] + [spec()] * 8,
        out_specs=(spec(), spec(), spec(space=SMEM)),
        compiler_params=params(),
        cost_estimate=pl.CostEstimate(flops=0, bytes_accessed=4 * NQ * D, transcendentals=0),
        name="assemble",
    )(meta, *left, *right)


def resid_kernel(offset, most, q_ref, pos_ref, wb_ref, out_ref):
    count = most[pl.program_id(0)]

    def fill(slots):
        q = q_ref[...]
        for t in range(LAB // TILE):
            rows = slice(t * TILE, (t + 1) * TILE)
            logits = lax.dot_general(
                wb_ref[rows, :], q, (((1,), (1,)), ((), ())), preferred_element_type=f32
            )
            share = pl.reciprocal(1.0 + jnp.exp(-logits), approx=True)
            label = lax.broadcasted_iota(i32, (TILE, BLOCK), 0)
            start = offset[0] + t * TILE
            hit = (pos_ref[0:1, :] - start) == label
            for j in range(1, slots):
                hit = hit | ((pos_ref[j : j + 1, :] - start) == label)
            out_ref[rows, :] = jnp.where(hit, share - 1.0, share).astype(bf16)

    pl.when(count <= 1)(lambda: fill(1))
    pl.when(count == 2)(lambda: fill(2))
    pl.when(count > 2)(lambda: fill(SLOTS))


def residuals(offset, most, q, pos, wb):
    return pl.pallas_call(
        resid_kernel,
        grid=(NBLOCK,),
        out_shape=jax.ShapeDtypeStruct((LAB, NQ), bf16),
        in_specs=[
            spec(space=SMEM),
            spec(space=SMEM),
            spec((BLOCK, D), lambda i: (i, 0)),
            spec((SLOTS, BLOCK), lambda i: (0, i)),
            spec((LAB, D), lambda i: (0, 0)),
        ],
        out_specs=spec((LAB, BLOCK), lambda i: (0, i)),
        compiler_params=params(),
        cost_estimate=pl.CostEstimate(
            flops=2 * LAB * NQ * D, bytes_accessed=2 * (NQ * D + LAB * D + LAB * NQ), transcendentals=2 * LAB * NQ
        ),
        name="resid",
    )(offset, most, q, pos, wb)


def terms_kernel(blocks, own_ref, other_ref, wb_own, wb_other, out_ref):
    dims = (((0,), (0,)), ((), ()))
    out_ref[...] = lax.dot_general(own_ref[...], wb_own[...], dims, preferred_element_type=f32) + lax.dot_general(
        other_ref[...], wb_other[...], dims, preferred_element_type=f32
    )


def terms(blocks, first, second, wb_first, wb_second):
    count = blocks.shape[0]
    return pl.pallas_call(
        terms_kernel,
        grid_spec=pltpu.PrefetchScalarGridSpec(
            num_scalar_prefetch=1,
            grid=(count,),
            in_specs=[
                spec((LAB, BLOCK), lambda i, blocks: (0, blocks[i])),
                spec((LAB, BLOCK), lambda i, blocks: (0, blocks[i])),
                spec((LAB, D), lambda i, blocks: (0, 0)),
                spec((LAB, D), lambda i, blocks: (0, 0)),
            ],
            out_specs=spec((BLOCK, D), lambda i, blocks: (i, 0)),
        ),
        out_shape=jax.ShapeDtypeStruct((count * BLOCK, D), f32),
        compiler_params=params(),
        cost_estimate=pl.CostEstimate(
            flops=4 * LAB * count * BLOCK * D, bytes_accessed=8 * 2**20, transcendentals=0
        ),
        name="terms",
    )(blocks, first, second, wb_first, wb_second)


def grad_kernel(resid_ref, q_ref, out_ref):
    out_ref[...] = jnp.dot(resid_ref[...], q_ref[...], preferred_element_type=f32)


def gradient(resid, q):
    return pl.pallas_call(
        grad_kernel,
        grid=(LAB // TILE,),
        out_shape=jax.ShapeDtypeStruct((LAB, D), f32),
        in_specs=[spec((TILE, NQ), lambda i: (i, 0)), spec((NQ, D), lambda i: (0, 0))],
        out_specs=spec((TILE, D), lambda i: (i, 0)),
        compiler_params=params(),
        cost_estimate=pl.CostEstimate(
            flops=2 * LAB * NQ * D, bytes_accessed=2 * (LAB * NQ + NQ * D) + 4 * LAB * D, transcendentals=0
        ),
        name="grad",
    )(resid, q)


def adamw_kernel(count, resid_ref, q_ref, part_ref, w_ref, m_ref, v_ref, w_out, m_out, v_out, *wb_out):
    grad = jnp.dot(resid_ref[...], q_ref[...], preferred_element_type=f32) + part_ref[...]
    first = beta_one * m_ref[...] + (1.0 - beta_one) * grad
    second = beta_two * v_ref[...] + (1.0 - beta_two) * grad * grad
    first_hat = first / (1.0 - beta_one**count)
    second_hat = second / (1.0 - beta_two**count)
    weight = w_ref[...]
    weight = weight - rate * (first_hat / (jnp.sqrt(second_hat) + epsilon) + decay * weight)
    w_out[...] = weight
    m_out[...] = first
    v_out[...] = second
    if wb_out:
        wb_out[0][...] = weight.astype(bf16)


def update(count, last, resid, q, part, weight, first, second):
    tile = spec((TILE, D), lambda i: (i, 0))
    full = jax.ShapeDtypeStruct((LAB, D), f32)
    return pl.pallas_call(
        lambda *refs: adamw_kernel(count, *refs),
        grid=(LAB // TILE,),
        out_shape=(full, full, full) + (() if last else (jax.ShapeDtypeStruct((LAB, D), bf16),)),
        in_specs=[spec((TILE, NQ), lambda i: (i, 0)), spec((NQ, D), lambda i: (0, 0))] + [tile] * 4,
        out_specs=(tile,) * (3 if last else 4),
        compiler_params=params(),
        cost_estimate=pl.CostEstimate(
            flops=2 * LAB * NQ * D, bytes_accessed=2 * (LAB * NQ + NQ * D) + 28 * LAB * D, transcendentals=2 * LAB * D
        ),
        name="adamw",
    )(resid, q, part, weight, first, second)


def shift(array, axis, by):
    if axis == "x":
        return lax.ppermute(array, "x", [(i, (i + by) % NX) for i in range(NX)])
    name = lambda y: (y % NLO) * NHI + y // NLO
    return lax.ppermute(array, ("ylo", "yhi"), [(name(y), name((y + by) % NY)) for y in range(NY)])


def swap(array):
    return lax.ppermute(array, "core", [(0, 1), (1, 0)])


def spread(array, axis):
    near = shift(array, axis, -1)
    far = shift(array, axis, 1)
    mid = shift(array, axis, 2)
    return [array, near, mid, far]


def gather(queries, positives):
    coded = positives.T.reshape(1, ROWS * SLOTS)
    pieces = [coded & 255, (coded >> 8) & 255, coded >> 16]
    pieces.append(jnp.zeros_like(coded))
    coded = jnp.concatenate(pieces, axis=1).astype(bf16)
    mine = jnp.concatenate([queries, coded, jnp.zeros((7, D), bf16)], axis=0)
    line = lax.all_to_all(
        jnp.broadcast_to(mine[None], (NZ, ROWS + 8, D)), "z", split_axis=0, concat_axis=0, tiled=True
    )
    rows = line[:, :ROWS].reshape(LINE, D)
    coded = line[:, ROWS, : 3 * LINE].reshape(NZ, 3, SLOTS, ROWS)
    coded = coded.transpose(2, 1, 0, 3).reshape(SLOTS, 3 * LINE)
    coded = jnp.pad(coded, ((0, PAD - HALF - SLOTS), (0, D - 3 * LINE)))
    left = jnp.concatenate([rows[:HALF], coded], axis=0)
    right = rows[HALF:]
    left = jnp.stack(spread(left, "x"))
    right = jnp.stack(spread(right, "y"))
    return spread(left, "y"), spread(right, "x")


def scatter_plane(parts):
    up = shift(parts[:BLOCK].astype(bf16), "y", 1)
    down = shift(parts[BLOCK : 2 * BLOCK].astype(bf16), "y", -1)
    plane = parts[2 * BLOCK :] + jnp.concatenate([up, down], axis=0).astype(f32)
    plane = plane.reshape(NX, LINE, D)
    got = [shift(plane[dx].astype(bf16), "x", dx) for dx in (1, 3, 2)]
    line = plane[0] + got[0].astype(f32) + got[1].astype(f32) + got[2].astype(f32)
    return line.reshape(NZ, ROWS, D)


def shards(queries, positives, weights, first_moment, second_moment):
    weight, first, second = weights, first_moment, second_moment
    core, high = lax.axis_index("core"), lax.axis_index("yhi")
    chip = (lax.axis_index("x") * NLO + lax.axis_index("ylo")) * NZ + lax.axis_index("z")
    meta = jnp.stack([high, chip * (NCORE * LAB)]).astype(i32)
    mine = (core * LAB).astype(i32).reshape(1)
    theirs = ((1 - core) * LAB).astype(i32).reshape(1)
    here = 4 * high
    blocks = jnp.stack([here + 2, 7 - here, here, here + 1]).astype(i32)

    wb = weight.astype(bf16)
    wb_other = swap(wb)
    left, right = gather(queries, positives)
    q, pos, most = assemble(meta, left, right)
    lines = []
    for step in range(STEPS):
        own = residuals(mine, most, q, pos, wb)
        other = residuals(theirs, most, q, pos, wb_other)
        parts = terms(blocks, own, other, wb, wb_other)
        part = swap(gradient(other, q))
        last = step == STEPS - 1
        out = update(past_steps + step + 1, last, own, q, part, weight, first, second)
        weight, first, second = out[:3]
        lines.append(scatter_plane(parts))
        if not last:
            wb = out[3]
            wb_other = swap(wb)
    line = jnp.stack(lines, axis=1)
    line = lax.all_to_all(line, "z", split_axis=0, concat_axis=0, tiled=True)
    return weight, first, second, jnp.sum(line, axis=0)


def solution(mesh):
    axes = ("x", "ylo", "z", "core", "yhi")
    devices = mesh.devices.reshape(NX, NLO, NZ, NCORE, NHI)
    label = ("x", "ylo", "z", "core")
    in_specs = (P(axes, None), P(axes, None), P(label, None), P(label, None), P(label, None))
    out_specs = (P(label, None), P(label, None), P(label, None), P(None, axes, None))
    return jax.shard_map(
        shards, mesh=Mesh(devices, axes), in_specs=in_specs, out_specs=out_specs, check_vma=False
    )
```

```python
import jax
import jax.numpy as jnp
from jax import lax
from jax.experimental import pallas as pl
from jax.experimental.pallas import tpu as pltpu
from jax.sharding import Mesh, PartitionSpec as P

STEPS = 2

beta_one = 0.9
beta_two = 0.95
rate = 0.02
decay = 0.1
epsilon = 1e-08
past_steps = 1000

f32 = jnp.float32
bf16 = jnp.bfloat16
i32 = jnp.int32

NX, NLO, NZ, NCORE, NHI = 4, 2, 8, 2, 2
NY = NLO * NHI
AXES = ("x", "ylo", "z", "core", "yhi")
D = 512
ROWS = 16
SLOTS = 8
LINE = NZ * ROWS
NQ = NX * NY * LINE
BLOCK = 2 * LINE
LAB = 1024
TILE = 256
VMEM = 16 * 2**20
LOG2E = 1.4426950408889634


def spec(shape=None, index=None, space=pltpu.VMEM):
    if shape is None:
        return pl.BlockSpec(memory_space=space)
    return pl.BlockSpec(shape, index, memory_space=space)


def params():
    return pltpu.CompilerParams(vmem_limit_bytes=VMEM)


def cost(flops=0, size=0, exps=0):
    return pl.CostEstimate(flops=flops, bytes_accessed=size, transcendentals=exps)


def descending(rows):
    rows = list(rows)
    for a, b in (
        (0, 1), (2, 3), (4, 5), (6, 7), (0, 2), (1, 3), (4, 6), (5, 7), (1, 2), (5, 6),
        (0, 4), (1, 5), (2, 6), (3, 7), (2, 4), (3, 5), (1, 2), (3, 4), (5, 6),
    ):
        rows[a], rows[b] = jnp.maximum(rows[a], rows[b]), jnp.minimum(rows[a], rows[b])
    return rows


def here_is():
    high, core = lax.axis_index("yhi"), lax.axis_index("core")
    chip = (lax.axis_index("x") * NLO + lax.axis_index("ylo")) * NZ + lax.axis_index("z")
    base = chip * NCORE * LAB
    return high, core, base + core * LAB, base + (1 - core) * LAB


def gray(slot):
    return slot ^ (slot >> 1)


def place_of(late, early):
    high, core = here_is()[:2]
    y = late + core * (early - late)
    x = early + core * (late - early)
    return (y ^ (2 * high)) * NX + ((x + core * (4 - 2 * x)) & 3)


FAST = 2


def contract_last(left, right):
    return lax.dot_general(left, right, (((1,), (1,)), ((), ())), preferred_element_type=f32)


def contract_first(left, right):
    return lax.dot_general(left, right, (((0,), (0,)), ((), ())), preferred_element_type=f32)


def fill_tile(logits, hits, first):
    share = pl.reciprocal(1.0 + jnp.exp2(logits * -LOG2E), approx=True)
    label = lax.broadcasted_iota(i32, logits.shape, 0) + first
    hit = hits[0] == label
    for row in hits[1:]:
        hit = hit | (row == label)
    return jnp.where(hit, share - 1.0, share).astype(bf16)


def more_hits(count, pos_ref, half, out_ref, at):
    @pl.loop(FAST, count)
    def _(j):
        slots = pos_ref[half, :, at]
        slots = jnp.where(lax.broadcasted_iota(i32, slots.shape, 0) == j, slots, -1)
        hit = jnp.max(slots, axis=0, keepdims=True)

        @pl.loop(0, LAB // TILE)
        def _(t):
            rows = pl.ds(pl.multiple_of(t * TILE, TILE), TILE)
            old = out_ref[rows, at].astype(f32)
            label = lax.broadcasted_iota(i32, old.shape, 0) + t * TILE
            out_ref[rows, at] = jnp.where(hit == label, old - 1.0, old).astype(bf16)


def fill_grad(resid_ref, q_ref, out_ref):
    for t in range(LAB // (2 * TILE)):
        rows = slice(2 * TILE * t, 2 * TILE * (t + 1))
        out_ref[rows, :] = jnp.dot(resid_ref[rows, :], q_ref[...], preferred_element_type=f32)


def part_kernel(part_ref, wb_own, wb_other, *refs, late):
    first_labels = here_is()[2:]
    grads = refs[-1:] if late == LAST else ()
    before = refs[4] if late else None
    q_ref, pos_ref, own_ref, other_ref, most_ref = refs[-5 - len(grads) : len(refs) - len(grads)]
    spans = [
        pl.ds(pl.multiple_of(place_of(late, gray(early)) * LINE, LINE), LINE) for early in range(4)
    ]
    coded = part_ref[NX * LINE :, : 3 * LINE].astype(f32)
    ids = coded[:, :LINE] + 256.0 * coded[:, LINE : 2 * LINE] + 65536.0 * coded[:, 2 * LINE :]
    ids = ids.astype(i32)
    rows = []
    for j in range(SLOTS):
        row = jnp.concatenate([ids[SLOTS * early + j : SLOTS * early + j + 1] for early in range(4)], axis=0)
        local = jnp.concatenate([row - first for first in first_labels], axis=0)
        rows.append(jnp.where((local >= 0) & (local < LAB), local, -1))
    rows = descending(rows)
    count = sum((row >= 0).astype(f32) for row in rows)
    most = jnp.max(count).astype(i32)
    most_ref[...] = count if before is None else jnp.maximum(count, before[...])
    rows = rows[:1] + [jnp.where(row == last, -1, row) for last, row in zip(rows, rows[1:])]
    for half in range(2):
        for early, at in enumerate(spans):
            k = 4 * half + early
            for j in range(SLOTS):
                pos_ref[half, j : j + 1, at] = rows[j][k : k + 1]
    for pair in range(2):
        q = part_ref[pair * BLOCK : (pair + 1) * BLOCK, :]
        for half, wb_ref, out_ref in ((1, wb_other, other_ref), (0, wb_own, own_ref)):
            for t in range(LAB // TILE):
                tile = slice(t * TILE, (t + 1) * TILE)
                logits = contract_last(wb_ref[tile, :], q)
                for k in range(2):
                    early = 2 * pair + k
                    hits = [row[4 * half + early : 4 * half + early + 1] for row in rows[:FAST]]
                    out_ref[tile, spans[early]] = fill_tile(logits[:, k * LINE : (k + 1) * LINE], hits, t * TILE)
    for early, at in enumerate(spans):
        q_ref[at, :] = part_ref[early * LINE : (early + 1) * LINE, :]

    @pl.when(most > FAST)
    def _():
        for half, out_ref in enumerate((own_ref, other_ref)):
            for at in spans:
                more_hits(most, pos_ref, half, out_ref, at)

    for out_ref in grads:
        fill_grad(other_ref, q_ref, out_ref)


LAST = 2


def first_residuals(part, wb, wb_other, late, into):
    shapes = (
        jax.ShapeDtypeStruct((NQ, D), bf16),
        jax.ShapeDtypeStruct((2, SLOTS, NQ), i32),
        jax.ShapeDtypeStruct((LAB, NQ), bf16),
        jax.ShapeDtypeStruct((LAB, NQ), bf16),
        jax.ShapeDtypeStruct((2 * NX, LINE), f32),
    )
    if late == LAST:
        shapes += (jax.ShapeDtypeStruct((LAB, D), f32),)
    size = LAB * NX * LINE
    return pl.pallas_call(
        lambda *refs: part_kernel(*refs, late=late),
        out_shape=shapes,
        in_specs=[spec()] * (3 + len(into)),
        out_specs=(spec(),) * len(shapes),
        input_output_aliases={3 + i: i for i in range(len(into))},
        compiler_params=params(),
        cost_estimate=cost((8 if late == LAST else 4) * size * D, 4 * size, 4 * size),
        name="part",
    )(part, wb, wb_other, *into)


def code_kernel(q_ref, pos_ref, out_ref):
    ids = pos_ref[...]
    out_ref[:, :D] = q_ref[...]
    digits = [ids & 255, (ids >> 8) & 255, ids >> 16]
    lane = lax.broadcasted_iota(i32, (SLOTS, LINE), 1) - lax.broadcasted_iota(i32, (SLOTS, LINE), 0)
    coded = jnp.zeros((ROWS, LINE), f32)
    for i, digit in enumerate(digits):
        put = (lane == i * SLOTS).astype(f32).astype(bf16)
        coded = coded + jnp.dot(digit.astype(f32).astype(bf16), put, preferred_element_type=f32)
    out_ref[:, D:] = coded.astype(bf16)


def code(queries, positives):
    return pl.pallas_call(
        code_kernel,
        out_shape=jax.ShapeDtypeStruct((ROWS, D + LINE), bf16),
        in_specs=[spec()] * 2,
        out_specs=spec(),
        compiler_params=params(),
        cost_estimate=cost(size=4 * ROWS * D),
        name="code",
    )(queries, positives)


def pack_kernel(*refs):
    out_ref = refs[-1]
    for i, ref in enumerate(refs[:-1]):
        out_ref[i * LINE : (i + 1) * LINE, :] = ref[:LINE, :]
    tails = [ref[LINE:, :] for ref in refs[:-1]]
    out_ref[NX * LINE :, :] = jnp.concatenate(tails, axis=0)


def pack(parts):
    return pl.pallas_call(
        pack_kernel,
        out_shape=jax.ShapeDtypeStruct((NX * (LINE + SLOTS), D), bf16),
        in_specs=[spec()] * 4,
        out_specs=spec(),
        compiler_params=params(),
        cost_estimate=cost(size=4 * NX * LINE * D),
        name="pack",
    )(*parts)


def beside():
    high, core = here_is()[:2]
    plane = (1 + 2 * core) ^ (2 * high)
    return [2 * plane, 2 * plane + 1]


def here():
    first = 4 * lax.axis_index("yhi")
    return [first, first + 1]


def remaining():
    return [block ^ 4 for block in beside() + here()]


def spans_of(blocks):
    return [pl.ds(pl.multiple_of(block * BLOCK, BLOCK), BLOCK) for block in blocks()]


def fill_resid(most, q_ref, pos_ref, wb_ref, out_ref, half, spans):
    for at in spans:
        q = q_ref[at, :]
        hits = [pos_ref[half, j : j + 1, at] for j in range(FAST)]
        for t in range(LAB // TILE):
            rows = slice(t * TILE, (t + 1) * TILE)
            out_ref[rows, at] = fill_tile(contract_last(wb_ref[rows, :], q), hits, t * TILE)
    count = jnp.max(most[...]).astype(i32)

    @pl.when(count > FAST)
    def _():
        for at in spans:
            more_hits(count, pos_ref, half, out_ref, at)


def fill_terms(own_ref, other_ref, wb_own, wb_other, out_ref, spans):
    for i, at in enumerate(spans):
        first = contract_first(own_ref[:, at], wb_own[...])
        second = contract_first(other_ref[:, at], wb_other[...])
        out_ref[i * BLOCK : (i + 1) * BLOCK, :] = (first + second).astype(out_ref.dtype)


def plane_kernel(most, q_ref, pos_ref, wb_own, wb_other, *refs, blocks):
    own_ref, other_ref, out_ref = refs[-3:]
    spans = spans_of(blocks)
    fill_resid(most, q_ref, pos_ref, wb_own, own_ref, 0, spans)
    fill_resid(most, q_ref, pos_ref, wb_other, other_ref, 1, spans)
    fill_terms(own_ref, other_ref, wb_own, wb_other, out_ref, spans)


def plane_terms(most, q, pos, wb, wb_other, blocks, kind, into=()):
    size = 2 * LAB * 2 * BLOCK
    resid = jax.ShapeDtypeStruct((LAB, NQ), bf16)
    return pl.pallas_call(
        lambda *refs: plane_kernel(*refs, blocks=blocks),
        out_shape=(resid, resid, jax.ShapeDtypeStruct((2 * BLOCK, D), kind)),
        in_specs=[spec()] * (5 + len(into)),
        out_specs=(spec(),) * 3,
        input_output_aliases={5 + i: i for i in range(len(into))},
        compiler_params=params(),
        cost_estimate=cost(4 * size * D, 4 * size, 2 * size),
        name="plane",
    )(most, q, pos, wb, wb_other, *into)


def terms_kernel(own_ref, other_ref, wb_own, wb_other, out_ref, *, blocks):
    fill_terms(own_ref, other_ref, wb_own, wb_other, out_ref, spans_of(blocks))


def terms(own, other, wb_own, wb_other, blocks, kind):
    return pl.pallas_call(
        lambda *refs: terms_kernel(*refs, blocks=blocks),
        out_shape=jax.ShapeDtypeStruct((2 * BLOCK, D), kind),
        in_specs=[spec()] * 4,
        out_specs=spec(),
        compiler_params=params(),
        cost_estimate=cost(8 * LAB * BLOCK * D, 4 * 2**20),
        name="terms",
    )(own, other, wb_own, wb_other)


def rest_kernel(most, q_ref, pos_ref, wb_ref, resid_ref, out_ref, *, half):
    fill_resid(most, q_ref, pos_ref, wb_ref, resid_ref, half, spans_of(remaining))
    fill_grad(resid_ref, q_ref, out_ref)


def rest_gradient(most, q, pos, wb, resid, half):
    size = LAB * 4 * BLOCK
    return pl.pallas_call(
        lambda most, q, pos, wb, old, resid, out: rest_kernel(most, q, pos, wb, resid, out, half=half),
        out_shape=(jax.ShapeDtypeStruct((LAB, NQ), bf16), jax.ShapeDtypeStruct((LAB, D), f32)),
        in_specs=[spec()] * 5,
        out_specs=(spec(),) * 2,
        input_output_aliases={4: 0},
        compiler_params=params(),
        cost_estimate=cost(6 * size * D, 8 * size, 2 * size),
        name="rest",
    )(most, q, pos, wb, resid)[1]


def grad_kernel(resid_ref, q_ref, out_ref):
    fill_grad(resid_ref, q_ref, out_ref)


def gradient(resid, q):
    return pl.pallas_call(
        grad_kernel,
        out_shape=jax.ShapeDtypeStruct((LAB, D), f32),
        in_specs=[spec()] * 2,
        out_specs=spec(),
        compiler_params=params(),
        cost_estimate=cost(2 * LAB * NQ * D, 8 * 2**20),
        name="grad",
    )(resid, q)


def adamw(count, grad, weight, first, second):
    first = beta_one * first + (1.0 - beta_one) * grad
    second = beta_two * second + (1.0 - beta_two) * grad * grad
    first_hat = first * (1.0 / (1.0 - beta_one**count))
    second_hat = second * (1.0 / (1.0 - beta_two**count))
    weight = weight - rate * (first_hat / (jnp.sqrt(second_hat) + epsilon) + decay * weight)
    return weight, first, second


def adamw_kernel(count, one, two, w_ref, m_ref, v_ref, w_out, m_out, v_out, *wb_out):
    @pl.loop(0, one.shape[0] // 64)
    def _(t):
        rows = pl.ds(pl.multiple_of(t * 64, 64), 64)
        grad = one[rows, :] + two[rows, :]
        weight, first, second = adamw(count, grad, w_ref[rows, :], m_ref[rows, :], v_ref[rows, :])
        w_out[rows, :] = weight
        m_out[rows, :] = first
        v_out[rows, :] = second
        if wb_out:
            wb_out[0][rows, :] = weight.astype(bf16)


def update(count, last, one, two, weight, first, second):
    full = jax.ShapeDtypeStruct((LAB, D), f32)
    return pl.pallas_call(
        lambda *refs: adamw_kernel(count, *refs),
        out_shape=(full, full, full) + (() if last else (jax.ShapeDtypeStruct((LAB, D), bf16),)),
        in_specs=[spec()] * 5,
        out_specs=(spec(),) * (3 if last else 4),
        compiler_params=params(),
        cost_estimate=cost(20 * LAB * D, 12 * LAB * D, 2 * LAB * D),
        name="adamw",
    )(one, two, weight, first, second)


def moved(move):
    pairs = []
    for x in range(NX):
        for y in range(NY):
            for z in range(NZ):
                for core in range(NCORE):
                    tx, ty, tz, tcore = move(x, y, z, core)
                    name = lambda x, y, z, core: (
                        (((x % NX) * NLO + y % NLO) * NZ + z % NZ) * NCORE + core
                    ) * NHI + (y % NY) // NLO
                    pairs.append((name(x, y, z, core), name(tx, ty, tz, tcore)))
    return pairs


def send(array, move):
    return lax.ppermute(array, AXES, moved(move))


def along_x(by):
    return lambda x, y, z, core: (x ^ by, y, z, core)


def along_y(by):
    return lambda x, y, z, core: (x, y ^ by, z, core)


def along_z(by):
    return lambda x, y, z, core: (x, y, z + by, core)


def by_core(zero, one):
    return lambda x, y, z, core: one(x, y, z, core) if core else zero(x, y, z, core)


def swap(array):
    return send(array, lambda x, y, z, core: (x, y, z, 1 - core))


def gather(queries, positives):
    line = code(queries, positives)
    line = jnp.concatenate([line, send(line, lambda x, y, z, core: (x, y, z - 1 + 2 * (core == 1), 1 - core))], axis=0)
    for by in (1, 2):
        line = jnp.concatenate([line, send(line, by_core(along_z(by), along_z(-by)))], axis=0)
    coded = line[:, D : D + 3 * SLOTS].T
    coded = jnp.concatenate([coded[i * SLOTS : (i + 1) * SLOTS] for i in range(3)], axis=1)
    coded = jnp.pad(coded, ((0, 0), (0, D - 3 * LINE)))
    chip = jnp.concatenate([line[:, :D], coded], axis=0)
    four = [chip] + [send(chip, by_core(along_x(by), along_y(by))) for by in (1, 3, 2)]
    four = pack(four)
    return [four] + [send(four, by_core(along_y(by), along_x(by))) for by in (1, 3, 2)]


def after(array, *others):
    return lax.optimization_barrier((array, *others))


def shards(queries, positives, weights, first_moment, second_moment):
    weight, first, second = weights, first_moment, second_moment
    to_plane = lambda part: send(part, by_core(along_y(1), along_y(3)))
    to_half = lambda plane: send(plane[1:3].astype(bf16), by_core(along_x(1), along_x(3)))
    to_line = lambda plane, got: send(plane[3] + got[1].astype(f32), by_core(along_x(3), along_x(1)))
    as_plane = lambda part, got: (part + got.astype(f32)).reshape(NX, LINE, D)

    wb = weight.astype(bf16)
    wb_other = swap(wb)
    state = ()
    for late, part in zip((0, 1, 3, LAST), gather(queries, positives)):
        *state, theirs = (*first_residuals(part, wb, wb_other, late, state[:5]), None)[:6]
    q, pos, own, other, most = state
    part = swap(theirs)
    mine = gradient(own, q)
    weight, first, second, wb_next = update(past_steps + 1, False, mine, part, weight, first, second)
    next_other = swap(wb_next)

    wb_next, own, other = after(wb_next, own, other)
    step0 = (own, other, wb, wb_other)
    out0 = to_plane(terms(*step0, beside, bf16))
    wb, wb_other = wb_next, next_other
    own, other, out1 = plane_terms(most, q, pos, wb, wb_other, beside, bf16)
    out1, own, other, *step0 = after(out1, own, other, *step0)
    out1 = to_plane(out1)
    own, other, part1 = plane_terms(most, q, pos, wb, wb_other, here, f32, (own, other))
    part1, *step0 = after(part1, *step0)
    part0 = terms(*step0, here, f32)

    plane0 = as_plane(part0, out0)
    plane1 = as_plane(part1, out1)
    half0, half1 = to_half(plane0), to_half(plane1)
    plane1, plane0, other, own = after(plane1, plane0, other, own)
    theirs = rest_gradient(most, q, pos, wb_other, other, 1)
    part = swap(theirs)
    quarter1, quarter0 = to_line(plane1, half1), to_line(plane0, half0)
    mine = rest_gradient(most, q, pos, wb, own, 0)
    line = [
        plane[0] + half[0].astype(f32) + quarter
        for plane, half, quarter in ((plane0, half0, quarter0), (plane1, half1, quarter1))
    ]
    line = jnp.stack([part.reshape(NZ, ROWS, D) for part in line], axis=1)
    line, mine = after(line, mine)
    got = send(line[4:].astype(bf16), by_core(along_z(-2), along_z(2)))
    weight, first, second = update(past_steps + 2, True, mine, part, weight, first, second)
    got, weight, first, second = after(got, weight, first, second)
    line = line[:4] + got.astype(f32)
    line = line[:2] + send(line[2:], by_core(along_z(-1), along_z(1)))
    line = line[0] + send(line[1], lambda x, y, z, core: (x, y, z - 1 + 2 * core, 1 - core))
    return weight, first, second, line


def solution(mesh):
    devices = mesh.devices.reshape(NX, NLO, NZ, NCORE, NHI)
    label = AXES[:4]
    in_specs = (P(AXES, None), P(AXES, None), P(label, None), P(label, None), P(label, None))
    out_specs = (P(label, None), P(label, None), P(label, None), P(None, AXES, None))
    return jax.shard_map(
        shards, mesh=Mesh(devices, AXES), in_specs=in_specs, out_specs=out_specs, check_vma=False
    )
```

```python
import jax
import jax.numpy as jnp
from jax import lax
from jax.experimental import pallas as pl
from jax.experimental.pallas import tpu as pltpu
from jax.sharding import Mesh, PartitionSpec as P

STEPS = 2

beta_one = 0.9
beta_two = 0.95
rate = 0.02
decay = 0.1
epsilon = 1e-08
past_steps = 1000

f32 = jnp.float32
bf16 = jnp.bfloat16
i32 = jnp.int32

NX, NLO, NZ, NCORE, NHI = 4, 2, 8, 2, 2
NY = NLO * NHI
AXES = ("x", "ylo", "z", "core", "yhi")
D = 512
ROWS = 16
SLOTS = 8
LINE = NZ * ROWS
NQ = NX * NY * LINE
BLOCK = 2 * LINE
LAB = 1024
TILE = 256
VMEM = 16 * 2**20
LOG2E = 1.4426950408889634


def spec(shape=None, index=None, space=pltpu.VMEM):
    if shape is None:
        return pl.BlockSpec(memory_space=space)
    return pl.BlockSpec(shape, index, memory_space=space)


def params():
    return pltpu.CompilerParams(vmem_limit_bytes=VMEM)


def cost(flops=0, size=0, exps=0):
    return pl.CostEstimate(flops=flops, bytes_accessed=size, transcendentals=exps)


def descending(rows):
    rows = list(rows)
    for a, b in (
        (0, 1), (2, 3), (4, 5), (6, 7), (0, 2), (1, 3), (4, 6), (5, 7), (1, 2), (5, 6),
        (0, 4), (1, 5), (2, 6), (3, 7), (2, 4), (3, 5), (1, 2), (3, 4), (5, 6),
    ):
        rows[a], rows[b] = jnp.maximum(rows[a], rows[b]), jnp.minimum(rows[a], rows[b])
    return rows


def here_is():
    high, core = lax.axis_index("yhi"), lax.axis_index("core")
    chip = (lax.axis_index("x") * NLO + lax.axis_index("ylo")) * NZ + lax.axis_index("z")
    base = chip * NCORE * LAB
    return high, core, base + core * LAB, base + (1 - core) * LAB


def gray(slot):
    return slot ^ (slot >> 1)


def place_of(late, early):
    high, core = here_is()[:2]
    y = late + core * (early - late)
    x = early + core * (late - early)
    return (y ^ (2 * high)) * NX + ((x + core * (4 - 2 * x)) & 3)


FAST = 2


def contract_last(left, right):
    return lax.dot_general(left, right, (((1,), (1,)), ((), ())), preferred_element_type=f32)


def contract_first(left, right):
    return lax.dot_general(left, right, (((0,), (0,)), ((), ())), preferred_element_type=f32)


def fill_tile(logits, hits, first):
    share = pl.reciprocal(1.0 + jnp.exp2(logits * -LOG2E), approx=True)
    label = lax.broadcasted_iota(i32, logits.shape, 0) + first
    hit = hits[0] == label
    for row in hits[1:]:
        hit = hit | (row == label)
    return jnp.where(hit, share - 1.0, share).astype(bf16)


def more_hits(count, pos_ref, half, out_ref, at):
    @pl.loop(FAST, count)
    def _(j):
        slots = pos_ref[half, :, at]
        slots = jnp.where(lax.broadcasted_iota(i32, slots.shape, 0) == j, slots, -1)
        hit = jnp.max(slots, axis=0, keepdims=True)

        @pl.loop(0, LAB // TILE)
        def _(t):
            rows = pl.ds(pl.multiple_of(t * TILE, TILE), TILE)
            old = out_ref[rows, at].astype(f32)
            label = lax.broadcasted_iota(i32, old.shape, 0) + t * TILE
            out_ref[rows, at] = jnp.where(hit == label, old - 1.0, old).astype(bf16)


def fill_grad(resid_ref, q_ref, out_ref):
    for t in range(LAB // (2 * TILE)):
        rows = slice(2 * TILE * t, 2 * TILE * (t + 1))
        out_ref[rows, :] = jnp.dot(resid_ref[rows, :], q_ref[...], preferred_element_type=f32)


def part_kernel(part_ref, wb_own, wb_other, *refs, late):
    first_labels = here_is()[2:]
    grads = refs[-1:] if late == LAST else ()
    before = refs[4] if late else None
    q_ref, pos_ref, own_ref, other_ref, most_ref = refs[-5 - len(grads) : len(refs) - len(grads)]
    spans = [
        pl.ds(pl.multiple_of(place_of(late, gray(early)) * LINE, LINE), LINE) for early in range(4)
    ]
    coded = part_ref[NX * LINE :, : 3 * LINE].astype(f32)
    ids = coded[:, :LINE] + 256.0 * coded[:, LINE : 2 * LINE] + 65536.0 * coded[:, 2 * LINE :]
    ids = ids.astype(i32)
    rows = []
    for j in range(SLOTS):
        row = jnp.concatenate([ids[SLOTS * early + j : SLOTS * early + j + 1] for early in range(4)], axis=0)
        local = jnp.concatenate([row - first for first in first_labels], axis=0)
        rows.append(jnp.where((local >= 0) & (local < LAB), local, -1))
    rows = descending(rows)
    count = sum((row >= 0).astype(f32) for row in rows)
    most = jnp.max(count).astype(i32)
    most_ref[...] = count if before is None else jnp.maximum(count, before[...])
    rows = rows[:1] + [jnp.where(row == last, -1, row) for last, row in zip(rows, rows[1:])]
    for half in range(2):
        for early, at in enumerate(spans):
            k = 4 * half + early
            for j in range(SLOTS):
                pos_ref[half, j : j + 1, at] = rows[j][k : k + 1]
    for pair in range(2):
        q = part_ref[pair * BLOCK : (pair + 1) * BLOCK, :]
        for half, wb_ref, out_ref in ((1, wb_other, other_ref), (0, wb_own, own_ref)):
            for t in range(LAB // TILE):
                tile = slice(t * TILE, (t + 1) * TILE)
                logits = contract_last(wb_ref[tile, :], q)
                for k in range(2):
                    early = 2 * pair + k
                    hits = [row[4 * half + early : 4 * half + early + 1] for row in rows[:FAST]]
                    out_ref[tile, spans[early]] = fill_tile(logits[:, k * LINE : (k + 1) * LINE], hits, t * TILE)
    for early, at in enumerate(spans):
        q_ref[at, :] = part_ref[early * LINE : (early + 1) * LINE, :]

    @pl.when(most > FAST)
    def _():
        for half, out_ref in enumerate((own_ref, other_ref)):
            for at in spans:
                more_hits(most, pos_ref, half, out_ref, at)

    for out_ref in grads:
        fill_grad(other_ref, q_ref, out_ref)


LAST = 2


def first_residuals(part, wb, wb_other, late, into):
    shapes = (
        jax.ShapeDtypeStruct((NQ, D), bf16),
        jax.ShapeDtypeStruct((2, SLOTS, NQ), i32),
        jax.ShapeDtypeStruct((LAB, NQ), bf16),
        jax.ShapeDtypeStruct((LAB, NQ), bf16),
        jax.ShapeDtypeStruct((2 * NX, LINE), f32),
    )
    if late == LAST:
        shapes += (jax.ShapeDtypeStruct((LAB, D), f32),)
    size = LAB * NX * LINE
    return pl.pallas_call(
        lambda *refs: part_kernel(*refs, late=late),
        out_shape=shapes,
        in_specs=[spec()] * (3 + len(into)),
        out_specs=(spec(),) * len(shapes),
        input_output_aliases={3 + i: i for i in range(len(into))},
        compiler_params=params(),
        cost_estimate=cost((8 if late == LAST else 4) * size * D, 4 * size, 4 * size),
        name="part",
    )(part, wb, wb_other, *into)


def code_kernel(q_ref, pos_ref, out_ref):
    ids = pos_ref[...]
    out_ref[:, :D] = q_ref[...]
    digits = [ids & 255, (ids >> 8) & 255, ids >> 16]
    lane = lax.broadcasted_iota(i32, (SLOTS, LINE), 1) - lax.broadcasted_iota(i32, (SLOTS, LINE), 0)
    coded = jnp.zeros((ROWS, LINE), f32)
    for i, digit in enumerate(digits):
        put = (lane == i * SLOTS).astype(f32).astype(bf16)
        coded = coded + jnp.dot(digit.astype(f32).astype(bf16), put, preferred_element_type=f32)
    out_ref[:, D:] = coded.astype(bf16)


def code(queries, positives):
    return pl.pallas_call(
        code_kernel,
        out_shape=jax.ShapeDtypeStruct((ROWS, D + LINE), bf16),
        in_specs=[spec()] * 2,
        out_specs=spec(),
        compiler_params=params(),
        cost_estimate=cost(size=4 * ROWS * D),
        name="code",
    )(queries, positives)


def pack_kernel(*refs):
    out_ref = refs[-1]
    for i, ref in enumerate(refs[:-1]):
        out_ref[i * LINE : (i + 1) * LINE, :] = ref[:LINE, :]
    tails = [ref[LINE:, :] for ref in refs[:-1]]
    out_ref[NX * LINE :, :] = jnp.concatenate(tails, axis=0)


def pack(parts):
    return pl.pallas_call(
        pack_kernel,
        out_shape=jax.ShapeDtypeStruct((NX * (LINE + SLOTS), D), bf16),
        in_specs=[spec()] * 4,
        out_specs=spec(),
        compiler_params=params(),
        cost_estimate=cost(size=4 * NX * LINE * D),
        name="pack",
    )(*parts)


def beside():
    high, core = here_is()[:2]
    plane = (1 + 2 * core) ^ (2 * high)
    return [2 * plane, 2 * plane + 1]


def here():
    first = 4 * lax.axis_index("yhi")
    return [first, first + 1]


def remaining():
    return [block ^ 4 for block in beside() + here()]


def spans_of(blocks):
    return [pl.ds(pl.multiple_of(block * BLOCK, BLOCK), BLOCK) for block in blocks()]


def fill_resid(most, q_ref, pos_ref, wb_ref, out_ref, half, spans):
    for at in spans:
        q = q_ref[at, :]
        hits = [pos_ref[half, j : j + 1, at] for j in range(FAST)]
        for t in range(LAB // TILE):
            rows = slice(t * TILE, (t + 1) * TILE)
            out_ref[rows, at] = fill_tile(contract_last(wb_ref[rows, :], q), hits, t * TILE)
    count = jnp.max(most[...]).astype(i32)

    @pl.when(count > FAST)
    def _():
        for at in spans:
            more_hits(count, pos_ref, half, out_ref, at)


def fill_terms(own_ref, other_ref, wb_own, wb_other, out_ref, spans):
    for i, at in enumerate(spans):
        first = contract_first(own_ref[:, at], wb_own[...])
        second = contract_first(other_ref[:, at], wb_other[...])
        out_ref[i * BLOCK : (i + 1) * BLOCK, :] = (first + second).astype(out_ref.dtype)


def plane_kernel(most, q_ref, pos_ref, wb_own, wb_other, *refs, blocks):
    own_ref, other_ref, out_ref = refs[-3:]
    spans = spans_of(blocks)
    fill_resid(most, q_ref, pos_ref, wb_own, own_ref, 0, spans)
    fill_resid(most, q_ref, pos_ref, wb_other, other_ref, 1, spans)
    fill_terms(own_ref, other_ref, wb_own, wb_other, out_ref, spans)


def plane_terms(most, q, pos, wb, wb_other, blocks, kind, into=()):
    size = 2 * LAB * 2 * BLOCK
    resid = jax.ShapeDtypeStruct((LAB, NQ), bf16)
    return pl.pallas_call(
        lambda *refs: plane_kernel(*refs, blocks=blocks),
        out_shape=(resid, resid, jax.ShapeDtypeStruct((2 * BLOCK, D), kind)),
        in_specs=[spec()] * (5 + len(into)),
        out_specs=(spec(),) * 3,
        input_output_aliases={5 + i: i for i in range(len(into))},
        compiler_params=params(),
        cost_estimate=cost(4 * size * D, 4 * size, 2 * size),
        name="plane",
    )(most, q, pos, wb, wb_other, *into)


def terms_kernel(own_ref, other_ref, wb_own, wb_other, out_ref, *, blocks):
    fill_terms(own_ref, other_ref, wb_own, wb_other, out_ref, spans_of(blocks))


def terms(own, other, wb_own, wb_other, blocks, kind):
    return pl.pallas_call(
        lambda *refs: terms_kernel(*refs, blocks=blocks),
        out_shape=jax.ShapeDtypeStruct((2 * BLOCK, D), kind),
        in_specs=[spec()] * 4,
        out_specs=spec(),
        compiler_params=params(),
        cost_estimate=cost(8 * LAB * BLOCK * D, 4 * 2**20),
        name="terms",
    )(own, other, wb_own, wb_other)


def rest_kernel(most, q_ref, pos_ref, wb_ref, resid_ref, out_ref, *, half):
    fill_resid(most, q_ref, pos_ref, wb_ref, resid_ref, half, spans_of(remaining))
    fill_grad(resid_ref, q_ref, out_ref)


def rest_gradient(most, q, pos, wb, resid, half):
    size = LAB * 4 * BLOCK
    return pl.pallas_call(
        lambda most, q, pos, wb, old, resid, out: rest_kernel(most, q, pos, wb, resid, out, half=half),
        out_shape=(jax.ShapeDtypeStruct((LAB, NQ), bf16), jax.ShapeDtypeStruct((LAB, D), f32)),
        in_specs=[spec()] * 5,
        out_specs=(spec(),) * 2,
        input_output_aliases={4: 0},
        compiler_params=params(),
        cost_estimate=cost(6 * size * D, 8 * size, 2 * size),
        name="rest",
    )(most, q, pos, wb, resid)[1]


def grad_kernel(resid_ref, q_ref, out_ref):
    fill_grad(resid_ref, q_ref, out_ref)


def gradient(resid, q):
    return pl.pallas_call(
        grad_kernel,
        out_shape=jax.ShapeDtypeStruct((LAB, D), f32),
        in_specs=[spec()] * 2,
        out_specs=spec(),
        compiler_params=params(),
        cost_estimate=cost(2 * LAB * NQ * D, 8 * 2**20),
        name="grad",
    )(resid, q)


def adamw(count, grad, weight, first, second):
    first = beta_one * first + (1.0 - beta_one) * grad
    second = beta_two * second + (1.0 - beta_two) * grad * grad
    first_hat = first * (1.0 / (1.0 - beta_one**count))
    second_hat = second * (1.0 / (1.0 - beta_two**count))
    weight = weight - rate * (first_hat / (jnp.sqrt(second_hat) + epsilon) + decay * weight)
    return weight, first, second


def adamw_kernel(count, one, two, w_ref, m_ref, v_ref, w_out, m_out, v_out, *wb_out):
    @pl.loop(0, one.shape[0] // 64)
    def _(t):
        rows = pl.ds(pl.multiple_of(t * 64, 64), 64)
        grad = one[rows, :] + two[rows, :]
        weight, first, second = adamw(count, grad, w_ref[rows, :], m_ref[rows, :], v_ref[rows, :])
        w_out[rows, :] = weight
        m_out[rows, :] = first
        v_out[rows, :] = second
        if wb_out:
            wb_out[0][rows, :] = weight.astype(bf16)


def update(count, last, one, two, weight, first, second):
    full = jax.ShapeDtypeStruct((LAB, D), f32)
    return pl.pallas_call(
        lambda *refs: adamw_kernel(count, *refs),
        out_shape=(full, full, full) + (() if last else (jax.ShapeDtypeStruct((LAB, D), bf16),)),
        in_specs=[spec()] * 5,
        out_specs=(spec(),) * (3 if last else 4),
        compiler_params=params(),
        cost_estimate=cost(20 * LAB * D, 12 * LAB * D, 2 * LAB * D),
        name="adamw",
    )(one, two, weight, first, second)


def moved(move):
    pairs = []
    for x in range(NX):
        for y in range(NY):
            for z in range(NZ):
                for core in range(NCORE):
                    tx, ty, tz, tcore = move(x, y, z, core)
                    name = lambda x, y, z, core: (
                        (((x % NX) * NLO + y % NLO) * NZ + z % NZ) * NCORE + core
                    ) * NHI + (y % NY) // NLO
                    pairs.append((name(x, y, z, core), name(tx, ty, tz, tcore)))
    return pairs


def send(array, move):
    return lax.ppermute(array, AXES, moved(move))


def along_x(by):
    return lambda x, y, z, core: (x ^ by, y, z, core)


def along_y(by):
    return lambda x, y, z, core: (x, y ^ by, z, core)


def along_z(by):
    return lambda x, y, z, core: (x, y, z + by, core)


def by_core(zero, one):
    return lambda x, y, z, core: one(x, y, z, core) if core else zero(x, y, z, core)


def onward(by):
    def move(x, y, z, core):
        place = 2 * z + core + (by if core else -by)
        return x, y, place // 2, place % 2

    return move


def back(by):
    moves = {onward(by)(0, 0, z, core)[2] % NZ * 2 + onward(by)(0, 0, z, core)[3]: (z, core) for z in range(NZ) for core in range(2)}
    return lambda x, y, z, core: (x, y, *moves[2 * z + core])


def swap(array):
    return send(array, lambda x, y, z, core: (x, y, z, 1 - core))


def gather(queries, positives):
    line = code(queries, positives)
    line = jnp.concatenate([line] + [send(line, back(by)) for by in (1, 2, 3)], axis=0)
    line = jnp.concatenate([line, send(line, back(4))], axis=0)
    coded = line[:, D : D + 3 * SLOTS].T
    coded = jnp.concatenate([coded[i * SLOTS : (i + 1) * SLOTS] for i in range(3)], axis=1)
    coded = jnp.pad(coded, ((0, 0), (0, D - 3 * LINE)))
    chip = jnp.concatenate([line[:, :D], coded], axis=0)
    four = [chip] + [send(chip, by_core(along_x(by), along_y(by))) for by in (1, 3, 2)]
    four = pack(four)
    return [four] + [send(four, by_core(along_y(by), along_x(by))) for by in (1, 3, 2)]


def after(array, *others):
    return lax.optimization_barrier((array, *others))


def shards(queries, positives, weights, first_moment, second_moment):
    weight, first, second = weights, first_moment, second_moment
    to_plane = lambda part: send(part, by_core(along_y(1), along_y(3)))
    to_half = lambda plane: send(plane[1:3].astype(bf16), by_core(along_x(1), along_x(3)))
    to_line = lambda plane, got: send(plane[3] + got[1].astype(f32), by_core(along_x(3), along_x(1)))
    as_plane = lambda part, got: (part + got.astype(f32)).reshape(NX, LINE, D)

    wb = weight.astype(bf16)
    wb_other = swap(wb)
    state = ()
    for late, part in zip((0, 1, 3, LAST), gather(queries, positives)):
        *state, theirs = (*first_residuals(part, wb, wb_other, late, state[:5]), None)[:6]
    q, pos, own, other, most = state
    step0 = (own, other, wb, wb_other)

    part = swap(theirs)
    mine = gradient(own, q)
    out0 = terms(*step0, beside, bf16)
    part, mine, out0 = after(part, mine, out0)
    weight, first, second, wb = update(past_steps + 1, False, mine, part, weight, first, second)

    wb_other = swap(wb)
    wb, out0, *step0 = after(wb, out0, *step0)
    out0 = to_plane(out0)
    part0 = terms(*step0, here, f32)
    wb_other, part0 = after(wb_other, part0)
    own, other, out1 = plane_terms(most, q, pos, wb, wb_other, beside, bf16)

    out1, own, other, out0 = after(out1, own, other, out0)
    out1 = to_plane(out1)
    own, other, part1 = plane_terms(most, q, pos, wb, wb_other, here, f32, (own, other))
    plane0 = as_plane(part0, out0)
    half0 = to_half(plane0)
    theirs = rest_gradient(most, q, pos, wb_other, other, 1)
    part = swap(theirs)
    out1, theirs = after(out1, theirs)
    plane1 = as_plane(part1, out1)
    half1 = to_half(plane1)
    quarter0 = to_line(plane0, half0)
    half1, own = after(half1, own)

    quarter1 = to_line(plane1, half1)
    mine = rest_gradient(most, q, pos, wb, own, 0)
    quarter1, mine = after(quarter1, mine)
    line = [
        plane[0] + half[0].astype(f32) + quarter
        for plane, half, quarter in ((plane0, half0, quarter0), (plane1, half1, quarter1))
    ]
    line = jnp.stack([part.reshape(NZ, ROWS, D) for part in line], axis=1)
    got = send(line[4:].astype(bf16), onward(4))
    weight, first, second = update(past_steps + 2, True, mine, part, weight, first, second)
    got, weight, first, second = after(got, weight, first, second)
    line = line[:4] + got.astype(f32)
    got = [send(line[by], onward(by)) for by in (1, 2, 3)]
    return weight, first, second, line[0] + got[0] + got[1] + got[2]


def solution(mesh):
    devices = mesh.devices.reshape(NX, NLO, NZ, NCORE, NHI)
    label = AXES[:4]
    in_specs = (P(AXES, None), P(AXES, None), P(label, None), P(label, None), P(label, None))
    out_specs = (P(label, None), P(label, None), P(label, None), P(None, AXES, None))
    return jax.shard_map(
        shards, mesh=Mesh(devices, AXES), in_specs=in_specs, out_specs=out_specs, check_vma=False
    )
```

```python
import jax
import jax.numpy as jnp
from jax import lax
from jax.experimental import pallas as pl
from jax.experimental.pallas import tpu as pltpu
from jax.sharding import Mesh, PartitionSpec as P

STEPS = 2

beta_one = 0.9
beta_two = 0.95
rate = 0.02
decay = 0.1
epsilon = 1e-08
past_steps = 1000

f32 = jnp.float32
bf16 = jnp.bfloat16
i32 = jnp.int32

NX, NLO, NZ, NCORE, NHI = 4, 2, 8, 2, 2
NY = NLO * NHI
AXES = ("x", "ylo", "z", "core", "yhi")
D = 512
ROWS = 16
SLOTS = 8
LINE = NZ * ROWS
NQ = NX * NY * LINE
BLOCK = 2 * LINE
LAB = 1024
TILE = 256
VMEM = 16 * 2**20
LOG2E = 1.4426950408889634


def spec(shape=None, index=None, space=pltpu.VMEM):
    if shape is None:
        return pl.BlockSpec(memory_space=space)
    return pl.BlockSpec(shape, index, memory_space=space)


def params():
    return pltpu.CompilerParams(vmem_limit_bytes=VMEM)


def cost(flops=0, size=0, exps=0):
    return pl.CostEstimate(flops=flops, bytes_accessed=size, transcendentals=exps)


def descending(rows):
    rows = list(rows)
    for a, b in (
        (0, 1), (2, 3), (4, 5), (6, 7), (0, 2), (1, 3), (4, 6), (5, 7), (1, 2), (5, 6),
        (0, 4), (1, 5), (2, 6), (3, 7), (2, 4), (3, 5), (1, 2), (3, 4), (5, 6),
    ):
        rows[a], rows[b] = jnp.maximum(rows[a], rows[b]), jnp.minimum(rows[a], rows[b])
    return rows


def here_is():
    high, core = lax.axis_index("yhi"), lax.axis_index("core")
    chip = (lax.axis_index("x") * NLO + lax.axis_index("ylo")) * NZ + lax.axis_index("z")
    base = chip * NCORE * LAB
    return high, core, base + core * LAB, base + (1 - core) * LAB


def gray(slot):
    return slot ^ (slot >> 1)


def place_of(late, early):
    high, core = here_is()[:2]
    y = late + core * (early - late)
    x = early + core * (late - early)
    return (y ^ (2 * high)) * NX + ((x + core * (4 - 2 * x)) & 3)


FAST = 2


def contract_last(left, right):
    return lax.dot_general(left, right, (((1,), (1,)), ((), ())), preferred_element_type=f32)


def contract_first(left, right):
    return lax.dot_general(left, right, (((0,), (0,)), ((), ())), preferred_element_type=f32)


def fill_tile(logits, hits, first):
    share = pl.reciprocal(1.0 + jnp.exp2(logits * -LOG2E), approx=True)
    label = lax.broadcasted_iota(i32, logits.shape, 0) + first
    hit = hits[0] == label
    for row in hits[1:]:
        hit = hit | (row == label)
    return jnp.where(hit, share - 1.0, share).astype(bf16)


def more_hits(count, pos_ref, half, out_ref, at):
    @pl.loop(FAST, count)
    def _(j):
        slots = pos_ref[half, :, at]
        slots = jnp.where(lax.broadcasted_iota(i32, slots.shape, 0) == j, slots, -1)
        hit = jnp.max(slots, axis=0, keepdims=True)

        @pl.loop(0, LAB // TILE)
        def _(t):
            rows = pl.ds(pl.multiple_of(t * TILE, TILE), TILE)
            old = out_ref[rows, at].astype(f32)
            label = lax.broadcasted_iota(i32, old.shape, 0) + t * TILE
            out_ref[rows, at] = jnp.where(hit == label, old - 1.0, old).astype(bf16)


def fill_grad(resid_ref, q_ref, out_ref):
    for t in range(LAB // (2 * TILE)):
        rows = slice(2 * TILE * t, 2 * TILE * (t + 1))
        out_ref[rows, :] = jnp.dot(resid_ref[rows, :], q_ref[...], preferred_element_type=f32)


def part_kernel(part_ref, wb_own, wb_other, *refs, late):
    first_labels = here_is()[2:]
    grads = refs[-1:] if late == LAST else ()
    before = refs[4] if late else None
    q_ref, pos_ref, own_ref, other_ref, most_ref = refs[-5 - len(grads) : len(refs) - len(grads)]
    spans = [
        pl.ds(pl.multiple_of(place_of(late, gray(early)) * LINE, LINE), LINE) for early in range(4)
    ]
    coded = part_ref[NX * LINE :, : 3 * LINE].astype(f32)
    ids = coded[:, :LINE] + 256.0 * coded[:, LINE : 2 * LINE] + 65536.0 * coded[:, 2 * LINE :]
    ids = ids.astype(i32)
    rows = []
    for j in range(SLOTS):
        row = jnp.concatenate([ids[SLOTS * early + j : SLOTS * early + j + 1] for early in range(4)], axis=0)
        local = jnp.concatenate([row - first for first in first_labels], axis=0)
        rows.append(jnp.where((local >= 0) & (local < LAB), local, -1))
    rows = descending(rows)
    count = sum((row >= 0).astype(f32) for row in rows)
    most = jnp.max(count).astype(i32)
    most_ref[...] = count if before is None else jnp.maximum(count, before[...])
    rows = rows[:1] + [jnp.where(row == last, -1, row) for last, row in zip(rows, rows[1:])]
    for half in range(2):
        for early, at in enumerate(spans):
            k = 4 * half + early
            for j in range(SLOTS):
                pos_ref[half, j : j + 1, at] = rows[j][k : k + 1]
    for pair in range(2):
        q = part_ref[pair * BLOCK : (pair + 1) * BLOCK, :]
        for half, wb_ref, out_ref in ((1, wb_other, other_ref), (0, wb_own, own_ref)):
            for t in range(LAB // TILE):
                tile = slice(t * TILE, (t + 1) * TILE)
                logits = contract_last(wb_ref[tile, :], q)
                for k in range(2):
                    early = 2 * pair + k
                    hits = [row[4 * half + early : 4 * half + early + 1] for row in rows[:FAST]]
                    out_ref[tile, spans[early]] = fill_tile(logits[:, k * LINE : (k + 1) * LINE], hits, t * TILE)
    for early, at in enumerate(spans):
        q_ref[at, :] = part_ref[early * LINE : (early + 1) * LINE, :]

    @pl.when(most > FAST)
    def _():
        for half, out_ref in enumerate((own_ref, other_ref)):
            for at in spans:
                more_hits(most, pos_ref, half, out_ref, at)

    for out_ref in grads:
        fill_grad(other_ref, q_ref, out_ref)


LAST = 2


def first_residuals(part, wb, wb_other, late, into):
    shapes = (
        jax.ShapeDtypeStruct((NQ, D), bf16),
        jax.ShapeDtypeStruct((2, SLOTS, NQ), i32),
        jax.ShapeDtypeStruct((LAB, NQ), bf16),
        jax.ShapeDtypeStruct((LAB, NQ), bf16),
        jax.ShapeDtypeStruct((2 * NX, LINE), f32),
    )
    if late == LAST:
        shapes += (jax.ShapeDtypeStruct((LAB, D), f32),)
    size = LAB * NX * LINE
    return pl.pallas_call(
        lambda *refs: part_kernel(*refs, late=late),
        out_shape=shapes,
        in_specs=[spec()] * (3 + len(into)),
        out_specs=(spec(),) * len(shapes),
        input_output_aliases={3 + i: i for i in range(len(into))},
        compiler_params=params(),
        cost_estimate=cost((8 if late == LAST else 4) * size * D, 4 * size, 4 * size),
        name="part",
    )(part, wb, wb_other, *into)


def code_kernel(q_ref, pos_ref, out_ref):
    ids = pos_ref[...]
    out_ref[:, :D] = q_ref[...]
    digits = [ids & 255, (ids >> 8) & 255, ids >> 16]
    lane = lax.broadcasted_iota(i32, (SLOTS, LINE), 1) - lax.broadcasted_iota(i32, (SLOTS, LINE), 0)
    coded = jnp.zeros((ROWS, LINE), f32)
    for i, digit in enumerate(digits):
        put = (lane == i * SLOTS).astype(f32).astype(bf16)
        coded = coded + contract_first(digit.astype(f32).astype(bf16), put)
    out_ref[:, D:] = coded.astype(bf16)


def code(queries, positives):
    return pl.pallas_call(
        code_kernel,
        out_shape=jax.ShapeDtypeStruct((ROWS, D + LINE), bf16),
        in_specs=[spec()] * 2,
        out_specs=spec(),
        compiler_params=params(),
        cost_estimate=cost(size=4 * ROWS * D),
        name="code",
    )(queries, positives.T)


def pack_kernel(*refs):
    out_ref = refs[-1]
    for i, ref in enumerate(refs[:-1]):
        out_ref[i * LINE : (i + 1) * LINE, :] = ref[:LINE, :]
    tails = [ref[LINE:, :] for ref in refs[:-1]]
    out_ref[NX * LINE :, :] = jnp.concatenate(tails, axis=0)


def pack(parts):
    return pl.pallas_call(
        pack_kernel,
        out_shape=jax.ShapeDtypeStruct((NX * (LINE + SLOTS), D), bf16),
        in_specs=[spec()] * 4,
        out_specs=spec(),
        compiler_params=params(),
        cost_estimate=cost(size=4 * NX * LINE * D),
        name="pack",
    )(*parts)


def beside():
    high, core = here_is()[:2]
    plane = (1 + 2 * core) ^ (2 * high)
    return [2 * plane, 2 * plane + 1]


def here():
    first = 4 * lax.axis_index("yhi")
    return [first, first + 1]


def remaining():
    return [block ^ 4 for block in beside() + here()]


def spans_of(blocks):
    return [pl.ds(pl.multiple_of(block * BLOCK, BLOCK), BLOCK) for block in blocks()]


def fill_resid(most, q_ref, pos_ref, wb_ref, out_ref, half, spans):
    for at in spans:
        q = q_ref[at, :]
        hits = [pos_ref[half, j : j + 1, at] for j in range(FAST)]
        for t in range(LAB // TILE):
            rows = slice(t * TILE, (t + 1) * TILE)
            out_ref[rows, at] = fill_tile(contract_last(wb_ref[rows, :], q), hits, t * TILE)
    count = jnp.max(most[...]).astype(i32)

    @pl.when(count > FAST)
    def _():
        for at in spans:
            more_hits(count, pos_ref, half, out_ref, at)


def fill_terms(own_ref, other_ref, wb_own, wb_other, out_ref, spans):
    for i, at in enumerate(spans):
        first = contract_first(own_ref[:, at], wb_own[...])
        second = contract_first(other_ref[:, at], wb_other[...])
        out_ref[i * BLOCK : (i + 1) * BLOCK, :] = (first + second).astype(out_ref.dtype)


def plane_kernel(most, q_ref, pos_ref, wb_own, wb_other, *refs, blocks):
    own_ref, other_ref, out_ref = refs[-3:]
    spans = spans_of(blocks)
    fill_resid(most, q_ref, pos_ref, wb_own, own_ref, 0, spans)
    fill_resid(most, q_ref, pos_ref, wb_other, other_ref, 1, spans)
    fill_terms(own_ref, other_ref, wb_own, wb_other, out_ref, spans)


def plane_terms(most, q, pos, wb, wb_other, blocks, kind, into=()):
    size = 2 * LAB * 2 * BLOCK
    resid = jax.ShapeDtypeStruct((LAB, NQ), bf16)
    return pl.pallas_call(
        lambda *refs: plane_kernel(*refs, blocks=blocks),
        out_shape=(resid, resid, jax.ShapeDtypeStruct((2 * BLOCK, D), kind)),
        in_specs=[spec()] * (5 + len(into)),
        out_specs=(spec(),) * 3,
        input_output_aliases={5 + i: i for i in range(len(into))},
        compiler_params=params(),
        cost_estimate=cost(4 * size * D, 4 * size, 2 * size),
        name="plane",
    )(most, q, pos, wb, wb_other, *into)


def terms_kernel(own_ref, other_ref, wb_own, wb_other, out_ref, *, blocks):
    fill_terms(own_ref, other_ref, wb_own, wb_other, out_ref, spans_of(blocks))


def terms(own, other, wb_own, wb_other, blocks, kind):
    return pl.pallas_call(
        lambda *refs: terms_kernel(*refs, blocks=blocks),
        out_shape=jax.ShapeDtypeStruct((2 * BLOCK, D), kind),
        in_specs=[spec()] * 4,
        out_specs=spec(),
        compiler_params=params(),
        cost_estimate=cost(8 * LAB * BLOCK * D, 4 * 2**20),
        name="terms",
    )(own, other, wb_own, wb_other)


def rest_kernel(most, q_ref, pos_ref, wb_ref, resid_ref, out_ref, *, half):
    fill_resid(most, q_ref, pos_ref, wb_ref, resid_ref, half, spans_of(remaining))
    fill_grad(resid_ref, q_ref, out_ref)


def rest_gradient(most, q, pos, wb, resid, half):
    size = LAB * 4 * BLOCK
    return pl.pallas_call(
        lambda most, q, pos, wb, old, resid, out: rest_kernel(most, q, pos, wb, resid, out, half=half),
        out_shape=(jax.ShapeDtypeStruct((LAB, NQ), bf16), jax.ShapeDtypeStruct((LAB, D), f32)),
        in_specs=[spec()] * 5,
        out_specs=(spec(),) * 2,
        input_output_aliases={4: 0},
        compiler_params=params(),
        cost_estimate=cost(6 * size * D, 8 * size, 2 * size),
        name="rest",
    )(most, q, pos, wb, resid)[1]


def grad_kernel(resid_ref, q_ref, out_ref):
    fill_grad(resid_ref, q_ref, out_ref)


def gradient(resid, q):
    return pl.pallas_call(
        grad_kernel,
        out_shape=jax.ShapeDtypeStruct((LAB, D), f32),
        in_specs=[spec()] * 2,
        out_specs=spec(),
        compiler_params=params(),
        cost_estimate=cost(2 * LAB * NQ * D, 8 * 2**20),
        name="grad",
    )(resid, q)


def adamw(count, grad, weight, first, second):
    first = beta_one * first + (1.0 - beta_one) * grad
    second = beta_two * second + (1.0 - beta_two) * grad * grad
    first_hat = first * (1.0 / (1.0 - beta_one**count))
    second_hat = second * (1.0 / (1.0 - beta_two**count))
    weight = weight - rate * (first_hat / (jnp.sqrt(second_hat) + epsilon) + decay * weight)
    return weight, first, second


def adamw_kernel(count, one, two, w_ref, m_ref, v_ref, w_out, m_out, v_out, *wb_out):
    @pl.loop(0, one.shape[0] // 64)
    def _(t):
        rows = pl.ds(pl.multiple_of(t * 64, 64), 64)
        grad = one[rows, :] + two[rows, :]
        weight, first, second = adamw(count, grad, w_ref[rows, :], m_ref[rows, :], v_ref[rows, :])
        w_out[rows, :] = weight
        m_out[rows, :] = first
        v_out[rows, :] = second
        if wb_out:
            wb_out[0][rows, :] = weight.astype(bf16)


def update(count, last, one, two, weight, first, second):
    full = jax.ShapeDtypeStruct((LAB, D), f32)
    tile = spec((TILE, D), lambda i: (i, 0)) if last else spec()
    return pl.pallas_call(
        lambda *refs: adamw_kernel(count, *refs),
        grid=(LAB // TILE,) if last else (),
        out_shape=(full, full, full) + (() if last else (jax.ShapeDtypeStruct((LAB, D), bf16),)),
        in_specs=[tile] * 5,
        out_specs=(tile,) * (3 if last else 4),
        compiler_params=params(),
        cost_estimate=cost(20 * LAB * D, 12 * LAB * D, 2 * LAB * D),
        name="adamw",
    )(one, two, weight, first, second)


def moved(move):
    pairs = []
    for x in range(NX):
        for y in range(NY):
            for z in range(NZ):
                for core in range(NCORE):
                    tx, ty, tz, tcore = move(x, y, z, core)
                    name = lambda x, y, z, core: (
                        (((x % NX) * NLO + y % NLO) * NZ + z % NZ) * NCORE + core
                    ) * NHI + (y % NY) // NLO
                    pairs.append((name(x, y, z, core), name(tx, ty, tz, tcore)))
    return pairs


def send(array, move):
    return lax.ppermute(array, AXES, moved(move))


def along_x(by):
    return lambda x, y, z, core: (x ^ by, y, z, core)


def along_y(by):
    return lambda x, y, z, core: (x, y ^ by, z, core)


def by_core(zero, one):
    return lambda x, y, z, core: one(x, y, z, core) if core else zero(x, y, z, core)


def onward(by):
    def move(x, y, z, core):
        place = 2 * z + core + (by if core else -by)
        return x, y, place // 2, place % 2

    return move


def back(by):
    moves = {onward(by)(0, 0, z, core)[2] % NZ * 2 + onward(by)(0, 0, z, core)[3]: (z, core) for z in range(NZ) for core in range(2)}
    return lambda x, y, z, core: (x, y, *moves[2 * z + core])


def swap(array):
    return send(array, lambda x, y, z, core: (x, y, z, 1 - core))


def gather(queries, positives):
    line = code(queries, positives)
    line = jnp.concatenate([line] + [send(line, back(by)) for by in (1, 2, 3)], axis=0)
    line = jnp.concatenate([line, send(line, back(4))], axis=0)
    coded = line[:, D : D + 3 * SLOTS].T
    coded = jnp.concatenate([coded[i * SLOTS : (i + 1) * SLOTS] for i in range(3)], axis=1)
    coded = jnp.pad(coded, ((0, 0), (0, D - 3 * LINE)))
    chip = jnp.concatenate([line[:, :D], coded], axis=0)
    four = [chip] + [send(chip, by_core(along_x(by), along_y(by))) for by in (1, 3, 2)]
    four = pack(four)
    return [four] + [send(four, by_core(along_y(by), along_x(by))) for by in (1, 3, 2)]


def after(array, *others):
    return lax.optimization_barrier((array, *others))


def shards(queries, positives, weights, first_moment, second_moment):
    weight, first, second = weights, first_moment, second_moment
    to_plane = lambda part: send(part, by_core(along_y(1), along_y(3)))
    to_half = lambda plane: send(plane[1:3].astype(bf16), by_core(along_x(1), along_x(3)))
    to_line = lambda plane, got: send(plane[3] + got[1].astype(f32), by_core(along_x(3), along_x(1)))
    as_plane = lambda part, got: (part + got.astype(f32)).reshape(NX, LINE, D)

    wb = weight.astype(bf16)
    wb_other = swap(wb)
    state = ()
    for late, part in zip((0, 1, 3, LAST), gather(queries, positives)):
        *state, theirs = (*first_residuals(part, wb, wb_other, late, state[:5]), None)[:6]
    q, pos, own, other, most = state
    step0 = (own, other, wb, wb_other)

    part = swap(theirs)
    mine = gradient(own, q)
    out0 = terms(*step0, beside, bf16)
    part, mine, out0 = after(part, mine, out0)
    weight, first, second, wb = update(past_steps + 1, False, mine, part, weight, first, second)

    wb_other = swap(wb)
    wb, out0, *step0 = after(wb, out0, *step0)
    out0 = to_plane(out0)
    part0 = terms(*step0, here, f32)
    wb_other, part0 = after(wb_other, part0)
    own, other, out1 = plane_terms(most, q, pos, wb, wb_other, beside, bf16)

    out1, own, other, out0 = after(out1, own, other, out0)
    out1 = to_plane(out1)
    plane0 = as_plane(part0, out0)
    half0 = to_half(plane0)
    own, other, part1 = plane_terms(most, q, pos, wb, wb_other, here, f32, (own, other))
    half0, part1, other = after(half0, part1, other)
    quarter0 = to_line(plane0, half0)
    theirs = rest_gradient(most, q, pos, wb_other, other, 1)
    part = swap(theirs)
    out1, quarter0, theirs, own = after(out1, quarter0, theirs, own)

    plane1 = as_plane(part1, out1)
    half1 = to_half(plane1)
    mine = rest_gradient(most, q, pos, wb, own, 0)
    half1, mine = after(half1, mine)
    quarter1 = to_line(plane1, half1)
    line = [
        plane[0] + half[0].astype(f32) + quarter
        for plane, half, quarter in ((plane0, half0, quarter0), (plane1, half1, quarter1))
    ]
    line = jnp.stack([part.reshape(NZ, ROWS, D) for part in line], axis=1)
    line = line[:4] + send(line[4:].astype(bf16), onward(4)).astype(f32)
    got = [send(line[by], onward(by)) for by in (1, 2, 3)]
    line = line[0] + got[0] + got[1] + got[2]
    line, mine, part = after(line, mine, part)
    weight, first, second = update(past_steps + 2, True, mine, part, weight, first, second)
    return weight, first, second, line


def solution(mesh):
    devices = mesh.devices.reshape(NX, NLO, NZ, NCORE, NHI)
    label = AXES[:4]
    in_specs = (P(AXES, None), P(AXES, None), P(label, None), P(label, None), P(label, None))
    out_specs = (P(label, None), P(label, None), P(label, None), P(None, AXES, None))
    return jax.shard_map(
        shards, mesh=Mesh(devices, AXES), in_specs=in_specs, out_specs=out_specs, check_vma=False
    )
```

```python
import jax
import jax.numpy as jnp
from jax import lax
from jax.experimental import pallas as pl
from jax.experimental.pallas import tpu as pltpu
from jax.sharding import Mesh, PartitionSpec as P

STEPS = 2

beta_one = 0.9
beta_two = 0.95
rate = 0.02
decay = 0.1
epsilon = 1e-08
past_steps = 1000

f32 = jnp.float32
bf16 = jnp.bfloat16
i32 = jnp.int32

NX, NLO, NZ, NCORE, NHI = 4, 2, 8, 2, 2
NY = NLO * NHI
AXES = ("x", "ylo", "z", "core", "yhi")
D = 512
ROWS = 16
SLOTS = 8
LINE = NZ * ROWS
NQ = NX * NY * LINE
BLOCK = 2 * LINE
LAB = 1024
TILE = 256
VMEM = 16 * 2**20
LOG2E = 1.4426950408889634


def spec(shape=None, index=None, space=pltpu.VMEM):
    if shape is None:
        return pl.BlockSpec(memory_space=space)
    return pl.BlockSpec(shape, index, memory_space=space)


def params():
    return pltpu.CompilerParams(vmem_limit_bytes=VMEM)


def cost(flops=0, size=0, exps=0):
    return pl.CostEstimate(flops=flops, bytes_accessed=size, transcendentals=exps)


def descending(rows):
    rows = list(rows)
    for a, b in (
        (0, 1), (2, 3), (4, 5), (6, 7), (0, 2), (1, 3), (4, 6), (5, 7), (1, 2), (5, 6),
        (0, 4), (1, 5), (2, 6), (3, 7), (2, 4), (3, 5), (1, 2), (3, 4), (5, 6),
    ):
        rows[a], rows[b] = jnp.maximum(rows[a], rows[b]), jnp.minimum(rows[a], rows[b])
    return rows


def here_is():
    high, core = lax.axis_index("yhi"), lax.axis_index("core")
    chip = (lax.axis_index("x") * NLO + lax.axis_index("ylo")) * NZ + lax.axis_index("z")
    base = chip * NCORE * LAB
    return high, core, base + core * LAB, base + (1 - core) * LAB


def gray(slot):
    return slot ^ (slot >> 1)


def place_of(late, early):
    high, core = here_is()[:2]
    y = late + core * (early - late)
    x = early + core * (late - early)
    return (y ^ (2 * high)) * NX + ((x + core * (4 - 2 * x)) & 3)


FAST = 2


def contract_last(left, right):
    return lax.dot_general(left, right, (((1,), (1,)), ((), ())), preferred_element_type=f32)


def contract_first(left, right):
    return lax.dot_general(left, right, (((0,), (0,)), ((), ())), preferred_element_type=f32)


def fill_tile(logits, hits, first):
    share = pl.reciprocal(1.0 + jnp.exp2(logits * -LOG2E), approx=True)
    label = lax.broadcasted_iota(i32, logits.shape, 0) + first
    hit = hits[0] == label
    for row in hits[1:]:
        hit = hit | (row == label)
    return jnp.where(hit, share - 1.0, share).astype(bf16)


def more_hits(count, pos_ref, half, out_ref, at):
    @pl.loop(FAST, count)
    def _(j):
        slots = pos_ref[half, :, at]
        slots = jnp.where(lax.broadcasted_iota(i32, slots.shape, 0) == j, slots, -1)
        hit = jnp.max(slots, axis=0, keepdims=True)

        @pl.loop(0, LAB // TILE)
        def _(t):
            rows = pl.ds(pl.multiple_of(t * TILE, TILE), TILE)
            old = out_ref[rows, at].astype(f32)
            label = lax.broadcasted_iota(i32, old.shape, 0) + t * TILE
            out_ref[rows, at] = jnp.where(hit == label, old - 1.0, old).astype(bf16)


def fill_grad(resid_ref, q_ref, out_ref):
    for t in range(LAB // (2 * TILE)):
        rows = slice(2 * TILE * t, 2 * TILE * (t + 1))
        out_ref[rows, :] = jnp.dot(resid_ref[rows, :], q_ref[...], preferred_element_type=f32)


def part_kernel(part_ref, wb_own, wb_other, *refs, late):
    first_labels = here_is()[2:]
    grads = refs[-1:] if late == LAST else ()
    before = refs[4] if late else None
    q_ref, pos_ref, own_ref, other_ref, most_ref = refs[-5 - len(grads) : len(refs) - len(grads)]
    spans = [
        pl.ds(pl.multiple_of(place_of(late, gray(early)) * LINE, LINE), LINE) for early in range(4)
    ]
    coded = part_ref[NX * LINE :, : 3 * LINE].astype(f32)
    ids = coded[:, :LINE] + 256.0 * coded[:, LINE : 2 * LINE] + 65536.0 * coded[:, 2 * LINE :]
    ids = ids.astype(i32)
    rows = []
    for j in range(SLOTS):
        row = jnp.concatenate([ids[SLOTS * early + j : SLOTS * early + j + 1] for early in range(4)], axis=0)
        local = jnp.concatenate([row - first for first in first_labels], axis=0)
        rows.append(jnp.where((local >= 0) & (local < LAB), local, -1))
    rows = descending(rows)
    count = sum((row >= 0).astype(f32) for row in rows)
    most = jnp.max(count).astype(i32)
    most_ref[...] = count if before is None else jnp.maximum(count, before[...])
    rows = rows[:1] + [jnp.where(row == last, -1, row) for last, row in zip(rows, rows[1:])]
    for half in range(2):
        for early, at in enumerate(spans):
            k = 4 * half + early
            for j in range(SLOTS):
                pos_ref[half, j : j + 1, at] = rows[j][k : k + 1]
    for pair in range(2):
        q = part_ref[pair * BLOCK : (pair + 1) * BLOCK, :]
        for half, wb_ref, out_ref in ((1, wb_other, other_ref), (0, wb_own, own_ref)):
            for t in range(LAB // TILE):
                tile = slice(t * TILE, (t + 1) * TILE)
                logits = contract_last(wb_ref[tile, :], q)
                for k in range(2):
                    early = 2 * pair + k
                    hits = [row[4 * half + early : 4 * half + early + 1] for row in rows[:FAST]]
                    out_ref[tile, spans[early]] = fill_tile(logits[:, k * LINE : (k + 1) * LINE], hits, t * TILE)
    for early, at in enumerate(spans):
        q_ref[at, :] = part_ref[early * LINE : (early + 1) * LINE, :]

    @pl.when(most > FAST)
    def _():
        for half, out_ref in enumerate((own_ref, other_ref)):
            for at in spans:
                more_hits(most, pos_ref, half, out_ref, at)

    for out_ref in grads:
        fill_grad(other_ref, q_ref, out_ref)


LAST = 2


def first_residuals(part, wb, wb_other, late, into):
    shapes = (
        jax.ShapeDtypeStruct((NQ, D), bf16),
        jax.ShapeDtypeStruct((2, SLOTS, NQ), i32),
        jax.ShapeDtypeStruct((LAB, NQ), bf16),
        jax.ShapeDtypeStruct((LAB, NQ), bf16),
        jax.ShapeDtypeStruct((2 * NX, LINE), f32),
    )
    if late == LAST:
        shapes += (jax.ShapeDtypeStruct((LAB, D), f32),)
    size = LAB * NX * LINE
    return pl.pallas_call(
        lambda *refs: part_kernel(*refs, late=late),
        out_shape=shapes,
        in_specs=[spec()] * (3 + len(into)),
        out_specs=(spec(),) * len(shapes),
        input_output_aliases={3 + i: i for i in range(len(into))},
        compiler_params=params(),
        cost_estimate=cost((8 if late == LAST else 4) * size * D, 4 * size, 4 * size),
        name="part",
    )(part, wb, wb_other, *into)


def code_kernel(q_ref, pos_ref, out_ref):
    ids = pos_ref[...]
    out_ref[:, :D] = q_ref[...]
    digits = [ids & 255, (ids >> 8) & 255, ids >> 16]
    lane = lax.broadcasted_iota(i32, (SLOTS, LINE), 1) - lax.broadcasted_iota(i32, (SLOTS, LINE), 0)
    coded = jnp.zeros((ROWS, LINE), f32)
    for i, digit in enumerate(digits):
        put = (lane == i * SLOTS).astype(f32).astype(bf16)
        coded = coded + contract_first(digit.astype(f32).astype(bf16), put)
    out_ref[:, D:] = coded.astype(bf16)


def code(queries, positives):
    return pl.pallas_call(
        code_kernel,
        out_shape=jax.ShapeDtypeStruct((ROWS, D + LINE), bf16),
        in_specs=[spec()] * 2,
        out_specs=spec(),
        compiler_params=params(),
        cost_estimate=cost(size=4 * ROWS * D),
        name="code",
    )(queries, positives.T)


def pack_kernel(*refs):
    out_ref = refs[-1]
    for i, ref in enumerate(refs[:-1]):
        out_ref[i * LINE : (i + 1) * LINE, :] = ref[:LINE, :]
    tails = [ref[LINE:, :] for ref in refs[:-1]]
    out_ref[NX * LINE :, :] = jnp.concatenate(tails, axis=0)


def pack(parts):
    return pl.pallas_call(
        pack_kernel,
        out_shape=jax.ShapeDtypeStruct((NX * (LINE + SLOTS), D), bf16),
        in_specs=[spec()] * 4,
        out_specs=spec(),
        compiler_params=params(),
        cost_estimate=cost(size=4 * NX * LINE * D),
        name="pack",
    )(*parts)


def beside():
    high, core = here_is()[:2]
    plane = (1 + 2 * core) ^ (2 * high)
    return [2 * plane, 2 * plane + 1]


def here():
    first = 4 * lax.axis_index("yhi")
    return [first, first + 1]


def remaining():
    return [block ^ 4 for block in beside() + here()]


def spans_of(blocks):
    return [pl.ds(pl.multiple_of(block * BLOCK, BLOCK), BLOCK) for block in blocks()]


def fill_resid(most, q_ref, pos_ref, wb_ref, out_ref, half, spans):
    for at in spans:
        q = q_ref[at, :]
        hits = [pos_ref[half, j : j + 1, at] for j in range(FAST)]
        for t in range(LAB // TILE):
            rows = slice(t * TILE, (t + 1) * TILE)
            out_ref[rows, at] = fill_tile(contract_last(wb_ref[rows, :], q), hits, t * TILE)
    count = jnp.max(most[...]).astype(i32)

    @pl.when(count > FAST)
    def _():
        for at in spans:
            more_hits(count, pos_ref, half, out_ref, at)


def fill_terms(own_ref, other_ref, wb_own, wb_other, out_ref, spans):
    for i, at in enumerate(spans):
        first = contract_first(own_ref[:, at], wb_own[...])
        second = contract_first(other_ref[:, at], wb_other[...])
        out_ref[i * BLOCK : (i + 1) * BLOCK, :] = (first + second).astype(out_ref.dtype)


def plane_kernel(most, q_ref, pos_ref, wb_own, wb_other, *refs, blocks):
    own_ref, other_ref, out_ref = refs[-3:]
    spans = spans_of(blocks)
    fill_resid(most, q_ref, pos_ref, wb_own, own_ref, 0, spans)
    fill_resid(most, q_ref, pos_ref, wb_other, other_ref, 1, spans)
    fill_terms(own_ref, other_ref, wb_own, wb_other, out_ref, spans)


def plane_terms(most, q, pos, wb, wb_other, blocks, kind, into=()):
    size = 2 * LAB * 2 * BLOCK
    resid = jax.ShapeDtypeStruct((LAB, NQ), bf16)
    return pl.pallas_call(
        lambda *refs: plane_kernel(*refs, blocks=blocks),
        out_shape=(resid, resid, jax.ShapeDtypeStruct((2 * BLOCK, D), kind)),
        in_specs=[spec()] * (5 + len(into)),
        out_specs=(spec(),) * 3,
        input_output_aliases={5 + i: i for i in range(len(into))},
        compiler_params=params(),
        cost_estimate=cost(4 * size * D, 4 * size, 2 * size),
        name="plane",
    )(most, q, pos, wb, wb_other, *into)


def terms_kernel(own_ref, other_ref, wb_own, wb_other, out_ref, *, blocks):
    fill_terms(own_ref, other_ref, wb_own, wb_other, out_ref, spans_of(blocks))


def terms(own, other, wb_own, wb_other, blocks, kind):
    return pl.pallas_call(
        lambda *refs: terms_kernel(*refs, blocks=blocks),
        out_shape=jax.ShapeDtypeStruct((2 * BLOCK, D), kind),
        in_specs=[spec()] * 4,
        out_specs=spec(),
        compiler_params=params(),
        cost_estimate=cost(8 * LAB * BLOCK * D, 4 * 2**20),
        name="terms",
    )(own, other, wb_own, wb_other)


def rest_kernel(most, q_ref, pos_ref, wb_ref, resid_ref, out_ref, *, half):
    fill_resid(most, q_ref, pos_ref, wb_ref, resid_ref, half, spans_of(remaining))
    fill_grad(resid_ref, q_ref, out_ref)


def rest_gradient(most, q, pos, wb, resid, half):
    size = LAB * 4 * BLOCK
    return pl.pallas_call(
        lambda most, q, pos, wb, old, resid, out: rest_kernel(most, q, pos, wb, resid, out, half=half),
        out_shape=(jax.ShapeDtypeStruct((LAB, NQ), bf16), jax.ShapeDtypeStruct((LAB, D), f32)),
        in_specs=[spec()] * 5,
        out_specs=(spec(),) * 2,
        input_output_aliases={4: 0},
        compiler_params=params(),
        cost_estimate=cost(6 * size * D, 8 * size, 2 * size),
        name="rest",
    )(most, q, pos, wb, resid)[1]


def grad_kernel(resid_ref, q_ref, out_ref):
    fill_grad(resid_ref, q_ref, out_ref)


def gradient(resid, q):
    return pl.pallas_call(
        grad_kernel,
        out_shape=jax.ShapeDtypeStruct((LAB, D), f32),
        in_specs=[spec()] * 2,
        out_specs=spec(),
        compiler_params=params(),
        cost_estimate=cost(2 * LAB * NQ * D, 8 * 2**20),
        name="grad",
    )(resid, q)


def adamw(count, grad, weight, first, second):
    first = beta_one * first + (1.0 - beta_one) * grad
    second = beta_two * second + (1.0 - beta_two) * grad * grad
    first_hat = first * (1.0 / (1.0 - beta_one**count))
    second_hat = second * (1.0 / (1.0 - beta_two**count))
    weight = weight - rate * (first_hat / (jnp.sqrt(second_hat) + epsilon) + decay * weight)
    return weight, first, second


def adamw_kernel(count, one, two, w_ref, m_ref, v_ref, w_out, m_out, v_out, *wb_out):
    @pl.loop(0, one.shape[0] // 64)
    def _(t):
        rows = pl.ds(pl.multiple_of(t * 64, 64), 64)
        grad = one[rows, :] + two[rows, :]
        weight, first, second = adamw(count, grad, w_ref[rows, :], m_ref[rows, :], v_ref[rows, :])
        w_out[rows, :] = weight
        m_out[rows, :] = first
        v_out[rows, :] = second
        if wb_out:
            wb_out[0][rows, :] = weight.astype(bf16)


def update(count, last, one, two, weight, first, second):
    full = jax.ShapeDtypeStruct((LAB, D), f32)
    tile = spec((TILE, D), lambda i: (i, 0)) if last else spec()
    return pl.pallas_call(
        lambda *refs: adamw_kernel(count, *refs),
        grid=(LAB // TILE,) if last else (),
        out_shape=(full, full, full) + (() if last else (jax.ShapeDtypeStruct((LAB, D), bf16),)),
        in_specs=[tile] * 5,
        out_specs=(tile,) * (3 if last else 4),
        compiler_params=params(),
        cost_estimate=cost(20 * LAB * D, 12 * LAB * D, 2 * LAB * D),
        name="adamw",
    )(one, two, weight, first, second)


def moved(move):
    pairs = []
    for x in range(NX):
        for y in range(NY):
            for z in range(NZ):
                for core in range(NCORE):
                    tx, ty, tz, tcore = move(x, y, z, core)
                    name = lambda x, y, z, core: (
                        (((x % NX) * NLO + y % NLO) * NZ + z % NZ) * NCORE + core
                    ) * NHI + (y % NY) // NLO
                    pairs.append((name(x, y, z, core), name(tx, ty, tz, tcore)))
    return pairs


def send(array, move):
    return lax.ppermute(array, AXES, moved(move))


def along_x(by):
    return lambda x, y, z, core: (x ^ by, y, z, core)


def along_y(by):
    return lambda x, y, z, core: (x, y ^ by, z, core)


def by_core(zero, one):
    return lambda x, y, z, core: one(x, y, z, core) if core else zero(x, y, z, core)


def onward(by):
    def move(x, y, z, core):
        place = 2 * z + core + (by if core else -by)
        return x, y, place // 2, place % 2

    return move


def back(by):
    moves = {onward(by)(0, 0, z, core)[2] % NZ * 2 + onward(by)(0, 0, z, core)[3]: (z, core) for z in range(NZ) for core in range(2)}
    return lambda x, y, z, core: (x, y, *moves[2 * z + core])


def swap(array):
    return send(array, lambda x, y, z, core: (x, y, z, 1 - core))


def gather(queries, positives):
    line = code(queries, positives)
    line = jnp.concatenate([line] + [send(line, back(by)) for by in (1, 2, 3)], axis=0)
    line = jnp.concatenate([line, send(line, back(4))], axis=0)
    coded = line[:, D : D + 3 * SLOTS].T
    coded = jnp.concatenate([coded[i * SLOTS : (i + 1) * SLOTS] for i in range(3)], axis=1)
    coded = jnp.pad(coded, ((0, 0), (0, D - 3 * LINE)))
    chip = jnp.concatenate([line[:, :D], coded], axis=0)
    four = [chip] + [send(chip, by_core(along_x(by), along_y(by))) for by in (1, 3, 2)]
    four = pack(four)
    return [four] + [send(four, by_core(along_y(by), along_x(by))) for by in (1, 3, 2)]


def after(array, *others):
    return lax.optimization_barrier((array, *others))


def shards(queries, positives, weights, first_moment, second_moment):
    weight, first, second = weights, first_moment, second_moment
    to_plane = lambda part: send(part, by_core(along_y(1), along_y(3)))
    to_half = lambda plane: send(plane[1:3].astype(bf16), by_core(along_x(1), along_x(3)))
    to_line = lambda plane, got: send(plane[3] + got[1].astype(f32), by_core(along_x(3), along_x(1)))
    as_plane = lambda part, got: (part + got.astype(f32)).reshape(NX, LINE, D)

    wb = weight.astype(bf16)
    wb_other = swap(wb)
    state = ()
    for late, part in zip((0, 1, 3, LAST), gather(queries, positives)):
        *state, theirs = (*first_residuals(part, wb, wb_other, late, state[:5]), None)[:6]
    q, pos, own, other, most = state
    step0 = (own, other, wb, wb_other)

    part = swap(theirs)
    mine = gradient(own, q)
    out0 = terms(*step0, beside, bf16)
    part, mine, out0 = after(part, mine, out0)
    weight, first, second, wb = update(past_steps + 1, False, mine, part, weight, first, second)

    wb_other = swap(wb)
    wb, out0, *step0 = after(wb, out0, *step0)
    out0 = to_plane(out0)
    part0 = terms(*step0, here, f32)
    wb_other, part0 = after(wb_other, part0)
    own, other, out1 = plane_terms(most, q, pos, wb, wb_other, beside, bf16)

    out1, own, other = after(out1, own, other)
    out1 = to_plane(out1)
    own, other, part1 = plane_terms(most, q, pos, wb, wb_other, here, f32, (own, other))
    out0, part1 = after(out0, part1)
    plane0 = as_plane(part0, out0)
    half0 = to_half(plane0)
    plane1 = as_plane(part1, out1)

    half1 = to_half(plane1)
    plane1, plane0, other = after(plane1, plane0, other)
    theirs = rest_gradient(most, q, pos, wb_other, other, 1)
    half1, half0, theirs, own = after(half1, half0, theirs, own)

    part = swap(theirs)
    quarter1 = to_line(plane1, half1)
    quarter0 = to_line(plane0, half0)
    mine = rest_gradient(most, q, pos, wb, own, 0)
    quarter1, quarter0, mine = after(quarter1, quarter0, mine)
    line = [
        plane[0] + half[0].astype(f32) + quarter
        for plane, half, quarter in ((plane0, half0, quarter0), (plane1, half1, quarter1))
    ]
    line = jnp.stack([part.reshape(NZ, ROWS, D) for part in line], axis=1)
    got = send(line[4:].astype(bf16), onward(4))
    weight, first, second = update(past_steps + 2, True, mine, part, weight, first, second)
    got, weight, first, second = after(got, weight, first, second)
    line = line[:4] + got.astype(f32)
    got = [send(line[by], onward(by)) for by in (1, 2, 3)]
    return weight, first, second, line[0] + got[0] + got[1] + got[2]


def solution(mesh):
    devices = mesh.devices.reshape(NX, NLO, NZ, NCORE, NHI)
    label = AXES[:4]
    in_specs = (P(AXES, None), P(AXES, None), P(label, None), P(label, None), P(label, None))
    out_specs = (P(label, None), P(label, None), P(label, None), P(None, AXES, None))
    return jax.shard_map(
        shards, mesh=Mesh(devices, AXES), in_specs=in_specs, out_specs=out_specs, check_vma=False
    )
```

```python
import jax
import jax.numpy as jnp
from jax import lax
from jax.experimental import pallas as pl
from jax.experimental.pallas import tpu as pltpu
from jax.sharding import Mesh, PartitionSpec as P

STEPS = 2

beta_one = 0.9
beta_two = 0.95
rate = 0.02
decay = 0.1
epsilon = 1e-08
past_steps = 1000

f32 = jnp.float32
bf16 = jnp.bfloat16
i32 = jnp.int32

NX, NLO, NZ, NCORE, NHI = 4, 2, 8, 2, 2
NY = NLO * NHI
AXES = ("x", "ylo", "z", "core", "yhi")
D = 512
ROWS = 16
SLOTS = 8
LINE = NZ * ROWS
NQ = NX * NY * LINE
BLOCK = 2 * LINE
LAB = 1024
TILE = 256
VMEM = 16 * 2**20
LOG2E = 1.4426950408889634


def spec(shape=None, index=None, space=pltpu.VMEM):
    if shape is None:
        return pl.BlockSpec(memory_space=space)
    return pl.BlockSpec(shape, index, memory_space=space)


def params():
    return pltpu.CompilerParams(vmem_limit_bytes=VMEM)


def cost(flops=0, size=0, exps=0):
    return pl.CostEstimate(flops=flops, bytes_accessed=size, transcendentals=exps)


def descending(rows):
    rows = list(rows)
    for a, b in (
        (0, 1), (2, 3), (4, 5), (6, 7), (0, 2), (1, 3), (4, 6), (5, 7), (1, 2), (5, 6),
        (0, 4), (1, 5), (2, 6), (3, 7), (2, 4), (3, 5), (1, 2), (3, 4), (5, 6),
    ):
        rows[a], rows[b] = jnp.maximum(rows[a], rows[b]), jnp.minimum(rows[a], rows[b])
    return rows


def here_is():
    high, core = lax.axis_index("yhi"), lax.axis_index("core")
    chip = (lax.axis_index("x") * NLO + lax.axis_index("ylo")) * NZ + lax.axis_index("z")
    base = chip * NCORE * LAB
    return high, core, base + core * LAB, base + (1 - core) * LAB


def gray(slot):
    return slot ^ (slot >> 1)


def place_of(late, early):
    high, core = here_is()[:2]
    y = late + core * (early - late)
    x = early + core * (late - early)
    return (y ^ (2 * high)) * NX + ((x + core * (4 - 2 * x)) & 3)


def span(late, early):
    return pl.ds(pl.multiple_of(place_of(late, early) * LINE, LINE), LINE)


FAST = 2


def contract_last(left, right):
    return lax.dot_general(left, right, (((1,), (1,)), ((), ())), preferred_element_type=f32)


def contract_first(left, right):
    return lax.dot_general(left, right, (((0,), (0,)), ((), ())), preferred_element_type=f32)


def fill_tile(logits, hits, first):
    share = pl.reciprocal(1.0 + jnp.exp2(logits * -LOG2E), approx=True)
    label = lax.broadcasted_iota(i32, logits.shape, 0) + first
    hit = hits[0] == label
    for row in hits[1:]:
        hit = hit | (row == label)
    return jnp.where(hit, share - 1.0, share).astype(bf16)


def more_hits(count, pos_ref, half, out_ref, at):
    @pl.loop(FAST, count)
    def _(j):
        slots = pos_ref[half, :, at]
        slots = jnp.where(lax.broadcasted_iota(i32, slots.shape, 0) == j, slots, -1)
        hit = jnp.max(slots, axis=0, keepdims=True)

        @pl.loop(0, LAB // TILE)
        def _(t):
            rows = pl.ds(pl.multiple_of(t * TILE, TILE), TILE)
            old = out_ref[rows, at].astype(f32)
            label = lax.broadcasted_iota(i32, old.shape, 0) + t * TILE
            out_ref[rows, at] = jnp.where(hit == label, old - 1.0, old).astype(bf16)


def fill_grad(resid_ref, q_ref, out_ref):
    @pl.loop(0, LAB // (2 * TILE))
    def _(t):
        rows = pl.ds(pl.multiple_of(2 * TILE * t, 2 * TILE), 2 * TILE)
        out_ref[rows, :] = jnp.dot(resid_ref[rows, :], q_ref[...], preferred_element_type=f32)


def part_kernel(part_ref, wb_own, wb_other, *refs, late):
    first_labels = here_is()[2:]
    grads = refs[-1:] if late == LAST else ()
    before = refs[4] if late else None
    q_ref, pos_ref, own_ref, other_ref, most_ref = refs[-5 - len(grads) : len(refs) - len(grads)]
    spans = [span(late, gray(early)) for early in range(4)]
    coded = part_ref[NX * LINE :, : 3 * LINE].astype(f32)
    ids = coded[:, :LINE] + 256.0 * coded[:, LINE : 2 * LINE] + 65536.0 * coded[:, 2 * LINE :]
    ids = ids.astype(i32)
    rows = []
    for j in range(SLOTS):
        row = jnp.concatenate([ids[SLOTS * early + j : SLOTS * early + j + 1] for early in range(4)], axis=0)
        local = jnp.concatenate([row - first for first in first_labels], axis=0)
        rows.append(jnp.where((local >= 0) & (local < LAB), local, -1))
    rows = descending(rows)
    count = sum((row >= 0).astype(f32) for row in rows)
    most = jnp.max(count).astype(i32)
    most_ref[...] = count if before is None else jnp.maximum(count, before[...])
    rows = rows[:1] + [jnp.where(row == last, -1, row) for last, row in zip(rows, rows[1:])]
    for half in range(2):
        for early, at in enumerate(spans):
            k = 4 * half + early
            for j in range(SLOTS):
                pos_ref[half, j : j + 1, at] = rows[j][k : k + 1]

    @pl.loop(0, 2)
    def _(pair):
        q = part_ref[pl.ds(pl.multiple_of(pair * BLOCK, BLOCK), BLOCK), :]
        ends = [span(late, 3 * pair), span(late, 1 + pair)]
        for half, wb_ref, out_ref in ((1, wb_other, other_ref), (0, wb_own, own_ref)):
            hits = [[pos_ref[half, j : j + 1, at] for j in range(FAST)] for at in ends]
            for t in range(LAB // TILE):
                tile = slice(t * TILE, (t + 1) * TILE)
                logits = contract_last(wb_ref[tile, :], q)
                for k, at in enumerate(ends):
                    out_ref[tile, at] = fill_tile(logits[:, k * LINE : (k + 1) * LINE], hits[k], t * TILE)

    for early, at in enumerate(spans):
        q_ref[at, :] = part_ref[early * LINE : (early + 1) * LINE, :]

    @pl.when(most > FAST)
    def _():
        @pl.loop(0, 4)
        def _(early):
            for half, out_ref in enumerate((own_ref, other_ref)):
                more_hits(most, pos_ref, half, out_ref, span(late, early))

    for out_ref in grads:
        fill_grad(other_ref, q_ref, out_ref)


LAST = 2


def first_residuals(part, wb, wb_other, late, into):
    shapes = (
        jax.ShapeDtypeStruct((NQ, D), bf16),
        jax.ShapeDtypeStruct((2, SLOTS, NQ), i32),
        jax.ShapeDtypeStruct((LAB, NQ), bf16),
        jax.ShapeDtypeStruct((LAB, NQ), bf16),
        jax.ShapeDtypeStruct((2 * NX, LINE), f32),
    )
    if late == LAST:
        shapes += (jax.ShapeDtypeStruct((LAB, D), f32),)
    size = LAB * NX * LINE
    return pl.pallas_call(
        lambda *refs: part_kernel(*refs, late=late),
        out_shape=shapes,
        in_specs=[spec()] * (3 + len(into)),
        out_specs=(spec(),) * len(shapes),
        input_output_aliases={3 + i: i for i in range(len(into))},
        compiler_params=params(),
        cost_estimate=cost((8 if late == LAST else 4) * size * D, 4 * size, 4 * size),
        name="part",
    )(part, wb, wb_other, *into)


def code_kernel(q_ref, pos_ref, out_ref):
    ids = pos_ref[...]
    out_ref[:, :D] = q_ref[...]
    digits = [ids & 255, (ids >> 8) & 255, ids >> 16]
    lane = lax.broadcasted_iota(i32, (SLOTS, LINE), 1) - lax.broadcasted_iota(i32, (SLOTS, LINE), 0)
    coded = jnp.zeros((ROWS, LINE), f32)
    for i, digit in enumerate(digits):
        put = (lane == i * SLOTS).astype(f32).astype(bf16)
        coded = coded + contract_first(digit.astype(f32).astype(bf16), put)
    out_ref[:, D:] = coded.astype(bf16)


def code(queries, positives):
    return pl.pallas_call(
        code_kernel,
        out_shape=jax.ShapeDtypeStruct((ROWS, D + LINE), bf16),
        in_specs=[spec()] * 2,
        out_specs=spec(),
        compiler_params=params(),
        cost_estimate=cost(size=4 * ROWS * D),
        name="code",
    )(queries, positives.T)


def pack_kernel(*refs):
    out_ref = refs[-1]
    for i, ref in enumerate(refs[:-1]):
        out_ref[i * LINE : (i + 1) * LINE, :] = ref[:LINE, :]
    tails = [ref[LINE:, :] for ref in refs[:-1]]
    out_ref[NX * LINE :, :] = jnp.concatenate(tails, axis=0)


def pack(parts):
    return pl.pallas_call(
        pack_kernel,
        out_shape=jax.ShapeDtypeStruct((NX * (LINE + SLOTS), D), bf16),
        in_specs=[spec()] * 4,
        out_specs=spec(),
        compiler_params=params(),
        cost_estimate=cost(size=4 * NX * LINE * D),
        name="pack",
    )(*parts)


def beside():
    high, core = here_is()[:2]
    plane = (1 + 2 * core) ^ (2 * high)
    return [2 * plane, 2 * plane + 1]


def here():
    first = 4 * lax.axis_index("yhi")
    return [first, first + 1]


def remaining():
    return [block ^ 4 for block in beside() + here()]


def chosen(blocks, i):
    block = blocks[0]
    for k in range(1, len(blocks)):
        block = jnp.where(i == k, blocks[k], block)
    return pl.ds(pl.multiple_of(block * BLOCK, BLOCK), BLOCK)


def fill_block(q_ref, pos_ref, wb_ref, out_ref, half, at):
    q = q_ref[at, :]
    hits = [pos_ref[half, j : j + 1, at] for j in range(FAST)]
    for t in range(LAB // TILE):
        rows = slice(t * TILE, (t + 1) * TILE)
        out_ref[rows, at] = fill_tile(contract_last(wb_ref[rows, :], q), hits, t * TILE)


def finish(most, pos_ref, parts, blocks):
    count = jnp.max(most[...]).astype(i32)

    @pl.when(count > FAST)
    def _():
        @pl.loop(0, len(blocks))
        def _(i):
            for half, out_ref in parts:
                more_hits(count, pos_ref, half, out_ref, chosen(blocks, i))


def fill_terms(own_ref, other_ref, wb_own, wb_other, out_ref, blocks):
    @pl.loop(0, len(blocks))
    def _(i):
        at = chosen(blocks, i)
        first = contract_first(own_ref[:, at], wb_own[...])
        second = contract_first(other_ref[:, at], wb_other[...])
        rows = pl.ds(pl.multiple_of(i * BLOCK, BLOCK), BLOCK)
        out_ref[rows, :] = (first + second).astype(out_ref.dtype)


def plane_kernel(most, q_ref, pos_ref, wb_own, wb_other, *refs, blocks):
    own_ref, other_ref, out_ref = refs[-3:]
    blocks = blocks()

    @pl.loop(0, len(blocks))
    def _(i):
        at = chosen(blocks, i)
        fill_block(q_ref, pos_ref, wb_own, own_ref, 0, at)
        fill_block(q_ref, pos_ref, wb_other, other_ref, 1, at)

    finish(most, pos_ref, ((0, own_ref), (1, other_ref)), blocks)
    fill_terms(own_ref, other_ref, wb_own, wb_other, out_ref, blocks)


def plane_terms(most, q, pos, wb, wb_other, blocks, kind, into=()):
    size = 2 * LAB * 2 * BLOCK
    resid = jax.ShapeDtypeStruct((LAB, NQ), bf16)
    return pl.pallas_call(
        lambda *refs: plane_kernel(*refs, blocks=blocks),
        out_shape=(resid, resid, jax.ShapeDtypeStruct((2 * BLOCK, D), kind)),
        in_specs=[spec()] * (5 + len(into)),
        out_specs=(spec(),) * 3,
        input_output_aliases={5 + i: i for i in range(len(into))},
        compiler_params=params(),
        cost_estimate=cost(4 * size * D, 4 * size, 2 * size),
        name="plane",
    )(most, q, pos, wb, wb_other, *into)


def terms_kernel(own_ref, other_ref, wb_own, wb_other, out_ref, *, blocks):
    fill_terms(own_ref, other_ref, wb_own, wb_other, out_ref, blocks())


def terms(own, other, wb_own, wb_other, blocks, kind):
    return pl.pallas_call(
        lambda *refs: terms_kernel(*refs, blocks=blocks),
        out_shape=jax.ShapeDtypeStruct((2 * BLOCK, D), kind),
        in_specs=[spec()] * 4,
        out_specs=spec(),
        compiler_params=params(),
        cost_estimate=cost(8 * LAB * BLOCK * D, 4 * 2**20),
        name="terms",
    )(own, other, wb_own, wb_other)


def rest_kernel(most, q_ref, pos_ref, wb_ref, resid_ref, out_ref, *, half):
    blocks = remaining()

    @pl.loop(0, len(blocks) // 2)
    def _(i):
        for k in range(2):
            fill_block(q_ref, pos_ref, wb_ref, resid_ref, half, chosen(blocks, 2 * i + k))

    finish(most, pos_ref, ((half, resid_ref),), blocks)
    fill_grad(resid_ref, q_ref, out_ref)


def rest_gradient(most, q, pos, wb, resid, half):
    size = LAB * 4 * BLOCK
    return pl.pallas_call(
        lambda most, q, pos, wb, old, resid, out: rest_kernel(most, q, pos, wb, resid, out, half=half),
        out_shape=(jax.ShapeDtypeStruct((LAB, NQ), bf16), jax.ShapeDtypeStruct((LAB, D), f32)),
        in_specs=[spec()] * 5,
        out_specs=(spec(),) * 2,
        input_output_aliases={4: 0},
        compiler_params=params(),
        cost_estimate=cost(6 * size * D, 8 * size, 2 * size),
        name="rest",
    )(most, q, pos, wb, resid)[1]


def grad_kernel(resid_ref, q_ref, out_ref):
    fill_grad(resid_ref, q_ref, out_ref)


def gradient(resid, q):
    return pl.pallas_call(
        grad_kernel,
        out_shape=jax.ShapeDtypeStruct((LAB, D), f32),
        in_specs=[spec()] * 2,
        out_specs=spec(),
        compiler_params=params(),
        cost_estimate=cost(2 * LAB * NQ * D, 8 * 2**20),
        name="grad",
    )(resid, q)


def adamw(count, grad, weight, first, second):
    first = beta_one * first + (1.0 - beta_one) * grad
    second = beta_two * second + (1.0 - beta_two) * grad * grad
    first_hat = first * (1.0 / (1.0 - beta_one**count))
    second_hat = second * (1.0 / (1.0 - beta_two**count))
    weight = weight - rate * (first_hat / (jnp.sqrt(second_hat) + epsilon) + decay * weight)
    return weight, first, second


def adamw_kernel(count, one, two, w_ref, m_ref, v_ref, w_out, m_out, v_out, *wb_out):
    @pl.loop(0, one.shape[0] // 64)
    def _(t):
        rows = pl.ds(pl.multiple_of(t * 64, 64), 64)
        grad = one[rows, :] + two[rows, :]
        weight, first, second = adamw(count, grad, w_ref[rows, :], m_ref[rows, :], v_ref[rows, :])
        w_out[rows, :] = weight
        m_out[rows, :] = first
        v_out[rows, :] = second
        if wb_out:
            wb_out[0][rows, :] = weight.astype(bf16)


def update(count, last, one, two, weight, first, second):
    full = jax.ShapeDtypeStruct((LAB, D), f32)
    tile = spec((TILE, D), lambda i: (i, 0)) if last else spec()
    return pl.pallas_call(
        lambda *refs: adamw_kernel(count, *refs),
        grid=(LAB // TILE,) if last else (),
        out_shape=(full, full, full) + (() if last else (jax.ShapeDtypeStruct((LAB, D), bf16),)),
        in_specs=[tile] * 5,
        out_specs=(tile,) * (3 if last else 4),
        compiler_params=params(),
        cost_estimate=cost(20 * LAB * D, 12 * LAB * D, 2 * LAB * D),
        name="adamw",
    )(one, two, weight, first, second)


def moved(move):
    pairs = []
    for x in range(NX):
        for y in range(NY):
            for z in range(NZ):
                for core in range(NCORE):
                    tx, ty, tz, tcore = move(x, y, z, core)
                    name = lambda x, y, z, core: (
                        (((x % NX) * NLO + y % NLO) * NZ + z % NZ) * NCORE + core
                    ) * NHI + (y % NY) // NLO
                    pairs.append((name(x, y, z, core), name(tx, ty, tz, tcore)))
    return pairs


def send(array, move):
    return lax.ppermute(array, AXES, moved(move))


def along_x(by):
    return lambda x, y, z, core: (x ^ by, y, z, core)


def along_y(by):
    return lambda x, y, z, core: (x, y ^ by, z, core)


def by_core(zero, one):
    return lambda x, y, z, core: one(x, y, z, core) if core else zero(x, y, z, core)


def onward(by):
    def move(x, y, z, core):
        place = 2 * z + core + (by if core else -by)
        return x, y, place // 2, place % 2

    return move


def back(by):
    moves = {onward(by)(0, 0, z, core)[2] % NZ * 2 + onward(by)(0, 0, z, core)[3]: (z, core) for z in range(NZ) for core in range(2)}
    return lambda x, y, z, core: (x, y, *moves[2 * z + core])


def swap(array):
    return send(array, lambda x, y, z, core: (x, y, z, 1 - core))


def gather(queries, positives):
    line = code(queries, positives)
    line = jnp.concatenate([line] + [send(line, back(by)) for by in (1, 2, 3)], axis=0)
    line = jnp.concatenate([line, send(line, back(4))], axis=0)
    coded = line[:, D : D + 3 * SLOTS].T
    coded = jnp.concatenate([coded[i * SLOTS : (i + 1) * SLOTS] for i in range(3)], axis=1)
    coded = jnp.pad(coded, ((0, 0), (0, D - 3 * LINE)))
    chip = jnp.concatenate([line[:, :D], coded], axis=0)
    four = [chip] + [send(chip, by_core(along_x(by), along_y(by))) for by in (1, 3, 2)]
    four = pack(four)
    return [four] + [send(four, by_core(along_y(by), along_x(by))) for by in (1, 3, 2)]


def after(array, *others):
    return lax.optimization_barrier((array, *others))


def shards(queries, positives, weights, first_moment, second_moment):
    weight, first, second = weights, first_moment, second_moment
    to_plane = lambda part: send(part, by_core(along_y(1), along_y(3)))
    to_half = lambda plane: send(plane[1:3].astype(bf16), by_core(along_x(1), along_x(3)))
    to_line = lambda plane, got: send(plane[3] + got[1].astype(f32), by_core(along_x(3), along_x(1)))
    as_plane = lambda part, got: (part + got.astype(f32)).reshape(NX, LINE, D)

    wb = weight.astype(bf16)
    wb_other = swap(wb)
    state = ()
    for late, part in zip((0, 1, 3, LAST), gather(queries, positives)):
        *state, theirs = (*first_residuals(part, wb, wb_other, late, state[:5]), None)[:6]
    q, pos, own, other, most = state
    step0 = (own, other, wb, wb_other)

    part = swap(theirs)
    mine = gradient(own, q)
    out0 = terms(*step0, beside, bf16)
    part, mine, out0 = after(part, mine, out0)
    weight, first, second, wb = update(past_steps + 1, False, mine, part, weight, first, second)

    wb_other = swap(wb)
    wb, out0, *step0 = after(wb, out0, *step0)
    out0 = to_plane(out0)
    part0 = terms(*step0, here, f32)
    wb_other, part0 = after(wb_other, part0)
    own, other, out1 = plane_terms(most, q, pos, wb, wb_other, beside, bf16)

    out1, own, other = after(out1, own, other)
    out1 = to_plane(out1)
    own, other, part1 = plane_terms(most, q, pos, wb, wb_other, here, f32, (own, other))
    out0, part1 = after(out0, part1)
    plane0 = as_plane(part0, out0)
    half0 = to_half(plane0)
    plane1 = as_plane(part1, out1)

    half1 = to_half(plane1)
    plane1, plane0, other = after(plane1, plane0, other)
    theirs = rest_gradient(most, q, pos, wb_other, other, 1)
    half1, half0, theirs, own = after(half1, half0, theirs, own)

    part = swap(theirs)
    quarter1 = to_line(plane1, half1)
    quarter0 = to_line(plane0, half0)
    mine = rest_gradient(most, q, pos, wb, own, 0)
    quarter1, quarter0, mine = after(quarter1, quarter0, mine)
    line = [
        plane[0] + half[0].astype(f32) + quarter
        for plane, half, quarter in ((plane0, half0, quarter0), (plane1, half1, quarter1))
    ]
    line = jnp.stack([part.reshape(NZ, ROWS, D) for part in line], axis=1)
    got = send(line[4:].astype(bf16), onward(4))
    weight, first, second = update(past_steps + 2, True, mine, part, weight, first, second)
    got, weight, first, second = after(got, weight, first, second)
    line = line[:4] + got.astype(f32)
    got = [send(line[by], onward(by)) for by in (1, 2, 3)]
    return weight, first, second, line[0] + got[0] + got[1] + got[2]


def solution(mesh):
    devices = mesh.devices.reshape(NX, NLO, NZ, NCORE, NHI)
    label = AXES[:4]
    in_specs = (P(AXES, None), P(AXES, None), P(label, None), P(label, None), P(label, None))
    out_specs = (P(label, None), P(label, None), P(label, None), P(None, AXES, None))
    return jax.shard_map(
        shards, mesh=Mesh(devices, AXES), in_specs=in_specs, out_specs=out_specs, check_vma=False
    )
```

```python
import jax
import jax.numpy as jnp
from jax import lax
from jax.experimental import pallas as pl
from jax.experimental.pallas import tpu as pltpu
from jax.sharding import Mesh, PartitionSpec as P

STEPS = 2

beta_one = 0.9
beta_two = 0.95
rate = 0.02
decay = 0.1
epsilon = 1e-08
past_steps = 1000

f32 = jnp.float32
bf16 = jnp.bfloat16
i32 = jnp.int32

NX, NLO, NZ, NCORE, NHI = 4, 2, 8, 2, 2
NY = NLO * NHI
AXES = ("x", "ylo", "z", "core", "yhi")
D = 512
ROWS = 16
SLOTS = 8
LINE = NZ * ROWS
NQ = NX * NY * LINE
BLOCK = 2 * LINE
LAB = 1024
TILE = 256
VMEM = 16 * 2**20
LOG2E = 1.4426950408889634


def spec(shape=None, index=None, space=pltpu.VMEM):
    if shape is None:
        return pl.BlockSpec(memory_space=space)
    return pl.BlockSpec(shape, index, memory_space=space)


def params():
    return pltpu.CompilerParams(vmem_limit_bytes=VMEM)


def cost(flops=0, size=0, exps=0):
    return pl.CostEstimate(flops=flops, bytes_accessed=size, transcendentals=exps)


def descending(rows):
    rows = list(rows)
    for a, b in (
        (0, 1), (2, 3), (4, 5), (6, 7), (0, 2), (1, 3), (4, 6), (5, 7), (1, 2), (5, 6),
        (0, 4), (1, 5), (2, 6), (3, 7), (2, 4), (3, 5), (1, 2), (3, 4), (5, 6),
    ):
        rows[a], rows[b] = jnp.maximum(rows[a], rows[b]), jnp.minimum(rows[a], rows[b])
    return rows


def here_is():
    high, core = lax.axis_index("yhi"), lax.axis_index("core")
    chip = (lax.axis_index("x") * NLO + lax.axis_index("ylo")) * NZ + lax.axis_index("z")
    base = chip * NCORE * LAB
    return high, core, base + core * LAB, base + (1 - core) * LAB


def gray(slot):
    return slot ^ (slot >> 1)


def place_of(late, early):
    high, core = here_is()[:2]
    y = late + core * (early - late)
    x = early + core * (late - early)
    return (y ^ (2 * high)) * NX + gray((x + (1 - core) * (4 - 2 * x)) & 3)


def span(late, early):
    return pl.ds(pl.multiple_of(place_of(late, early) * LINE, LINE), LINE)


FAST = 2


def contract_last(left, right):
    return lax.dot_general(left, right, (((1,), (1,)), ((), ())), preferred_element_type=f32)


def contract_first(left, right):
    return lax.dot_general(left, right, (((0,), (0,)), ((), ())), preferred_element_type=f32)


def fill_tile(logits, hits, first):
    share = pl.reciprocal(1.0 + jnp.exp2(logits * -LOG2E), approx=True)
    label = lax.broadcasted_iota(i32, logits.shape, 0) + first
    hit = hits[0] == label
    for row in hits[1:]:
        hit = hit | (row == label)
    return jnp.where(hit, share - 1.0, share).astype(bf16)


def more_hits(count, pos_ref, half, out_ref, at):
    @pl.loop(FAST, count)
    def _(j):
        slots = pos_ref[half, :, at]
        slots = jnp.where(lax.broadcasted_iota(i32, slots.shape, 0) == j, slots, -1)
        hit = jnp.max(slots, axis=0, keepdims=True)

        @pl.loop(0, LAB // TILE)
        def _(t):
            rows = pl.ds(pl.multiple_of(t * TILE, TILE), TILE)
            old = out_ref[rows, at].astype(f32)
            label = lax.broadcasted_iota(i32, old.shape, 0) + t * TILE
            out_ref[rows, at] = jnp.where(hit == label, old - 1.0, old).astype(bf16)


def fill_grad(resid_ref, q_ref, out_ref):
    @pl.loop(0, LAB // (2 * TILE))
    def _(t):
        rows = pl.ds(pl.multiple_of(2 * TILE * t, 2 * TILE), 2 * TILE)
        out_ref[rows, :] = jnp.dot(resid_ref[rows, :], q_ref[...], preferred_element_type=f32)


def part_kernel(part_ref, wb_own, wb_other, *refs, late):
    first_labels = here_is()[2:]
    grads = refs[-1:] if late == LAST else ()
    before = refs[4] if late else None
    q_ref, pos_ref, own_ref, other_ref, most_ref = refs[-5 - len(grads) : len(refs) - len(grads)]
    spans = [span(late, gray(early)) for early in range(4)]
    coded = part_ref[NX * LINE :, : 3 * LINE].astype(f32)
    ids = coded[:, :LINE] + 256.0 * coded[:, LINE : 2 * LINE] + 65536.0 * coded[:, 2 * LINE :]
    ids = ids.astype(i32)
    rows = []
    for j in range(SLOTS):
        row = jnp.concatenate([ids[SLOTS * early + j : SLOTS * early + j + 1] for early in range(4)], axis=0)
        local = jnp.concatenate([row - first for first in first_labels], axis=0)
        rows.append(jnp.where((local >= 0) & (local < LAB), local, -1))
    rows = descending(rows)
    count = sum((row >= 0).astype(f32) for row in rows)
    most = jnp.max(count).astype(i32)
    most_ref[...] = count if before is None else jnp.maximum(count, before[...])
    rows = rows[:1] + [jnp.where(row == last, -1, row) for last, row in zip(rows, rows[1:])]
    for half in range(2):
        for early, at in enumerate(spans):
            k = 4 * half + early
            for j in range(SLOTS):
                pos_ref[half, j : j + 1, at] = rows[j][k : k + 1]

    @pl.loop(0, 2)
    def _(pair):
        q = part_ref[pl.ds(pl.multiple_of(pair * BLOCK, BLOCK), BLOCK), :]
        ends = [span(late, 3 * pair), span(late, 1 + pair)]
        for half, wb_ref, out_ref in ((1, wb_other, other_ref), (0, wb_own, own_ref)):
            hits = [[pos_ref[half, j : j + 1, at] for j in range(FAST)] for at in ends]
            for t in range(LAB // TILE):
                tile = slice(t * TILE, (t + 1) * TILE)
                logits = contract_last(wb_ref[tile, :], q)
                for k, at in enumerate(ends):
                    out_ref[tile, at] = fill_tile(logits[:, k * LINE : (k + 1) * LINE], hits[k], t * TILE)

    for early, at in enumerate(spans):
        q_ref[at, :] = part_ref[early * LINE : (early + 1) * LINE, :]

    @pl.when(most > FAST)
    def _():
        @pl.loop(0, 4)
        def _(early):
            for half, out_ref in enumerate((own_ref, other_ref)):
                more_hits(most, pos_ref, half, out_ref, span(late, early))

    for out_ref in grads:
        fill_grad(other_ref, q_ref, out_ref)


LAST = 2


def first_residuals(part, wb, wb_other, late, into):
    shapes = (
        jax.ShapeDtypeStruct((NQ, D), bf16),
        jax.ShapeDtypeStruct((2, SLOTS, NQ), i32),
        jax.ShapeDtypeStruct((LAB, NQ), bf16),
        jax.ShapeDtypeStruct((LAB, NQ), bf16),
        jax.ShapeDtypeStruct((2 * NX, LINE), f32),
    )
    if late == LAST:
        shapes += (jax.ShapeDtypeStruct((LAB, D), f32),)
    size = LAB * NX * LINE
    return pl.pallas_call(
        lambda *refs: part_kernel(*refs, late=late),
        out_shape=shapes,
        in_specs=[spec()] * (3 + len(into)),
        out_specs=(spec(),) * len(shapes),
        input_output_aliases={3 + i: i for i in range(len(into))},
        compiler_params=params(),
        cost_estimate=cost((8 if late == LAST else 4) * size * D, 4 * size, 4 * size),
        name="part",
    )(part, wb, wb_other, *into)


def code_kernel(q_ref, pos_ref, out_ref):
    ids = pos_ref[...]
    out_ref[:, :D] = q_ref[...]
    digits = [ids & 255, (ids >> 8) & 255, ids >> 16]
    lane = lax.broadcasted_iota(i32, (SLOTS, LINE), 1) - lax.broadcasted_iota(i32, (SLOTS, LINE), 0)
    coded = jnp.zeros((ROWS, LINE), f32)
    for i, digit in enumerate(digits):
        put = (lane == i * SLOTS).astype(f32).astype(bf16)
        coded = coded + contract_first(digit.astype(f32).astype(bf16), put)
    out_ref[:, D:] = coded.astype(bf16)


def code(queries, positives):
    return pl.pallas_call(
        code_kernel,
        out_shape=jax.ShapeDtypeStruct((ROWS, D + LINE), bf16),
        in_specs=[spec()] * 2,
        out_specs=spec(),
        compiler_params=params(),
        cost_estimate=cost(size=4 * ROWS * D),
        name="code",
    )(queries, positives.T)


def pack_kernel(*refs):
    out_ref = refs[-1]
    for i, ref in enumerate(refs[:-1]):
        out_ref[i * LINE : (i + 1) * LINE, :] = ref[:LINE, :]
    tails = [ref[LINE:, :] for ref in refs[:-1]]
    out_ref[NX * LINE :, :] = jnp.concatenate(tails, axis=0)


def pack(parts):
    return pl.pallas_call(
        pack_kernel,
        out_shape=jax.ShapeDtypeStruct((NX * (LINE + SLOTS), D), bf16),
        in_specs=[spec()] * 4,
        out_specs=spec(),
        compiler_params=params(),
        cost_estimate=cost(size=4 * NX * LINE * D),
        name="pack",
    )(*parts)


def beside():
    high, core = here_is()[:2]
    plane = (1 + 2 * core) ^ (2 * high)
    return [2 * plane, 2 * plane + 1]


def here():
    first = 4 * lax.axis_index("yhi")
    return [first, first + 1]


def remaining():
    return [block ^ 4 for block in beside() + here()]


def chosen(blocks, i):
    block = blocks[0]
    for k in range(1, len(blocks)):
        block = jnp.where(i == k, blocks[k], block)
    return pl.ds(pl.multiple_of(block * BLOCK, BLOCK), BLOCK)


def fill_block(q_ref, pos_ref, wb_ref, out_ref, half, at):
    q = q_ref[at, :]
    hits = [pos_ref[half, j : j + 1, at] for j in range(FAST)]
    for t in range(LAB // TILE):
        rows = slice(t * TILE, (t + 1) * TILE)
        out_ref[rows, at] = fill_tile(contract_last(wb_ref[rows, :], q), hits, t * TILE)


def finish(most, pos_ref, parts, blocks):
    count = jnp.max(most[...]).astype(i32)

    @pl.when(count > FAST)
    def _():
        @pl.loop(0, len(blocks))
        def _(i):
            for half, out_ref in parts:
                more_hits(count, pos_ref, half, out_ref, chosen(blocks, i))


def fill_terms(own_ref, other_ref, wb_own, wb_other, out_ref, blocks):
    @pl.loop(0, len(blocks))
    def _(i):
        at = chosen(blocks, i)
        first = contract_first(own_ref[:, at], wb_own[...])
        second = contract_first(other_ref[:, at], wb_other[...])
        rows = pl.ds(pl.multiple_of(i * BLOCK, BLOCK), BLOCK)
        out_ref[rows, :] = (first + second).astype(out_ref.dtype)


def plane_kernel(most, q_ref, pos_ref, wb_own, wb_other, *refs, blocks):
    own_ref, other_ref, out_ref = refs[-3:]
    blocks = blocks()

    @pl.loop(0, len(blocks))
    def _(i):
        at = chosen(blocks, i)
        fill_block(q_ref, pos_ref, wb_own, own_ref, 0, at)
        fill_block(q_ref, pos_ref, wb_other, other_ref, 1, at)

    finish(most, pos_ref, ((0, own_ref), (1, other_ref)), blocks)
    fill_terms(own_ref, other_ref, wb_own, wb_other, out_ref, blocks)


def plane_terms(most, q, pos, wb, wb_other, blocks, kind, into=()):
    size = 2 * LAB * 2 * BLOCK
    resid = jax.ShapeDtypeStruct((LAB, NQ), bf16)
    return pl.pallas_call(
        lambda *refs: plane_kernel(*refs, blocks=blocks),
        out_shape=(resid, resid, jax.ShapeDtypeStruct((2 * BLOCK, D), kind)),
        in_specs=[spec()] * (5 + len(into)),
        out_specs=(spec(),) * 3,
        input_output_aliases={5 + i: i for i in range(len(into))},
        compiler_params=params(),
        cost_estimate=cost(4 * size * D, 4 * size, 2 * size),
        name="plane",
    )(most, q, pos, wb, wb_other, *into)


def terms_kernel(own_ref, other_ref, wb_own, wb_other, out_ref, *, blocks):
    fill_terms(own_ref, other_ref, wb_own, wb_other, out_ref, blocks())


def terms(own, other, wb_own, wb_other, blocks, kind):
    return pl.pallas_call(
        lambda *refs: terms_kernel(*refs, blocks=blocks),
        out_shape=jax.ShapeDtypeStruct((2 * BLOCK, D), kind),
        in_specs=[spec()] * 4,
        out_specs=spec(),
        compiler_params=params(),
        cost_estimate=cost(8 * LAB * BLOCK * D, 4 * 2**20),
        name="terms",
    )(own, other, wb_own, wb_other)


def rest_kernel(most, q_ref, pos_ref, wb_ref, resid_ref, out_ref, *, half):
    blocks = remaining()

    @pl.loop(0, len(blocks) // 2)
    def _(i):
        for k in range(2):
            fill_block(q_ref, pos_ref, wb_ref, resid_ref, half, chosen(blocks, 2 * i + k))

    finish(most, pos_ref, ((half, resid_ref),), blocks)
    fill_grad(resid_ref, q_ref, out_ref)


def rest_gradient(most, q, pos, wb, resid, half):
    size = LAB * 4 * BLOCK
    return pl.pallas_call(
        lambda most, q, pos, wb, old, resid, out: rest_kernel(most, q, pos, wb, resid, out, half=half),
        out_shape=(jax.ShapeDtypeStruct((LAB, NQ), bf16), jax.ShapeDtypeStruct((LAB, D), f32)),
        in_specs=[spec()] * 5,
        out_specs=(spec(),) * 2,
        input_output_aliases={4: 0},
        compiler_params=params(),
        cost_estimate=cost(6 * size * D, 8 * size, 2 * size),
        name="rest",
    )(most, q, pos, wb, resid)[1]


def grad_kernel(resid_ref, q_ref, out_ref):
    fill_grad(resid_ref, q_ref, out_ref)


def gradient(resid, q):
    return pl.pallas_call(
        grad_kernel,
        out_shape=jax.ShapeDtypeStruct((LAB, D), f32),
        in_specs=[spec()] * 2,
        out_specs=spec(),
        compiler_params=params(),
        cost_estimate=cost(2 * LAB * NQ * D, 8 * 2**20),
        name="grad",
    )(resid, q)


def adamw(count, grad, weight, first, second):
    first = beta_one * first + (1.0 - beta_one) * grad
    second = beta_two * second + (1.0 - beta_two) * grad * grad
    first_hat = first * (1.0 / (1.0 - beta_one**count))
    second_hat = second * (1.0 / (1.0 - beta_two**count))
    weight = weight - rate * (first_hat / (jnp.sqrt(second_hat) + epsilon) + decay * weight)
    return weight, first, second


def adamw_kernel(count, one, two, w_ref, m_ref, v_ref, w_out, m_out, v_out, *wb_out):
    @pl.loop(0, one.shape[0] // 64)
    def _(t):
        rows = pl.ds(pl.multiple_of(t * 64, 64), 64)
        grad = one[rows, :] + two[rows, :]
        weight, first, second = adamw(count, grad, w_ref[rows, :], m_ref[rows, :], v_ref[rows, :])
        w_out[rows, :] = weight
        m_out[rows, :] = first
        v_out[rows, :] = second
        if wb_out:
            wb_out[0][rows, :] = weight.astype(bf16)


def update(count, last, one, two, weight, first, second):
    full = jax.ShapeDtypeStruct((LAB, D), f32)
    tile = spec((TILE, D), lambda i: (i, 0)) if last else spec()
    return pl.pallas_call(
        lambda *refs: adamw_kernel(count, *refs),
        grid=(LAB // TILE,) if last else (),
        out_shape=(full, full, full) + (() if last else (jax.ShapeDtypeStruct((LAB, D), bf16),)),
        in_specs=[tile] * 5,
        out_specs=(tile,) * (3 if last else 4),
        compiler_params=params(),
        cost_estimate=cost(20 * LAB * D, 12 * LAB * D, 2 * LAB * D),
        name="adamw",
    )(one, two, weight, first, second)


def moved(move):
    pairs = []
    for x in range(NX):
        for y in range(NY):
            for z in range(NZ):
                for core in range(NCORE):
                    tx, ty, tz, tcore = move(x, y, z, core)
                    name = lambda x, y, z, core: (
                        (((x % NX) * NLO + y % NLO) * NZ + z % NZ) * NCORE + core
                    ) * NHI + (y % NY) // NLO
                    pairs.append((name(x, y, z, core), name(tx, ty, tz, tcore)))
    return pairs


def send(array, move):
    return lax.ppermute(array, AXES, moved(move))


def along_x(by):
    return lambda x, y, z, core: (x ^ by, y, z, core)


def along_y(by):
    return lambda x, y, z, core: (x, y ^ by, z, core)


def by_core(zero, one):
    return lambda x, y, z, core: one(x, y, z, core) if core else zero(x, y, z, core)


def onward(by):
    def move(x, y, z, core):
        place = 2 * z + core + (by if core else -by)
        return x, y, place // 2, place % 2

    return move


def back(by):
    moves = {onward(by)(0, 0, z, core)[2] % NZ * 2 + onward(by)(0, 0, z, core)[3]: (z, core) for z in range(NZ) for core in range(2)}
    return lambda x, y, z, core: (x, y, *moves[2 * z + core])


def then(one, two):
    return lambda *at: two(*(i % n for i, n in zip(one(*at), (NX, NY, NZ, NCORE))))


def swap(array):
    return send(array, lambda x, y, z, core: (x, y, z, 1 - core))


def gather(queries, positives):
    line = code(queries, positives)
    line = jnp.concatenate([line] + [send(line, back(by)) for by in (1, 2, 3)], axis=0)
    line = jnp.concatenate([line, send(line, back(4))], axis=0)
    coded = line[:, D : D + 3 * SLOTS].T
    coded = jnp.concatenate([coded[i * SLOTS : (i + 1) * SLOTS] for i in range(3)], axis=1)
    coded = jnp.pad(coded, ((0, 0), (0, D - 3 * LINE)))
    chip = jnp.concatenate([line[:, :D], coded], axis=0)
    four = [chip] + [send(chip, by_core(along_x(by), along_y(by))) for by in (1, 3, 2)]
    four = pack(four)
    return [four] + [send(four, by_core(along_y(by), along_x(by))) for by in (1, 3, 2)]


def after(array, *others):
    return lax.optimization_barrier((array, *others))


def shards(queries, positives, weights, first_moment, second_moment):
    weight, first, second = weights, first_moment, second_moment
    over_y = by_core(along_y(1), along_y(3))
    first_x = by_core(along_x(1), along_x(3))
    second_x = by_core(along_x(3), along_x(1))

    wb = weight.astype(bf16)
    wb_other = swap(wb)
    state = ()
    for late, part in zip((0, 1, 3, LAST), gather(queries, positives)):
        *state, theirs = (*first_residuals(part, wb, wb_other, late, state[:5]), None)[:6]
    q, pos, own, other, most = state
    step0 = (own, other, wb, wb_other)

    part = swap(theirs)
    mine = gradient(own, q)
    out0 = terms(*step0, beside, bf16)
    part, mine, out0 = after(part, mine, out0)
    weight, first, second, wb = update(past_steps + 1, False, mine, part, weight, first, second)

    wb_other = swap(wb)
    wb, out0, *step0 = after(wb, out0, *step0)
    out0 = send(out0, over_y)
    part0 = terms(*step0, here, f32)
    wb_other, part0 = after(wb_other, part0)
    own, other, out1 = plane_terms(most, q, pos, wb, wb_other, beside, bf16)

    out1, own, other = after(out1, own, other)
    got = [send(out1[:BLOCK], over_y), send(out1[BLOCK:], then(over_y, first_x))]
    own, other, part1 = plane_terms(most, q, pos, wb, wb_other, here, f32, (own, other))
    out0, part1 = after(out0, part1)
    got.append(send(part1[BLOCK:].astype(bf16), first_x))
    part0 = part0 + out0.astype(f32)
    half0 = send(part0[BLOCK:].astype(bf16), first_x)

    part1, part0, other = after(part1, part0, other)
    theirs = rest_gradient(most, q, pos, wb_other, other, 1)
    *got, half0, theirs, own = after(*got, half0, theirs, own)
    part = swap(theirs)
    pair0 = part0[:BLOCK] + half0.astype(f32)
    pair1 = part1[:BLOCK] + got[0].astype(f32) + got[1].astype(f32) + got[2].astype(f32)

    lines = jnp.stack([pair.reshape(2, NZ, ROWS, D) for pair in (pair0, pair1)], axis=2)
    far = lines.astype(bf16)
    got = [send(far[1, :4], second_x), send(far[0, 4:], onward(4)), send(far[1, 4:], then(second_x, onward(4)))]
    lines, own = after(lines, own)
    mine = rest_gradient(most, q, pos, wb, own, 0)
    *got, mine = after(*got, mine)
    line = lines[0, :4] + got[0].astype(f32) + got[1].astype(f32) + got[2].astype(f32)

    got = [send(line[by], onward(by)) for by in (1, 2, 3)]
    line, mine = after(line, mine)
    weight, first, second = update(past_steps + 2, True, mine, part, weight, first, second)
    *got, weight, first, second = after(*got, weight, first, second)
    return weight, first, second, line[0] + got[0] + got[1] + got[2]


def solution(mesh):
    devices = mesh.devices.reshape(NX, NLO, NZ, NCORE, NHI)
    label = AXES[:4]
    in_specs = (P(AXES, None), P(AXES, None), P(label, None), P(label, None), P(label, None))
    out_specs = (P(label, None), P(label, None), P(label, None), P(None, AXES, None))
    return jax.shard_map(
        shards, mesh=Mesh(devices, AXES), in_specs=in_specs, out_specs=out_specs, check_vma=False
    )
```

```python
import jax
import jax.numpy as jnp
from jax import lax
from jax.experimental import pallas as pl
from jax.experimental.pallas import tpu as pltpu
from jax.sharding import Mesh, PartitionSpec as P

STEPS = 2

beta_one = 0.9
beta_two = 0.95
rate = 0.02
decay = 0.1
epsilon = 1e-08
past_steps = 1000

f32 = jnp.float32
bf16 = jnp.bfloat16
i32 = jnp.int32

NX, NLO, NZ, NCORE, NHI = 4, 2, 8, 2, 2
NY = NLO * NHI
AXES = ("x", "ylo", "z", "core", "yhi")
D = 512
ROWS = 16
SLOTS = 8
LINE = NZ * ROWS
NQ = NX * NY * LINE
BLOCK = 2 * LINE
LAB = 1024
TILE = 256
VMEM = 16 * 2**20
LOG2E = 1.4426950408889634


def spec(shape=None, index=None, space=pltpu.VMEM):
    if shape is None:
        return pl.BlockSpec(memory_space=space)
    return pl.BlockSpec(shape, index, memory_space=space)


def params():
    return pltpu.CompilerParams(vmem_limit_bytes=VMEM)


def cost(flops=0, size=0, exps=0):
    return pl.CostEstimate(flops=flops, bytes_accessed=size, transcendentals=exps)


def descending(rows):
    rows = list(rows)
    for a, b in (
        (0, 1), (2, 3), (4, 5), (6, 7), (0, 2), (1, 3), (4, 6), (5, 7), (1, 2), (5, 6),
        (0, 4), (1, 5), (2, 6), (3, 7), (2, 4), (3, 5), (1, 2), (3, 4), (5, 6),
    ):
        rows[a], rows[b] = jnp.maximum(rows[a], rows[b]), jnp.minimum(rows[a], rows[b])
    return rows


def here_is():
    high, core = lax.axis_index("yhi"), lax.axis_index("core")
    chip = (lax.axis_index("x") * NLO + lax.axis_index("ylo")) * NZ + lax.axis_index("z")
    base = chip * NCORE * LAB
    return high, core, base + core * LAB, base + (1 - core) * LAB


def gray(slot):
    return slot ^ (slot >> 1)


def place_of(late, early):
    high, core = here_is()[:2]
    y = late + core * (early - late)
    x = early + core * (late - early)
    return (y ^ (2 * high)) * NX + gray((x + (1 - core) * (4 - 2 * x)) & 3)


def span(late, early):
    return pl.ds(pl.multiple_of(place_of(late, early) * LINE, LINE), LINE)


FAST = 2


def contract_last(left, right):
    return lax.dot_general(left, right, (((1,), (1,)), ((), ())), preferred_element_type=f32)


def contract_first(left, right):
    return lax.dot_general(left, right, (((0,), (0,)), ((), ())), preferred_element_type=f32)


def fill_tile(logits, hits, first):
    share = pl.reciprocal(1.0 + jnp.exp2(logits * -LOG2E), approx=True)
    label = lax.broadcasted_iota(i32, logits.shape, 0) + first
    hit = hits[0] == label
    for row in hits[1:]:
        hit = hit | (row == label)
    return jnp.where(hit, share - 1.0, share).astype(bf16)


def more_hits(count, pos_ref, half, out_ref, at):
    @pl.loop(FAST, count)
    def _(j):
        slots = pos_ref[half, :, at]
        slots = jnp.where(lax.broadcasted_iota(i32, slots.shape, 0) == j, slots, -1)
        hit = jnp.max(slots, axis=0, keepdims=True)

        @pl.loop(0, LAB // TILE)
        def _(t):
            rows = pl.ds(pl.multiple_of(t * TILE, TILE), TILE)
            old = out_ref[rows, at].astype(f32)
            label = lax.broadcasted_iota(i32, old.shape, 0) + t * TILE
            out_ref[rows, at] = jnp.where(hit == label, old - 1.0, old).astype(bf16)


def fill_grad(resid_ref, q_ref, out_ref):
    for t in range(LAB // (2 * TILE)):
        rows = slice(2 * TILE * t, 2 * TILE * (t + 1))
        out_ref[rows, :] = jnp.dot(resid_ref[rows, :], q_ref[...], preferred_element_type=f32)


def part_kernel(part_ref, wb_own, wb_other, *refs, late):
    first_labels = here_is()[2:]
    grads = refs[-1:] if late == LAST else ()
    before = refs[4] if late else None
    q_ref, pos_ref, own_ref, other_ref, most_ref = refs[-5 - len(grads) : len(refs) - len(grads)]
    spans = [span(late, gray(early)) for early in range(4)]
    coded = part_ref[NX * LINE :, : 3 * LINE].astype(f32)
    ids = coded[:, :LINE] + 256.0 * coded[:, LINE : 2 * LINE] + 65536.0 * coded[:, 2 * LINE :]
    ids = ids.astype(i32)
    rows = []
    for j in range(SLOTS):
        row = jnp.concatenate([ids[SLOTS * early + j : SLOTS * early + j + 1] for early in range(4)], axis=0)
        local = jnp.concatenate([row - first for first in first_labels], axis=0)
        rows.append(jnp.where((local >= 0) & (local < LAB), local, -1))
    rows = descending(rows)
    count = sum((row >= 0).astype(f32) for row in rows)
    most = jnp.max(count).astype(i32)
    most_ref[...] = count if before is None else jnp.maximum(count, before[...])
    rows = rows[:1] + [jnp.where(row == last, -1, row) for last, row in zip(rows, rows[1:])]
    for half in range(2):
        for early, at in enumerate(spans):
            k = 4 * half + early
            for j in range(SLOTS):
                pos_ref[half, j : j + 1, at] = rows[j][k : k + 1]

    @pl.loop(0, 2)
    def _(pair):
        q = part_ref[pl.ds(pl.multiple_of(pair * BLOCK, BLOCK), BLOCK), :]
        ends = [span(late, 3 * pair), span(late, 1 + pair)]
        for half, wb_ref, out_ref in ((1, wb_other, other_ref), (0, wb_own, own_ref)):
            hits = [[pos_ref[half, j : j + 1, at] for j in range(FAST)] for at in ends]
            for t in range(LAB // TILE):
                tile = slice(t * TILE, (t + 1) * TILE)
                logits = contract_last(wb_ref[tile, :], q)
                for k, at in enumerate(ends):
                    out_ref[tile, at] = fill_tile(logits[:, k * LINE : (k + 1) * LINE], hits[k], t * TILE)

    for early, at in enumerate(spans):
        q_ref[at, :] = part_ref[early * LINE : (early + 1) * LINE, :]

    @pl.when(most > FAST)
    def _():
        @pl.loop(0, 4)
        def _(early):
            for half, out_ref in enumerate((own_ref, other_ref)):
                more_hits(most, pos_ref, half, out_ref, span(late, early))

    for out_ref in grads:
        fill_grad(other_ref, q_ref, out_ref)


LAST = 2


def first_residuals(part, wb, wb_other, late, into):
    shapes = (
        jax.ShapeDtypeStruct((NQ, D), bf16),
        jax.ShapeDtypeStruct((2, SLOTS, NQ), i32),
        jax.ShapeDtypeStruct((LAB, NQ), bf16),
        jax.ShapeDtypeStruct((LAB, NQ), bf16),
        jax.ShapeDtypeStruct((2 * NX, LINE), f32),
    )
    if late == LAST:
        shapes += (jax.ShapeDtypeStruct((LAB, D), f32),)
    size = LAB * NX * LINE
    return pl.pallas_call(
        lambda *refs: part_kernel(*refs, late=late),
        out_shape=shapes,
        in_specs=[spec()] * (3 + len(into)),
        out_specs=(spec(),) * len(shapes),
        input_output_aliases={3 + i: i for i in range(len(into))},
        compiler_params=params(),
        cost_estimate=cost((8 if late == LAST else 4) * size * D, 4 * size, 4 * size),
        name="part",
    )(part, wb, wb_other, *into)


def code_kernel(q_ref, pos_ref, out_ref):
    ids = pos_ref[...]
    out_ref[:, :D] = q_ref[...]
    digits = [ids & 255, (ids >> 8) & 255, ids >> 16]
    lane = lax.broadcasted_iota(i32, (SLOTS, LINE), 1) - lax.broadcasted_iota(i32, (SLOTS, LINE), 0)
    coded = jnp.zeros((ROWS, LINE), f32)
    for i, digit in enumerate(digits):
        put = (lane == i * SLOTS).astype(f32).astype(bf16)
        coded = coded + contract_first(digit.astype(f32).astype(bf16), put)
    out_ref[:, D:] = coded.astype(bf16)


def code(queries, positives):
    return pl.pallas_call(
        code_kernel,
        out_shape=jax.ShapeDtypeStruct((ROWS, D + LINE), bf16),
        in_specs=[spec()] * 2,
        out_specs=spec(),
        compiler_params=params(),
        cost_estimate=cost(size=4 * ROWS * D),
        name="code",
    )(queries, positives.T)


def pack_kernel(*refs):
    out_ref = refs[-1]
    for i, ref in enumerate(refs[:-1]):
        out_ref[i * LINE : (i + 1) * LINE, :] = ref[:LINE, :]
    tails = [ref[LINE:, :] for ref in refs[:-1]]
    out_ref[NX * LINE :, :] = jnp.concatenate(tails, axis=0)


def pack(parts):
    return pl.pallas_call(
        pack_kernel,
        out_shape=jax.ShapeDtypeStruct((NX * (LINE + SLOTS), D), bf16),
        in_specs=[spec()] * 4,
        out_specs=spec(),
        compiler_params=params(),
        cost_estimate=cost(size=4 * NX * LINE * D),
        name="pack",
    )(*parts)


def beside():
    high, core = here_is()[:2]
    plane = (1 + 2 * core) ^ (2 * high)
    return [2 * plane, 2 * plane + 1]


def here():
    first = 4 * lax.axis_index("yhi")
    return [first, first + 1]


def remaining():
    return [block ^ 4 for block in beside() + here()]


def chosen(blocks, i):
    block = blocks[0]
    for k in range(1, len(blocks)):
        block = jnp.where(i == k, blocks[k], block)
    return pl.ds(pl.multiple_of(block * BLOCK, BLOCK), BLOCK)


def fill_block(q_ref, pos_ref, wb_ref, out_ref, half, at):
    q = q_ref[at, :]
    hits = [pos_ref[half, j : j + 1, at] for j in range(FAST)]
    for t in range(LAB // TILE):
        rows = slice(t * TILE, (t + 1) * TILE)
        out_ref[rows, at] = fill_tile(contract_last(wb_ref[rows, :], q), hits, t * TILE)


def finish(most, pos_ref, parts, blocks):
    count = jnp.max(most[...]).astype(i32)

    @pl.when(count > FAST)
    def _():
        @pl.loop(0, len(blocks))
        def _(i):
            for half, out_ref in parts:
                more_hits(count, pos_ref, half, out_ref, chosen(blocks, i))


def fill_terms(own_ref, other_ref, wb_own, wb_other, out_ref, blocks):
    @pl.loop(0, len(blocks))
    def _(i):
        at = chosen(blocks, i)
        first = contract_first(own_ref[:, at], wb_own[...])
        second = contract_first(other_ref[:, at], wb_other[...])
        rows = pl.ds(pl.multiple_of(i * BLOCK, BLOCK), BLOCK)
        out_ref[rows, :] = (first + second).astype(out_ref.dtype)


def plane_kernel(most, q_ref, pos_ref, wb_own, wb_other, *refs, blocks):
    own_ref, other_ref, out_ref = refs[-3:]
    blocks = blocks()

    @pl.loop(0, len(blocks))
    def _(i):
        at = chosen(blocks, i)
        fill_block(q_ref, pos_ref, wb_own, own_ref, 0, at)
        fill_block(q_ref, pos_ref, wb_other, other_ref, 1, at)

    finish(most, pos_ref, ((0, own_ref), (1, other_ref)), blocks)
    fill_terms(own_ref, other_ref, wb_own, wb_other, out_ref, blocks)


def plane_terms(most, q, pos, wb, wb_other, blocks, kind, into=()):
    size = 2 * LAB * 2 * BLOCK
    resid = jax.ShapeDtypeStruct((LAB, NQ), bf16)
    return pl.pallas_call(
        lambda *refs: plane_kernel(*refs, blocks=blocks),
        out_shape=(resid, resid, jax.ShapeDtypeStruct((2 * BLOCK, D), kind)),
        in_specs=[spec()] * (5 + len(into)),
        out_specs=(spec(),) * 3,
        input_output_aliases={5 + i: i for i in range(len(into))},
        compiler_params=params(),
        cost_estimate=cost(4 * size * D, 4 * size, 2 * size),
        name="plane",
    )(most, q, pos, wb, wb_other, *into)


def terms_kernel(own_ref, other_ref, wb_own, wb_other, out_ref, *, blocks):
    fill_terms(own_ref, other_ref, wb_own, wb_other, out_ref, blocks())


def terms(own, other, wb_own, wb_other, blocks, kind):
    return pl.pallas_call(
        lambda *refs: terms_kernel(*refs, blocks=blocks),
        out_shape=jax.ShapeDtypeStruct((2 * BLOCK, D), kind),
        in_specs=[spec()] * 4,
        out_specs=spec(),
        compiler_params=params(),
        cost_estimate=cost(8 * LAB * BLOCK * D, 4 * 2**20),
        name="terms",
    )(own, other, wb_own, wb_other)


def rest_kernel(most, q_ref, pos_ref, wb_ref, resid_ref, out_ref, *, half):
    blocks = remaining()

    @pl.loop(0, len(blocks) // 2)
    def _(i):
        for k in range(2):
            fill_block(q_ref, pos_ref, wb_ref, resid_ref, half, chosen(blocks, 2 * i + k))

    finish(most, pos_ref, ((half, resid_ref),), blocks)
    fill_grad(resid_ref, q_ref, out_ref)


def rest_gradient(most, q, pos, wb, resid, half):
    size = LAB * 4 * BLOCK
    return pl.pallas_call(
        lambda most, q, pos, wb, old, resid, out: rest_kernel(most, q, pos, wb, resid, out, half=half),
        out_shape=(jax.ShapeDtypeStruct((LAB, NQ), bf16), jax.ShapeDtypeStruct((LAB, D), f32)),
        in_specs=[spec()] * 5,
        out_specs=(spec(),) * 2,
        input_output_aliases={4: 0},
        compiler_params=params(),
        cost_estimate=cost(6 * size * D, 8 * size, 2 * size),
        name="rest",
    )(most, q, pos, wb, resid)[1]


def grad_kernel(resid_ref, q_ref, out_ref):
    fill_grad(resid_ref, q_ref, out_ref)


def gradient(resid, q):
    return pl.pallas_call(
        grad_kernel,
        out_shape=jax.ShapeDtypeStruct((LAB, D), f32),
        in_specs=[spec()] * 2,
        out_specs=spec(),
        compiler_params=params(),
        cost_estimate=cost(2 * LAB * NQ * D, 8 * 2**20),
        name="grad",
    )(resid, q)


def adamw(count, grad, weight, first, second):
    first = beta_one * first + (1.0 - beta_one) * grad
    second = beta_two * second + (1.0 - beta_two) * grad * grad
    first_hat = first * (1.0 / (1.0 - beta_one**count))
    second_hat = second * (1.0 / (1.0 - beta_two**count))
    weight = weight - rate * (first_hat / (jnp.sqrt(second_hat) + epsilon) + decay * weight)
    return weight, first, second


def fill_update(count, ins, outs, start, size):
    @pl.loop(0, size // 64)
    def _(t):
        rows = pl.ds(pl.multiple_of(start + t * 64, 64), 64)
        one, two, weight, first, second = (ref[rows, :] for ref in ins)
        new = adamw(count, one + two, weight, first, second)
        for ref, value in zip(outs, new + new[:1]):
            ref[rows, :] = value.astype(ref.dtype)


def adamw_kernel(count, *refs):
    fill_update(count, refs[:5], refs[5:], 0, LAB)


def last_adamw_kernel(count, *refs):
    ins, outs, held, sems = refs[:5], refs[5:8], refs[8:11], refs[11]
    copies = []
    for i in range(LAB // TILE):
        fill_update(count, ins, held, i * TILE, TILE)
        rows = slice(i * TILE, (i + 1) * TILE)
        for k in range(3):
            copies.append(pltpu.make_async_copy(held[k].at[rows], outs[k].at[rows], sems.at[i, k]))
            copies[-1].start()
    for copy in copies:
        copy.wait()


def update(count, last, *arrays):
    full = jax.ShapeDtypeStruct((LAB, D), f32)
    kernel = last_adamw_kernel if last else adamw_kernel
    held = [pltpu.VMEM((LAB, D), f32)] * 3 + [pltpu.SemaphoreType.DMA((LAB // TILE, 3))]
    return pl.pallas_call(
        lambda *refs: kernel(count, *refs),
        out_shape=(full, full, full) + (() if last else (jax.ShapeDtypeStruct((LAB, D), bf16),)),
        in_specs=[spec()] * 5,
        out_specs=(spec(space=pl.ANY),) * 3 if last else (spec(),) * 4,
        scratch_shapes=held if last else [],
        compiler_params=params(),
        cost_estimate=cost(20 * LAB * D, 12 * LAB * D, 2 * LAB * D),
        name="adamw",
    )(*arrays)


def moved(move):
    pairs = []
    for x in range(NX):
        for y in range(NY):
            for z in range(NZ):
                for core in range(NCORE):
                    tx, ty, tz, tcore = move(x, y, z, core)
                    name = lambda x, y, z, core: (
                        (((x % NX) * NLO + y % NLO) * NZ + z % NZ) * NCORE + core
                    ) * NHI + (y % NY) // NLO
                    pairs.append((name(x, y, z, core), name(tx, ty, tz, tcore)))
    return pairs


def send(array, move):
    return lax.ppermute(array, AXES, moved(move))


def along_x(by):
    return lambda x, y, z, core: (x ^ by, y, z, core)


def along_y(by):
    return lambda x, y, z, core: (x, y ^ by, z, core)


def by_core(zero, one):
    return lambda x, y, z, core: one(x, y, z, core) if core else zero(x, y, z, core)


def onward(by):
    def move(x, y, z, core):
        place = 2 * z + core + (by if core else -by)
        return x, y, place // 2, place % 2

    return move


def back(by):
    moves = {onward(by)(0, 0, z, core)[2] % NZ * 2 + onward(by)(0, 0, z, core)[3]: (z, core) for z in range(NZ) for core in range(2)}
    return lambda x, y, z, core: (x, y, *moves[2 * z + core])


def then(one, two):
    return lambda *at: two(*(i % n for i, n in zip(one(*at), (NX, NY, NZ, NCORE))))


def swap(array):
    return send(array, lambda x, y, z, core: (x, y, z, 1 - core))


def gather(queries, positives):
    line = code(queries, positives)
    line = jnp.concatenate([line] + [send(line, back(by)) for by in (1, 2, 3)], axis=0)
    line = jnp.concatenate([line, send(line, back(4))], axis=0)
    coded = line[:, D : D + 3 * SLOTS].T
    coded = jnp.concatenate([coded[i * SLOTS : (i + 1) * SLOTS] for i in range(3)], axis=1)
    coded = jnp.pad(coded, ((0, 0), (0, D - 3 * LINE)))
    chip = jnp.concatenate([line[:, :D], coded], axis=0)
    four = [chip] + [send(chip, by_core(along_x(by), along_y(by))) for by in (1, 3, 2)]
    four = pack(four)
    return four


def after(array, *others):
    return lax.optimization_barrier((array, *others))


def shards(queries, positives, weights, first_moment, second_moment):
    weight, first, second = weights, first_moment, second_moment
    over_y = by_core(along_y(1), along_y(3))
    first_x = by_core(along_x(1), along_x(3))
    second_x = by_core(along_x(3), along_x(1))

    wb = weight.astype(bf16)
    wb_other = swap(wb)
    four = gather(queries, positives)
    near = [send(four, by_core(along_y(by), along_x(by))) for by in (1, 3)]
    state = first_residuals(four, wb, wb_other, 0, ())
    far, *state = after(four, *state)
    far = send(far, by_core(along_y(LAST), along_x(LAST)))
    for late, part in zip((1, 3), near):
        state = first_residuals(part, wb, wb_other, late, state)
    q, pos, own, other, most, theirs = first_residuals(far, wb, wb_other, LAST, state)
    step0 = (own, other, wb, wb_other)

    part = swap(theirs)
    mine = gradient(own, q)
    out0 = terms(*step0, beside, bf16)
    part, mine, out0 = after(part, mine, out0)
    weight, first, second, wb = update(past_steps + 1, False, mine, part, weight, first, second)

    wb_other = swap(wb)
    wb, out0, *step0 = after(wb, out0, *step0)
    out0 = send(out0, over_y)
    part0 = terms(*step0, here, f32)
    wb_other, part0 = after(wb_other, part0)
    own, other, out1 = plane_terms(most, q, pos, wb, wb_other, beside, bf16)

    out1, own, other = after(out1, own, other)
    got = [send(out1[:BLOCK], over_y), send(out1[BLOCK:], then(over_y, first_x))]
    own, other, part1 = plane_terms(most, q, pos, wb, wb_other, here, f32, (own, other))
    out0, part1 = after(out0, part1)
    got.append(send(part1[BLOCK:].astype(bf16), first_x))
    part0 = part0 + out0.astype(f32)
    half0 = send(part0[BLOCK:].astype(bf16), first_x)

    part1, part0, other = after(part1, part0, other)
    theirs = rest_gradient(most, q, pos, wb_other, other, 1)
    *got, half0, theirs, own = after(*got, half0, theirs, own)
    part = swap(theirs)
    pair0 = part0[:BLOCK] + half0.astype(f32)
    pair1 = part1[:BLOCK] + got[0].astype(f32) + got[1].astype(f32) + got[2].astype(f32)

    lines = jnp.stack([pair.reshape(2, NZ, ROWS, D) for pair in (pair0, pair1)], axis=2)
    far = lines.astype(bf16)
    got = [send(far[1, :4], second_x), send(far[0, 4:], onward(4)), send(far[1, 4:], then(second_x, onward(4)))]
    lines, own = after(lines, own)
    mine = rest_gradient(most, q, pos, wb, own, 0)
    *got, mine = after(*got, mine)
    line = lines[0, :4] + got[0].astype(f32) + got[1].astype(f32) + got[2].astype(f32)

    got = [send(line[by], onward(by)) for by in (1, 2, 3)]
    line, mine = after(line, mine)
    weight, first, second = update(past_steps + 2, True, mine, part, weight, first, second)
    *got, weight, first, second = after(*got, weight, first, second)
    return weight, first, second, line[0] + got[0] + got[1] + got[2]


def solution(mesh):
    devices = mesh.devices.reshape(NX, NLO, NZ, NCORE, NHI)
    label = AXES[:4]
    in_specs = (P(AXES, None), P(AXES, None), P(label, None), P(label, None), P(label, None))
    out_specs = (P(label, None), P(label, None), P(label, None), P(None, AXES, None))
    return jax.shard_map(
        shards, mesh=Mesh(devices, AXES), in_specs=in_specs, out_specs=out_specs, check_vma=False
    )
```

```python
import jax
import jax.numpy as jnp
from jax import lax
from jax.experimental import pallas as pl
from jax.experimental.pallas import tpu as pltpu
from jax.sharding import Mesh, PartitionSpec as P

STEPS = 2

beta_one = 0.9
beta_two = 0.95
rate = 0.02
decay = 0.1
epsilon = 1e-08
past_steps = 1000

f32 = jnp.float32
bf16 = jnp.bfloat16
i32 = jnp.int32

NX, NLO, NZ, NCORE, NHI = 4, 2, 8, 2, 2
NY = NLO * NHI
AXES = ("x", "ylo", "z", "core", "yhi")
D = 512
ROWS = 16
SLOTS = 8
LINE = NZ * ROWS
NQ = NX * NY * LINE
BLOCK = 2 * LINE
LAB = 1024
TILE = 256
VMEM = 16 * 2**20
LOG2E = 1.4426950408889634


def spec(shape=None, index=None, space=pltpu.VMEM):
    if shape is None:
        return pl.BlockSpec(memory_space=space)
    return pl.BlockSpec(shape, index, memory_space=space)


def params():
    return pltpu.CompilerParams(vmem_limit_bytes=VMEM)


def cost(flops=0, size=0, exps=0):
    return pl.CostEstimate(flops=flops, bytes_accessed=size, transcendentals=exps)


def descending(rows):
    rows = list(rows)
    for a, b in (
        (0, 1), (2, 3), (4, 5), (6, 7), (0, 2), (1, 3), (4, 6), (5, 7), (1, 2), (5, 6),
        (0, 4), (1, 5), (2, 6), (3, 7), (2, 4), (3, 5), (1, 2), (3, 4), (5, 6),
    ):
        rows[a], rows[b] = jnp.maximum(rows[a], rows[b]), jnp.minimum(rows[a], rows[b])
    return rows


def here_is():
    high, core = lax.axis_index("yhi"), lax.axis_index("core")
    chip = (lax.axis_index("x") * NLO + lax.axis_index("ylo")) * NZ + lax.axis_index("z")
    base = chip * NCORE * LAB
    return high, core, base + core * LAB, base + (1 - core) * LAB


def gray(slot):
    return slot ^ (slot >> 1)


def place_of(late, early):
    high, core = here_is()[:2]
    y = late + core * (early - late)
    x = early + core * (late - early)
    return (y ^ (2 * high)) * NX + gray((x + (1 - core) * (4 - 2 * x)) & 3)


def span(late, early):
    return pl.ds(pl.multiple_of(place_of(late, early) * LINE, LINE), LINE)


FAST = 2


def contract_last(left, right):
    return lax.dot_general(left, right, (((1,), (1,)), ((), ())), preferred_element_type=f32)


def contract_first(left, right):
    return lax.dot_general(left, right, (((0,), (0,)), ((), ())), preferred_element_type=f32)


def fill_tile(logits, hits, first):
    share = pl.reciprocal(1.0 + jnp.exp2(logits * -LOG2E), approx=True)
    label = lax.broadcasted_iota(i32, logits.shape, 0) + first
    hit = hits[0] == label
    for row in hits[1:]:
        hit = hit | (row == label)
    return jnp.where(hit, share - 1.0, share).astype(bf16)


def more_hits(count, pos_ref, half, out_ref, at):
    @pl.loop(FAST, count)
    def _(j):
        slots = pos_ref[half, :, at]
        slots = jnp.where(lax.broadcasted_iota(i32, slots.shape, 0) == j, slots, -1)
        hit = jnp.max(slots, axis=0, keepdims=True)

        @pl.loop(0, LAB // TILE)
        def _(t):
            rows = pl.ds(pl.multiple_of(t * TILE, TILE), TILE)
            old = out_ref[rows, at].astype(f32)
            label = lax.broadcasted_iota(i32, old.shape, 0) + t * TILE
            out_ref[rows, at] = jnp.where(hit == label, old - 1.0, old).astype(bf16)


def fill_grad(resid_ref, q_ref, out_ref):
    for t in range(LAB // (2 * TILE)):
        rows = slice(2 * TILE * t, 2 * TILE * (t + 1))
        out_ref[rows, :] = jnp.dot(resid_ref[rows, :], q_ref[...], preferred_element_type=f32)


def part_kernel(part_ref, wb_own, wb_other, *refs, late):
    first_labels = here_is()[2:]
    grads = refs[-1:] if late == LAST else ()
    before = refs[4] if late else None
    q_ref, pos_ref, own_ref, other_ref, most_ref = refs[-5 - len(grads) : len(refs) - len(grads)]
    spans = [span(late, gray(early)) for early in range(4)]
    coded = part_ref[NX * LINE :, : 3 * LINE].astype(f32)
    ids = coded[:, :LINE] + 256.0 * coded[:, LINE : 2 * LINE] + 65536.0 * coded[:, 2 * LINE :]
    ids = ids.astype(i32)
    rows = []
    for j in range(SLOTS):
        row = jnp.concatenate([ids[SLOTS * early + j : SLOTS * early + j + 1] for early in range(4)], axis=0)
        local = jnp.concatenate([row - first for first in first_labels], axis=0)
        rows.append(jnp.where((local >= 0) & (local < LAB), local, -1))
    rows = descending(rows)
    count = sum((row >= 0).astype(f32) for row in rows)
    most = jnp.max(count).astype(i32)
    most_ref[...] = count if before is None else jnp.maximum(count, before[...])
    rows = rows[:1] + [jnp.where(row == last, -1, row) for last, row in zip(rows, rows[1:])]
    for half in range(2):
        for early, at in enumerate(spans):
            k = 4 * half + early
            for j in range(SLOTS):
                pos_ref[half, j : j + 1, at] = rows[j][k : k + 1]

    @pl.loop(0, 2)
    def _(pair):
        q = part_ref[pl.ds(pl.multiple_of(pair * BLOCK, BLOCK), BLOCK), :]
        ends = [span(late, 3 * pair), span(late, 1 + pair)]
        for half, wb_ref, out_ref in ((1, wb_other, other_ref), (0, wb_own, own_ref)):
            hits = [[pos_ref[half, j : j + 1, at] for j in range(FAST)] for at in ends]
            for t in range(LAB // TILE):
                tile = slice(t * TILE, (t + 1) * TILE)
                logits = contract_last(wb_ref[tile, :], q)
                for k, at in enumerate(ends):
                    out_ref[tile, at] = fill_tile(logits[:, k * LINE : (k + 1) * LINE], hits[k], t * TILE)

    for early, at in enumerate(spans):
        q_ref[at, :] = part_ref[early * LINE : (early + 1) * LINE, :]

    @pl.when(most > FAST)
    def _():
        @pl.loop(0, 4)
        def _(early):
            for half, out_ref in enumerate((own_ref, other_ref)):
                more_hits(most, pos_ref, half, out_ref, span(late, early))

    for out_ref in grads:
        fill_grad(other_ref, q_ref, out_ref)


LAST = 2


def first_residuals(part, wb, wb_other, late, into):
    shapes = (
        jax.ShapeDtypeStruct((NQ, D), bf16),
        jax.ShapeDtypeStruct((2, SLOTS, NQ), i32),
        jax.ShapeDtypeStruct((LAB, NQ), bf16),
        jax.ShapeDtypeStruct((LAB, NQ), bf16),
        jax.ShapeDtypeStruct((2 * NX, LINE), f32),
    )
    if late == LAST:
        shapes += (jax.ShapeDtypeStruct((LAB, D), f32),)
    size = LAB * NX * LINE
    return pl.pallas_call(
        lambda *refs: part_kernel(*refs, late=late),
        out_shape=shapes,
        in_specs=[spec()] * (3 + len(into)),
        out_specs=(spec(),) * len(shapes),
        input_output_aliases={3 + i: i for i in range(len(into))},
        compiler_params=params(),
        cost_estimate=cost((8 if late == LAST else 4) * size * D, 4 * size, 4 * size),
        name="part",
    )(part, wb, wb_other, *into)


def code_kernel(q_ref, pos_ref, out_ref, ids_ref, sems):
    rows = pltpu.make_async_copy(q_ref, out_ref.at[:, :D], sems.at[0])
    slots = pltpu.make_async_copy(pos_ref, ids_ref, sems.at[1])
    slots.start()
    rows.start()
    slots.wait()
    ids = ids_ref[...]
    digits = [ids & 255, (ids >> 8) & 255, ids >> 16]
    lane = lax.broadcasted_iota(i32, (SLOTS, LINE), 1) - lax.broadcasted_iota(i32, (SLOTS, LINE), 0)
    coded = jnp.zeros((ROWS, LINE), f32)
    for i, digit in enumerate(digits):
        put = (lane == i * SLOTS).astype(f32).astype(bf16)
        coded = coded + contract_first(digit.astype(f32).astype(bf16), put)
    out_ref[:, D:] = coded.astype(bf16)
    rows.wait()


def code(queries, positives):
    return pl.pallas_call(
        code_kernel,
        out_shape=jax.ShapeDtypeStruct((ROWS, D + LINE), bf16),
        in_specs=[spec(space=pl.ANY)] * 2,
        out_specs=spec(),
        scratch_shapes=[pltpu.VMEM((SLOTS, ROWS), i32), pltpu.SemaphoreType.DMA((2,))],
        compiler_params=params(),
        cost_estimate=cost(size=4 * ROWS * D),
        name="code",
    )(queries, positives.T)


def pack_kernel(*refs):
    out_ref = refs[-1]
    for i, ref in enumerate(refs[:-1]):
        out_ref[i * LINE : (i + 1) * LINE, :] = ref[:LINE, :]
    tails = [ref[LINE:, :] for ref in refs[:-1]]
    out_ref[NX * LINE :, :] = jnp.concatenate(tails, axis=0)


def pack(parts):
    return pl.pallas_call(
        pack_kernel,
        out_shape=jax.ShapeDtypeStruct((NX * (LINE + SLOTS), D), bf16),
        in_specs=[spec()] * 4,
        out_specs=spec(),
        compiler_params=params(),
        cost_estimate=cost(size=4 * NX * LINE * D),
        name="pack",
    )(*parts)


def beside():
    high, core = here_is()[:2]
    plane = (1 + 2 * core) ^ (2 * high)
    return [2 * plane, 2 * plane + 1]


def here():
    first = 4 * lax.axis_index("yhi")
    return [first, first + 1]


def remaining():
    return [block ^ 4 for block in beside() + here()]


def chosen(blocks, i):
    block = blocks[0]
    for k in range(1, len(blocks)):
        block = jnp.where(i == k, blocks[k], block)
    return pl.ds(pl.multiple_of(block * BLOCK, BLOCK), BLOCK)


def fill_block(q_ref, pos_ref, wb_ref, out_ref, half, at):
    q = q_ref[at, :]
    hits = [pos_ref[half, j : j + 1, at] for j in range(FAST)]
    for t in range(LAB // TILE):
        rows = slice(t * TILE, (t + 1) * TILE)
        out_ref[rows, at] = fill_tile(contract_last(wb_ref[rows, :], q), hits, t * TILE)


def finish(most, pos_ref, parts, blocks):
    count = jnp.max(most[...]).astype(i32)

    @pl.when(count > FAST)
    def _():
        @pl.loop(0, len(blocks))
        def _(i):
            for half, out_ref in parts:
                more_hits(count, pos_ref, half, out_ref, chosen(blocks, i))


def fill_terms(own_ref, other_ref, wb_own, wb_other, out_ref, blocks):
    @pl.loop(0, len(blocks))
    def _(i):
        at = chosen(blocks, i)
        first = contract_first(own_ref[:, at], wb_own[...])
        second = contract_first(other_ref[:, at], wb_other[...])
        rows = pl.ds(pl.multiple_of(i * BLOCK, BLOCK), BLOCK)
        out_ref[rows, :] = (first + second).astype(out_ref.dtype)


def plane_kernel(most, q_ref, pos_ref, wb_own, wb_other, *refs, blocks):
    own_ref, other_ref, out_ref = refs[-3:]
    blocks = blocks()

    @pl.loop(0, len(blocks))
    def _(i):
        at = chosen(blocks, i)
        fill_block(q_ref, pos_ref, wb_own, own_ref, 0, at)
        fill_block(q_ref, pos_ref, wb_other, other_ref, 1, at)

    finish(most, pos_ref, ((0, own_ref), (1, other_ref)), blocks)
    fill_terms(own_ref, other_ref, wb_own, wb_other, out_ref, blocks)


def plane_terms(most, q, pos, wb, wb_other, blocks, kind, into=()):
    size = 2 * LAB * 2 * BLOCK
    resid = jax.ShapeDtypeStruct((LAB, NQ), bf16)
    return pl.pallas_call(
        lambda *refs: plane_kernel(*refs, blocks=blocks),
        out_shape=(resid, resid, jax.ShapeDtypeStruct((2 * BLOCK, D), kind)),
        in_specs=[spec()] * (5 + len(into)),
        out_specs=(spec(),) * 3,
        input_output_aliases={5 + i: i for i in range(len(into))},
        compiler_params=params(),
        cost_estimate=cost(4 * size * D, 4 * size, 2 * size),
        name="plane",
    )(most, q, pos, wb, wb_other, *into)


def terms_kernel(own_ref, other_ref, wb_own, wb_other, out_ref, *, blocks):
    fill_terms(own_ref, other_ref, wb_own, wb_other, out_ref, blocks())


def terms(own, other, wb_own, wb_other, blocks, kind):
    return pl.pallas_call(
        lambda *refs: terms_kernel(*refs, blocks=blocks),
        out_shape=jax.ShapeDtypeStruct((2 * BLOCK, D), kind),
        in_specs=[spec()] * 4,
        out_specs=spec(),
        compiler_params=params(),
        cost_estimate=cost(8 * LAB * BLOCK * D, 4 * 2**20),
        name="terms",
    )(own, other, wb_own, wb_other)


def rest_kernel(most, q_ref, pos_ref, wb_ref, resid_ref, out_ref, *, half):
    blocks = remaining()

    @pl.loop(0, len(blocks) // 2)
    def _(i):
        for k in range(2):
            fill_block(q_ref, pos_ref, wb_ref, resid_ref, half, chosen(blocks, 2 * i + k))

    finish(most, pos_ref, ((half, resid_ref),), blocks)
    fill_grad(resid_ref, q_ref, out_ref)


def rest_gradient(most, q, pos, wb, resid, half):
    size = LAB * 4 * BLOCK
    return pl.pallas_call(
        lambda most, q, pos, wb, old, resid, out: rest_kernel(most, q, pos, wb, resid, out, half=half),
        out_shape=(jax.ShapeDtypeStruct((LAB, NQ), bf16), jax.ShapeDtypeStruct((LAB, D), f32)),
        in_specs=[spec()] * 5,
        out_specs=(spec(),) * 2,
        input_output_aliases={4: 0},
        compiler_params=params(),
        cost_estimate=cost(6 * size * D, 8 * size, 2 * size),
        name="rest",
    )(most, q, pos, wb, resid)[1]


def grad_kernel(resid_ref, q_ref, out_ref):
    fill_grad(resid_ref, q_ref, out_ref)


def gradient(resid, q):
    return pl.pallas_call(
        grad_kernel,
        out_shape=jax.ShapeDtypeStruct((LAB, D), f32),
        in_specs=[spec()] * 2,
        out_specs=spec(),
        compiler_params=params(),
        cost_estimate=cost(2 * LAB * NQ * D, 8 * 2**20),
        name="grad",
    )(resid, q)


def adamw(count, grad, weight, first, second):
    first = beta_one * first + (1.0 - beta_one) * grad
    second = beta_two * second + (1.0 - beta_two) * grad * grad
    first_hat = first * (1.0 / (1.0 - beta_one**count))
    second_hat = second * (1.0 / (1.0 - beta_two**count))
    weight = weight - rate * (first_hat / (jnp.sqrt(second_hat) + epsilon) + decay * weight)
    return weight, first, second


def fill_update(count, ins, outs, start, size):
    @pl.loop(0, size // 64)
    def _(t):
        rows = pl.ds(pl.multiple_of(start + t * 64, 64), 64)
        one, two, weight, first, second = (ref[rows, :] for ref in ins)
        new = adamw(count, one + two, weight, first, second)
        for ref, value in zip(outs, new + new[:1]):
            ref[rows, :] = value.astype(ref.dtype)


def adamw_kernel(count, *refs):
    fill_update(count, refs[:5], refs[5:], 0, LAB)


def last_adamw_kernel(count, *refs):
    ins, outs, held, sems = refs[:5], refs[5:8], refs[8:11], refs[11]
    copies = []
    for i in range(LAB // TILE):
        fill_update(count, ins, held, i * TILE, TILE)
        rows = slice(i * TILE, (i + 1) * TILE)
        for k in range(3):
            copies.append(pltpu.make_async_copy(held[k].at[rows], outs[k].at[rows], sems.at[i, k]))
            copies[-1].start()
    for copy in copies:
        copy.wait()


def update(count, last, *arrays):
    full = jax.ShapeDtypeStruct((LAB, D), f32)
    kernel = last_adamw_kernel if last else adamw_kernel
    held = [pltpu.VMEM((LAB, D), f32)] * 3 + [pltpu.SemaphoreType.DMA((LAB // TILE, 3))]
    return pl.pallas_call(
        lambda *refs: kernel(count, *refs),
        out_shape=(full, full, full) + (() if last else (jax.ShapeDtypeStruct((LAB, D), bf16),)),
        in_specs=[spec()] * 5,
        out_specs=(spec(space=pl.ANY),) * 3 if last else (spec(),) * 4,
        scratch_shapes=held if last else [],
        compiler_params=params(),
        cost_estimate=cost(20 * LAB * D, 12 * LAB * D, 2 * LAB * D),
        name="adamw",
    )(*arrays)


def moved(move):
    pairs = []
    for x in range(NX):
        for y in range(NY):
            for z in range(NZ):
                for core in range(NCORE):
                    tx, ty, tz, tcore = move(x, y, z, core)
                    name = lambda x, y, z, core: (
                        (((x % NX) * NLO + y % NLO) * NZ + z % NZ) * NCORE + core
                    ) * NHI + (y % NY) // NLO
                    pairs.append((name(x, y, z, core), name(tx, ty, tz, tcore)))
    return pairs


def send(array, move):
    return lax.ppermute(array, AXES, moved(move))


def along_x(by):
    return lambda x, y, z, core: (x ^ by, y, z, core)


def along_y(by):
    return lambda x, y, z, core: (x, y ^ by, z, core)


def by_core(zero, one):
    return lambda x, y, z, core: one(x, y, z, core) if core else zero(x, y, z, core)


def onward(by):
    def move(x, y, z, core):
        place = 2 * z + core + (by if core else -by)
        return x, y, place // 2, place % 2

    return move


def back(by):
    moves = {onward(by)(0, 0, z, core)[2] % NZ * 2 + onward(by)(0, 0, z, core)[3]: (z, core) for z in range(NZ) for core in range(2)}
    return lambda x, y, z, core: (x, y, *moves[2 * z + core])


def then(one, two):
    return lambda *at: two(*(i % n for i, n in zip(one(*at), (NX, NY, NZ, NCORE))))


def swap(array):
    return send(array, lambda x, y, z, core: (x, y, z, 1 - core))


def gather(queries, positives):
    line = code(queries, positives)
    line = jnp.concatenate([line] + [send(line, back(by)) for by in (1, 2, 3)], axis=0)
    line = jnp.concatenate([line, send(line, back(4))], axis=0)
    coded = line[:, D : D + 3 * SLOTS].T
    coded = jnp.concatenate([coded[i * SLOTS : (i + 1) * SLOTS] for i in range(3)], axis=1)
    coded = jnp.pad(coded, ((0, 0), (0, D - 3 * LINE)))
    chip = jnp.concatenate([line[:, :D], coded], axis=0)
    four = [chip] + [send(chip, by_core(along_x(by), along_y(by))) for by in (1, 3, 2)]
    four = pack(four)
    return four


def after(array, *others):
    return lax.optimization_barrier((array, *others))


def shards(queries, positives, weights, first_moment, second_moment):
    weight, first, second = weights, first_moment, second_moment
    over_y = by_core(along_y(1), along_y(3))
    first_x = by_core(along_x(1), along_x(3))
    second_x = by_core(along_x(3), along_x(1))

    wb = weight.astype(bf16)
    wb_other = swap(wb)
    four = gather(queries, positives)
    near = [send(four, by_core(along_y(by), along_x(by))) for by in (1, 3)]
    state = first_residuals(four, wb, wb_other, 0, ())
    far, *state = after(four, *state)
    far = send(far, by_core(along_y(LAST), along_x(LAST)))
    for late, part in zip((1, 3), near):
        state = first_residuals(part, wb, wb_other, late, state)
    q, pos, own, other, most, theirs = first_residuals(far, wb, wb_other, LAST, state)
    step0 = (own, other, wb, wb_other)

    part = swap(theirs)
    mine = gradient(own, q)
    out0 = send(terms(*step0, beside, bf16), over_y)
    part, mine = after(part, mine)
    weight, first, second, wb = update(past_steps + 1, False, mine, part, weight, first, second)

    wb_other = swap(wb)
    wb, *step0 = after(wb, *step0)
    part0 = terms(*step0, here, f32) + out0.astype(f32)
    half0 = send(part0[BLOCK:].astype(bf16), first_x)
    wb_other, part0 = after(wb_other, part0)
    own, other, out1 = plane_terms(most, q, pos, wb, wb_other, beside, bf16)
    half0, out1 = after(half0, out1)

    out1, own, other = after(out1, own, other)
    got = [send(out1[:BLOCK], over_y), send(out1[BLOCK:], then(over_y, first_x))]
    own, other, part1 = plane_terms(most, q, pos, wb, wb_other, here, f32, (own, other))
    got.append(send(part1[BLOCK:].astype(bf16), first_x))

    part1, other = after(part1, other)
    theirs = rest_gradient(most, q, pos, wb_other, other, 1)
    *got, theirs, own = after(*got, theirs, own)
    part = swap(theirs)
    pair0 = part0[:BLOCK] + half0.astype(f32)
    pair1 = part1[:BLOCK] + got[0].astype(f32) + got[1].astype(f32) + got[2].astype(f32)

    lines = jnp.stack([pair.reshape(2, NZ, ROWS, D) for pair in (pair0, pair1)], axis=2)
    far = lines.astype(bf16)
    got = [send(far[1, :4], second_x), send(far[0, 4:], onward(4)), send(far[1, 4:], then(second_x, onward(4)))]
    lines, own = after(lines, own)
    mine = rest_gradient(most, q, pos, wb, own, 0)
    *got, mine = after(*got, mine)
    line = lines[0, :4] + got[0].astype(f32) + got[1].astype(f32) + got[2].astype(f32)

    got = [send(line[by], onward(by)) for by in (1, 2, 3)]
    line, mine = after(line, mine)
    weight, first, second = update(past_steps + 2, True, mine, part, weight, first, second)
    *got, weight, first, second = after(*got, weight, first, second)
    return weight, first, second, line[0] + got[0] + got[1] + got[2]


def solution(mesh):
    devices = mesh.devices.reshape(NX, NLO, NZ, NCORE, NHI)
    label = AXES[:4]
    in_specs = (P(AXES, None), P(AXES, None), P(label, None), P(label, None), P(label, None))
    out_specs = (P(label, None), P(label, None), P(label, None), P(None, AXES, None))
    return jax.shard_map(
        shards, mesh=Mesh(devices, AXES), in_specs=in_specs, out_specs=out_specs, check_vma=False
    )
```

```python
import jax
import jax.numpy as jnp
from jax import lax
from jax.experimental import pallas as pl
from jax.experimental.pallas import tpu as pltpu
from jax.sharding import Mesh, PartitionSpec as P

STEPS = 2

beta_one = 0.9
beta_two = 0.95
rate = 0.02
decay = 0.1
epsilon = 1e-08
past_steps = 1000

f32 = jnp.float32
bf16 = jnp.bfloat16
i32 = jnp.int32

NX, NLO, NZ, NCORE, NHI = 4, 2, 8, 2, 2
NY = NLO * NHI
AXES = ("x", "ylo", "z", "core", "yhi")
D = 512
ROWS = 16
SLOTS = 8
LINE = NZ * ROWS
NQ = NX * NY * LINE
BLOCK = 2 * LINE
LAB = 1024
TILE = 256
VMEM = 16 * 2**20
LOG2E = 1.4426950408889634


def spec(shape=None, index=None, space=pltpu.VMEM):
    if shape is None:
        return pl.BlockSpec(memory_space=space)
    return pl.BlockSpec(shape, index, memory_space=space)


def params():
    return pltpu.CompilerParams(vmem_limit_bytes=VMEM)


def cost(flops=0, size=0, exps=0):
    return pl.CostEstimate(flops=flops, bytes_accessed=size, transcendentals=exps)


def descending(rows):
    rows = list(rows)
    for a, b in (
        (0, 1), (2, 3), (4, 5), (6, 7), (0, 2), (1, 3), (4, 6), (5, 7), (1, 2), (5, 6),
        (0, 4), (1, 5), (2, 6), (3, 7), (2, 4), (3, 5), (1, 2), (3, 4), (5, 6),
    ):
        rows[a], rows[b] = jnp.maximum(rows[a], rows[b]), jnp.minimum(rows[a], rows[b])
    return rows


def here_is():
    high, core = lax.axis_index("yhi"), lax.axis_index("core")
    chip = (lax.axis_index("x") * NLO + lax.axis_index("ylo")) * NZ + lax.axis_index("z")
    base = chip * NCORE * LAB
    return high, core, base + core * LAB, base + (1 - core) * LAB


def gray(slot):
    return slot ^ (slot >> 1)


def place_of(late, early):
    high, core = here_is()[:2]
    y = late + core * (early - late)
    x = early + core * (late - early)
    return (y ^ (2 * high)) * NX + gray((x + (1 - core) * (4 - 2 * x)) & 3)


def span(late, early):
    return pl.ds(pl.multiple_of(place_of(late, early) * LINE, LINE), LINE)


FAST = 2


def contract_last(left, right):
    return lax.dot_general(left, right, (((1,), (1,)), ((), ())), preferred_element_type=f32)


def contract_first(left, right):
    return lax.dot_general(left, right, (((0,), (0,)), ((), ())), preferred_element_type=f32)


def fill_tile(logits, hits, first):
    share = pl.reciprocal(1.0 + jnp.exp2(logits * -LOG2E), approx=True)
    label = lax.broadcasted_iota(i32, logits.shape, 0) + first
    hit = hits[0] == label
    for row in hits[1:]:
        hit = hit | (row == label)
    return jnp.where(hit, share - 1.0, share).astype(bf16)


def more_hits(count, pos_ref, half, out_ref, at):
    @pl.loop(FAST, count)
    def _(j):
        slots = pos_ref[half, :, at]
        slots = jnp.where(lax.broadcasted_iota(i32, slots.shape, 0) == j, slots, -1)
        hit = jnp.max(slots, axis=0, keepdims=True)

        @pl.loop(0, LAB // TILE)
        def _(t):
            rows = pl.ds(pl.multiple_of(t * TILE, TILE), TILE)
            old = out_ref[rows, at].astype(f32)
            label = lax.broadcasted_iota(i32, old.shape, 0) + t * TILE
            out_ref[rows, at] = jnp.where(hit == label, old - 1.0, old).astype(bf16)


def fill_grad(resid_ref, q_ref, out_ref):
    for t in range(LAB // (2 * TILE)):
        rows = slice(2 * TILE * t, 2 * TILE * (t + 1))
        out_ref[rows, :] = jnp.dot(resid_ref[rows, :], q_ref[...], preferred_element_type=f32)


def part_kernel(part_ref, wb_own, wb_other, *refs, late):
    first_labels = here_is()[2:]
    grads = refs[-1:] if late == LAST else ()
    before = refs[4] if late else None
    q_ref, pos_ref, own_ref, other_ref, most_ref = refs[-5 - len(grads) : len(refs) - len(grads)]
    spans = [span(late, gray(early)) for early in range(4)]
    coded = part_ref[NX * LINE :, : 3 * LINE].astype(f32)
    ids = coded[:, :LINE] + 256.0 * coded[:, LINE : 2 * LINE] + 65536.0 * coded[:, 2 * LINE :]
    ids = ids.astype(i32)
    rows = []
    for j in range(SLOTS):
        row = jnp.concatenate([ids[SLOTS * early + j : SLOTS * early + j + 1] for early in range(4)], axis=0)
        local = jnp.concatenate([row - first for first in first_labels], axis=0)
        rows.append(jnp.where((local >= 0) & (local < LAB), local, -1))
    rows = descending(rows)
    count = sum((row >= 0).astype(f32) for row in rows)
    most = jnp.max(count).astype(i32)
    most_ref[...] = count if before is None else jnp.maximum(count, before[...])
    rows = rows[:1] + [jnp.where(row == last, -1, row) for last, row in zip(rows, rows[1:])]
    for half in range(2):
        for early, at in enumerate(spans):
            k = 4 * half + early
            for j in range(SLOTS):
                pos_ref[half, j : j + 1, at] = rows[j][k : k + 1]

    @pl.loop(0, 2)
    def _(pair):
        q = part_ref[pl.ds(pl.multiple_of(pair * BLOCK, BLOCK), BLOCK), :]
        ends = [span(late, 3 * pair), span(late, 1 + pair)]
        for half, wb_ref, out_ref in ((1, wb_other, other_ref), (0, wb_own, own_ref)):
            hits = [[pos_ref[half, j : j + 1, at] for j in range(FAST)] for at in ends]
            for t in range(LAB // TILE):
                tile = slice(t * TILE, (t + 1) * TILE)
                logits = contract_last(wb_ref[tile, :], q)
                for k, at in enumerate(ends):
                    out_ref[tile, at] = fill_tile(logits[:, k * LINE : (k + 1) * LINE], hits[k], t * TILE)

    for early, at in enumerate(spans):
        q_ref[at, :] = part_ref[early * LINE : (early + 1) * LINE, :]

    @pl.when(most > FAST)
    def _():
        @pl.loop(0, 4)
        def _(early):
            for half, out_ref in enumerate((own_ref, other_ref)):
                more_hits(most, pos_ref, half, out_ref, span(late, early))

    for out_ref in grads:
        fill_grad(other_ref, q_ref, out_ref)


LAST = 2


def first_residuals(part, wb, wb_other, late, into):
    shapes = (
        jax.ShapeDtypeStruct((NQ, D), bf16),
        jax.ShapeDtypeStruct((2, SLOTS, NQ), i32),
        jax.ShapeDtypeStruct((LAB, NQ), bf16),
        jax.ShapeDtypeStruct((LAB, NQ), bf16),
        jax.ShapeDtypeStruct((2 * NX, LINE), f32),
    )
    if late == LAST:
        shapes += (jax.ShapeDtypeStruct((LAB, D), f32),)
    size = LAB * NX * LINE
    return pl.pallas_call(
        lambda *refs: part_kernel(*refs, late=late),
        out_shape=shapes,
        in_specs=[spec()] * (3 + len(into)),
        out_specs=(spec(),) * len(shapes),
        input_output_aliases={3 + i: i for i in range(len(into))},
        compiler_params=params(),
        cost_estimate=cost((8 if late == LAST else 4) * size * D, 4 * size, 4 * size),
        name="part",
    )(part, wb, wb_other, *into)


def code_kernel(q_ref, pos_ref, out_ref):
    ids = pos_ref[...]
    out_ref[:, :D] = q_ref[...]
    digits = [ids & 255, (ids >> 8) & 255, ids >> 16]
    lane = lax.broadcasted_iota(i32, (SLOTS, LINE), 1) - lax.broadcasted_iota(i32, (SLOTS, LINE), 0)
    coded = jnp.zeros((ROWS, LINE), f32)
    for i, digit in enumerate(digits):
        put = (lane == i * SLOTS).astype(f32).astype(bf16)
        coded = coded + contract_first(digit.astype(f32).astype(bf16), put)
    out_ref[:, D:] = coded.astype(bf16)


def code(queries, positives):
    return pl.pallas_call(
        code_kernel,
        out_shape=jax.ShapeDtypeStruct((ROWS, D + LINE), bf16),
        in_specs=[spec()] * 2,
        out_specs=spec(),
        compiler_params=params(),
        cost_estimate=cost(size=4 * ROWS * D),
        name="code",
    )(queries, positives.T)


def pack_kernel(*refs):
    out_ref = refs[-1]
    for i, ref in enumerate(refs[:-1]):
        out_ref[i * LINE : (i + 1) * LINE, :] = ref[:LINE, :]
    tails = [ref[LINE:, :] for ref in refs[:-1]]
    out_ref[NX * LINE :, :] = jnp.concatenate(tails, axis=0)


def pack(parts):
    return pl.pallas_call(
        pack_kernel,
        out_shape=jax.ShapeDtypeStruct((NX * (LINE + SLOTS), D), bf16),
        in_specs=[spec()] * 4,
        out_specs=spec(),
        compiler_params=params(),
        cost_estimate=cost(size=4 * NX * LINE * D),
        name="pack",
    )(*parts)


def beside():
    high, core = here_is()[:2]
    plane = (1 + 2 * core) ^ (2 * high)
    return [2 * plane, 2 * plane + 1]


def here():
    first = 4 * lax.axis_index("yhi")
    return [first, first + 1]


def remaining():
    return [block ^ 4 for block in beside() + here()]


def chosen(blocks, i):
    block = blocks[0]
    for k in range(1, len(blocks)):
        block = jnp.where(i == k, blocks[k], block)
    return pl.ds(pl.multiple_of(block * BLOCK, BLOCK), BLOCK)


def fill_block(q_ref, pos_ref, wb_ref, out_ref, half, at):
    q = q_ref[at, :]
    hits = [pos_ref[half, j : j + 1, at] for j in range(FAST)]
    for t in range(LAB // TILE):
        rows = slice(t * TILE, (t + 1) * TILE)
        out_ref[rows, at] = fill_tile(contract_last(wb_ref[rows, :], q), hits, t * TILE)


def finish(most, pos_ref, parts, blocks):
    count = jnp.max(most[...]).astype(i32)

    @pl.when(count > FAST)
    def _():
        @pl.loop(0, len(blocks))
        def _(i):
            for half, out_ref in parts:
                more_hits(count, pos_ref, half, out_ref, chosen(blocks, i))


def fill_terms(own_ref, other_ref, wb_own, wb_other, out_ref, blocks):
    @pl.loop(0, len(blocks))
    def _(i):
        at = chosen(blocks, i)
        first = contract_first(own_ref[:, at], wb_own[...])
        second = contract_first(other_ref[:, at], wb_other[...])
        rows = pl.ds(pl.multiple_of(i * BLOCK, BLOCK), BLOCK)
        out_ref[rows, :] = (first + second).astype(out_ref.dtype)


def plane_kernel(most, q_ref, pos_ref, wb_own, wb_other, *refs, blocks):
    own_ref, other_ref, out_ref = refs[-3:]
    blocks = blocks()

    @pl.loop(0, len(blocks))
    def _(i):
        at = chosen(blocks, i)
        fill_block(q_ref, pos_ref, wb_own, own_ref, 0, at)
        fill_block(q_ref, pos_ref, wb_other, other_ref, 1, at)

    finish(most, pos_ref, ((0, own_ref), (1, other_ref)), blocks)
    fill_terms(own_ref, other_ref, wb_own, wb_other, out_ref, blocks)


def plane_terms(most, q, pos, wb, wb_other, blocks, kind, into=()):
    size = 2 * LAB * 2 * BLOCK
    resid = jax.ShapeDtypeStruct((LAB, NQ), bf16)
    return pl.pallas_call(
        lambda *refs: plane_kernel(*refs, blocks=blocks),
        out_shape=(resid, resid, jax.ShapeDtypeStruct((2 * BLOCK, D), kind)),
        in_specs=[spec()] * (5 + len(into)),
        out_specs=(spec(),) * 3,
        input_output_aliases={5 + i: i for i in range(len(into))},
        compiler_params=params(),
        cost_estimate=cost(4 * size * D, 4 * size, 2 * size),
        name="plane",
    )(most, q, pos, wb, wb_other, *into)


def terms_kernel(own_ref, other_ref, wb_own, wb_other, out_ref, *, blocks):
    fill_terms(own_ref, other_ref, wb_own, wb_other, out_ref, blocks())


def terms(own, other, wb_own, wb_other, blocks, kind):
    return pl.pallas_call(
        lambda *refs: terms_kernel(*refs, blocks=blocks),
        out_shape=jax.ShapeDtypeStruct((2 * BLOCK, D), kind),
        in_specs=[spec()] * 4,
        out_specs=spec(),
        compiler_params=params(),
        cost_estimate=cost(8 * LAB * BLOCK * D, 4 * 2**20),
        name="terms",
    )(own, other, wb_own, wb_other)


def rest_kernel(most, q_ref, pos_ref, wb_ref, old_ref, resid_ref, *out_ref, half):
    blocks = remaining()

    @pl.loop(0, len(blocks) // 2)
    def _(i):
        for k in range(2):
            fill_block(q_ref, pos_ref, wb_ref, resid_ref, half, chosen(blocks, 2 * i + k))

    finish(most, pos_ref, ((half, resid_ref),), blocks)
    for ref in out_ref:
        fill_grad(resid_ref, q_ref, ref)


def rest(most, q, pos, wb, resid, half, grad):
    size = LAB * 4 * BLOCK
    shapes = (jax.ShapeDtypeStruct((LAB, NQ), bf16), jax.ShapeDtypeStruct((LAB, D), f32))[: 1 + grad]
    return pl.pallas_call(
        lambda *refs: rest_kernel(*refs, half=half),
        out_shape=shapes,
        in_specs=[spec()] * 5,
        out_specs=(spec(),) * len(shapes),
        input_output_aliases={4: 0},
        compiler_params=params(),
        cost_estimate=cost((2 + 4 * grad) * size * D, 8 * size, 2 * size),
        name="rest",
    )(most, q, pos, wb, resid)[-1]


def grad_kernel(resid_ref, q_ref, out_ref):
    fill_grad(resid_ref, q_ref, out_ref)


def gradient(resid, q):
    return pl.pallas_call(
        grad_kernel,
        out_shape=jax.ShapeDtypeStruct((LAB, D), f32),
        in_specs=[spec()] * 2,
        out_specs=spec(),
        compiler_params=params(),
        cost_estimate=cost(2 * LAB * NQ * D, 8 * 2**20),
        name="grad",
    )(resid, q)


def adamw(count, grad, weight, first, second):
    first = beta_one * first + (1.0 - beta_one) * grad
    second = beta_two * second + (1.0 - beta_two) * grad * grad
    first_hat = first * (1.0 / (1.0 - beta_one**count))
    second_hat = second * (1.0 / (1.0 - beta_two**count))
    weight = weight - rate * (first_hat / (jnp.sqrt(second_hat) + epsilon) + decay * weight)
    return weight, first, second


def fill_update(count, ins, outs, start, size):
    @pl.loop(0, size // 64)
    def _(t):
        rows = pl.ds(pl.multiple_of(start + t * 64, 64), 64)
        one, two, weight, first, second = (ref[rows, :] for ref in ins)
        new = adamw(count, one + two, weight, first, second)
        for ref, value in zip(outs, new + new[:1]):
            ref[rows, :] = value.astype(ref.dtype)


def adamw_kernel(count, *refs):
    fill_update(count, refs[:5], refs[5:], 0, LAB)


def last_adamw_kernel(count, *refs):
    ins, outs, held, sems = refs[:5], refs[5:8], refs[8:11], refs[11]
    copies = []
    for i in range(LAB // TILE):
        fill_update(count, ins, held, i * TILE, TILE)
        rows = slice(i * TILE, (i + 1) * TILE)
        for k in range(3):
            copies.append(pltpu.make_async_copy(held[k].at[rows], outs[k].at[rows], sems.at[i, k]))
            copies[-1].start()
    for copy in copies:
        copy.wait()


def update(count, last, *arrays):
    full = jax.ShapeDtypeStruct((LAB, D), f32)
    kernel = last_adamw_kernel if last else adamw_kernel
    held = [pltpu.VMEM((LAB, D), f32)] * 3 + [pltpu.SemaphoreType.DMA((LAB // TILE, 3))]
    return pl.pallas_call(
        lambda *refs: kernel(count, *refs),
        out_shape=(full, full, full) + (() if last else (jax.ShapeDtypeStruct((LAB, D), bf16),)),
        in_specs=[spec()] * 5,
        out_specs=(spec(space=pl.ANY),) * 3 if last else (spec(),) * 4,
        scratch_shapes=held if last else [],
        compiler_params=params(),
        cost_estimate=cost(20 * LAB * D, 12 * LAB * D, 2 * LAB * D),
        name="adamw",
    )(*arrays)


def moved(move):
    pairs = []
    for x in range(NX):
        for y in range(NY):
            for z in range(NZ):
                for core in range(NCORE):
                    tx, ty, tz, tcore = move(x, y, z, core)
                    name = lambda x, y, z, core: (
                        (((x % NX) * NLO + y % NLO) * NZ + z % NZ) * NCORE + core
                    ) * NHI + (y % NY) // NLO
                    pairs.append((name(x, y, z, core), name(tx, ty, tz, tcore)))
    return pairs


def send(array, move):
    return lax.ppermute(array, AXES, moved(move))


def along_x(by):
    return lambda x, y, z, core: (x ^ by, y, z, core)


def along_y(by):
    return lambda x, y, z, core: (x, y ^ by, z, core)


def by_core(zero, one):
    return lambda x, y, z, core: one(x, y, z, core) if core else zero(x, y, z, core)


def onward(by):
    def move(x, y, z, core):
        place = 2 * z + core + (by if core else -by)
        return x, y, place // 2, place % 2

    return move


def back(by):
    moves = {onward(by)(0, 0, z, core)[2] % NZ * 2 + onward(by)(0, 0, z, core)[3]: (z, core) for z in range(NZ) for core in range(2)}
    return lambda x, y, z, core: (x, y, *moves[2 * z + core])


def then(one, two):
    return lambda *at: two(*(i % n for i, n in zip(one(*at), (NX, NY, NZ, NCORE))))


def swap(array):
    return send(array, lambda x, y, z, core: (x, y, z, 1 - core))


def gather(queries, positives):
    line = code(queries, positives)
    line = jnp.concatenate([line] + [send(line, back(by)) for by in (1, 2, 3)], axis=0)
    line = jnp.concatenate([line, send(line, back(4))], axis=0)
    coded = line[:, D : D + 3 * SLOTS].T
    coded = jnp.concatenate([coded[i * SLOTS : (i + 1) * SLOTS] for i in range(3)], axis=1)
    coded = jnp.pad(coded, ((0, 0), (0, D - 3 * LINE)))
    chip = jnp.concatenate([line[:, :D], coded], axis=0)
    four = [chip] + [send(chip, by_core(along_x(by), along_y(by))) for by in (1, 3, 2)]
    four = pack(four)
    return four


def after(array, *others):
    return lax.optimization_barrier((array, *others))


def shards(queries, positives, weights, first_moment, second_moment):
    weight, first, second = weights, first_moment, second_moment
    over_y = by_core(along_y(1), along_y(3))
    first_x = by_core(along_x(1), along_x(3))
    second_x = by_core(along_x(3), along_x(1))

    wb = weight.astype(bf16)
    wb_other = swap(wb)
    four = gather(queries, positives)
    near = [send(four, by_core(along_y(by), along_x(by))) for by in (1, 3)]
    state = first_residuals(four, wb, wb_other, 0, ())
    far, *state = after(four, *state)
    far = send(far, by_core(along_y(LAST), along_x(LAST)))
    for late, part in zip((1, 3), near):
        state = first_residuals(part, wb, wb_other, late, state)
    q, pos, own, other, most, theirs = first_residuals(far, wb, wb_other, LAST, state)
    step0 = (own, other, wb, wb_other)

    part = swap(theirs)
    mine = gradient(own, q)
    out0 = terms(*step0, beside, bf16)
    part, mine, out0 = after(part, mine, out0)
    weight, first, second, wb = update(past_steps + 1, False, mine, part, weight, first, second)

    wb_other = swap(wb)
    wb, out0, *step0 = after(wb, out0, *step0)
    out0 = send(out0, over_y)
    part0 = terms(*step0, here, f32)
    wb_other, part0 = after(wb_other, part0)
    own, other, out1 = plane_terms(most, q, pos, wb, wb_other, beside, bf16)

    out1, own, other = after(out1, own, other)
    got = [send(out1[:BLOCK], over_y), send(out1[BLOCK:], then(over_y, first_x))]
    own, other, part1 = plane_terms(most, q, pos, wb, wb_other, here, f32, (own, other))
    out0, part1 = after(out0, part1)
    got.append(send(part1[BLOCK:].astype(bf16), first_x))
    part0 = part0 + out0.astype(f32)
    half0 = send(part0[BLOCK:].astype(bf16), first_x)

    part1, part0, other, own = after(part1, part0, other, own)
    theirs = rest(most, q, pos, wb_other, other, 1, True)
    own = rest(most, q, pos, wb, own, 0, False)
    *got, half0, theirs, own = after(*got, half0, theirs, own)
    part = swap(theirs)
    pair0 = part0[:BLOCK] + half0.astype(f32)
    pair1 = part1[:BLOCK] + got[0].astype(f32) + got[1].astype(f32) + got[2].astype(f32)

    lines = jnp.stack([pair.reshape(2, NZ, ROWS, D) for pair in (pair0, pair1)], axis=2)
    far = lines.astype(bf16)
    got = [send(far[1, :4], second_x), send(far[0, 4:], onward(4)), send(far[1, 4:], then(second_x, onward(4)))]
    lines, own = after(lines, own)
    mine = gradient(own, q)
    *got, mine = after(*got, mine)
    line = lines[0, :4] + got[0].astype(f32) + got[1].astype(f32) + got[2].astype(f32)

    got = [send(line[by], onward(by)) for by in (1, 2, 3)]
    line, mine = after(line, mine)
    weight, first, second = update(past_steps + 2, True, mine, part, weight, first, second)
    *got, weight, first, second = after(*got, weight, first, second)
    return weight, first, second, line[0] + got[0] + got[1] + got[2]


def solution(mesh):
    devices = mesh.devices.reshape(NX, NLO, NZ, NCORE, NHI)
    label = AXES[:4]
    in_specs = (P(AXES, None), P(AXES, None), P(label, None), P(label, None), P(label, None))
    out_specs = (P(label, None), P(label, None), P(label, None), P(None, AXES, None))
    return jax.shard_map(
        shards, mesh=Mesh(devices, AXES), in_specs=in_specs, out_specs=out_specs, check_vma=False
    )
```

```python
import jax
import jax.numpy as jnp
from jax import lax
from jax.experimental import pallas as pl
from jax.experimental.pallas import tpu as pltpu
from jax.sharding import Mesh, PartitionSpec as P

STEPS = 2

beta_one = 0.9
beta_two = 0.95
rate = 0.02
decay = 0.1
epsilon = 1e-08
past_steps = 1000

f32 = jnp.float32
bf16 = jnp.bfloat16
i32 = jnp.int32

NX, NLO, NZ, NCORE, NHI = 4, 2, 8, 2, 2
NY = NLO * NHI
AXES = ("x", "ylo", "z", "core", "yhi")
D = 512
ROWS = 16
SLOTS = 8
LINE = NZ * ROWS
NQ = NX * NY * LINE
BLOCK = 2 * LINE
LAB = 1024
TILE = 256
VMEM = 16 * 2**20
LOG2E = 1.4426950408889634


def spec(shape=None, index=None, space=pltpu.VMEM):
    if shape is None:
        return pl.BlockSpec(memory_space=space)
    return pl.BlockSpec(shape, index, memory_space=space)


def params():
    return pltpu.CompilerParams(vmem_limit_bytes=VMEM)


def cost(flops=0, size=0, exps=0):
    return pl.CostEstimate(flops=flops, bytes_accessed=size, transcendentals=exps)


def descending(rows):
    rows = list(rows)
    for a, b in (
        (0, 1), (2, 3), (4, 5), (6, 7), (0, 2), (1, 3), (4, 6), (5, 7), (1, 2), (5, 6),
        (0, 4), (1, 5), (2, 6), (3, 7), (2, 4), (3, 5), (1, 2), (3, 4), (5, 6),
    ):
        rows[a], rows[b] = jnp.maximum(rows[a], rows[b]), jnp.minimum(rows[a], rows[b])
    return rows


def here_is():
    high, core = lax.axis_index("yhi"), lax.axis_index("core")
    chip = (lax.axis_index("x") * NLO + lax.axis_index("ylo")) * NZ + lax.axis_index("z")
    base = chip * NCORE * LAB
    return high, core, base + core * LAB, base + (1 - core) * LAB


def gray(slot):
    return slot ^ (slot >> 1)


def place_of(late, early):
    high, core = here_is()[:2]
    y = late + core * (early - late)
    x = early + core * (late - early)
    return (y ^ (2 * high)) * NX + gray((x + (1 - core) * (4 - 2 * x)) & 3)


def span(late, early):
    return pl.ds(pl.multiple_of(place_of(late, early) * LINE, LINE), LINE)


FAST = 2


def contract_last(left, right):
    return lax.dot_general(left, right, (((1,), (1,)), ((), ())), preferred_element_type=f32)


def contract_first(left, right):
    return lax.dot_general(left, right, (((0,), (0,)), ((), ())), preferred_element_type=f32)


def fill_tile(logits, hits, first):
    share = pl.reciprocal(1.0 + jnp.exp2(logits * -LOG2E), approx=True)
    label = lax.broadcasted_iota(i32, logits.shape, 0) + first
    hit = hits[0] == label
    for row in hits[1:]:
        hit = hit | (row == label)
    return jnp.where(hit, share - 1.0, share).astype(bf16)


def more_hits(count, pos_ref, half, out_ref, at):
    @pl.loop(FAST, count)
    def _(j):
        slots = pos_ref[half, :, at]
        slots = jnp.where(lax.broadcasted_iota(i32, slots.shape, 0) == j, slots, -1)
        hit = jnp.max(slots, axis=0, keepdims=True)

        @pl.loop(0, LAB // TILE)
        def _(t):
            rows = pl.ds(pl.multiple_of(t * TILE, TILE), TILE)
            old = out_ref[rows, at].astype(f32)
            label = lax.broadcasted_iota(i32, old.shape, 0) + t * TILE
            out_ref[rows, at] = jnp.where(hit == label, old - 1.0, old).astype(bf16)


def fill_grad(resid_ref, q_ref, out_ref):
    for t in range(LAB // (2 * TILE)):
        rows = slice(2 * TILE * t, 2 * TILE * (t + 1))
        out_ref[rows, :] = jnp.dot(resid_ref[rows, :], q_ref[...], preferred_element_type=f32)


def part_kernel(part_ref, wb_own, wb_other, *refs, late):
    first_labels = here_is()[2:]
    grads = refs[-1:] if late == LAST else ()
    before = refs[4] if late else None
    q_ref, pos_ref, own_ref, other_ref, most_ref = refs[-5 - len(grads) : len(refs) - len(grads)]
    spans = [span(late, gray(early)) for early in range(4)]
    coded = part_ref[NX * LINE :, : 3 * LINE].astype(f32)
    ids = coded[:, :LINE] + 256.0 * coded[:, LINE : 2 * LINE] + 65536.0 * coded[:, 2 * LINE :]
    ids = ids.astype(i32)
    rows = []
    for j in range(SLOTS):
        row = jnp.concatenate([ids[SLOTS * early + j : SLOTS * early + j + 1] for early in range(4)], axis=0)
        local = jnp.concatenate([row - first for first in first_labels], axis=0)
        rows.append(jnp.where((local >= 0) & (local < LAB), local, -1))
    rows = descending(rows)
    count = sum((row >= 0).astype(f32) for row in rows)
    most = jnp.max(count).astype(i32)
    most_ref[...] = count if before is None else jnp.maximum(count, before[...])
    rows = rows[:1] + [jnp.where(row == last, -1, row) for last, row in zip(rows, rows[1:])]
    for half in range(2):
        for early, at in enumerate(spans):
            k = 4 * half + early
            for j in range(SLOTS):
                pos_ref[half, j : j + 1, at] = rows[j][k : k + 1]

    @pl.loop(0, 2)
    def _(pair):
        q = part_ref[pl.ds(pl.multiple_of(pair * BLOCK, BLOCK), BLOCK), :]
        ends = [span(late, 3 * pair), span(late, 1 + pair)]
        for half, wb_ref, out_ref in ((1, wb_other, other_ref), (0, wb_own, own_ref)):
            hits = [[pos_ref[half, j : j + 1, at] for j in range(FAST)] for at in ends]
            for t in range(LAB // TILE):
                tile = slice(t * TILE, (t + 1) * TILE)
                logits = contract_last(wb_ref[tile, :], q)
                for k, at in enumerate(ends):
                    out_ref[tile, at] = fill_tile(logits[:, k * LINE : (k + 1) * LINE], hits[k], t * TILE)

    for early, at in enumerate(spans):
        q_ref[at, :] = part_ref[early * LINE : (early + 1) * LINE, :]

    @pl.when(most > FAST)
    def _():
        @pl.loop(0, 4)
        def _(early):
            for half, out_ref in enumerate((own_ref, other_ref)):
                more_hits(most, pos_ref, half, out_ref, span(late, early))

    for out_ref in grads:
        fill_grad(other_ref, q_ref, out_ref)


LAST = 2


def first_residuals(part, wb, wb_other, late, into):
    shapes = (
        jax.ShapeDtypeStruct((NQ, D), bf16),
        jax.ShapeDtypeStruct((2, SLOTS, NQ), i32),
        jax.ShapeDtypeStruct((LAB, NQ), bf16),
        jax.ShapeDtypeStruct((LAB, NQ), bf16),
        jax.ShapeDtypeStruct((2 * NX, LINE), f32),
    )
    if late == LAST:
        shapes += (jax.ShapeDtypeStruct((LAB, D), f32),)
    size = LAB * NX * LINE
    return pl.pallas_call(
        lambda *refs: part_kernel(*refs, late=late),
        out_shape=shapes,
        in_specs=[spec()] * (3 + len(into)),
        out_specs=(spec(),) * len(shapes),
        input_output_aliases={3 + i: i for i in range(len(into))},
        compiler_params=params(),
        cost_estimate=cost((8 if late == LAST else 4) * size * D, 4 * size, 4 * size),
        name="part",
    )(part, wb, wb_other, *into)


def code_kernel(q_ref, pos_ref, out_ref):
    ids = pos_ref[...]
    out_ref[:, :D] = q_ref[...]
    digits = [ids & 255, (ids >> 8) & 255, ids >> 16]
    lane = lax.broadcasted_iota(i32, (SLOTS, LINE), 1) - lax.broadcasted_iota(i32, (SLOTS, LINE), 0)
    coded = jnp.zeros((ROWS, LINE), f32)
    for i, digit in enumerate(digits):
        put = (lane == i * SLOTS).astype(f32).astype(bf16)
        coded = coded + contract_first(digit.astype(f32).astype(bf16), put)
    out_ref[:, D:] = coded.astype(bf16)


def code(queries, positives):
    return pl.pallas_call(
        code_kernel,
        out_shape=jax.ShapeDtypeStruct((ROWS, D + LINE), bf16),
        in_specs=[spec()] * 2,
        out_specs=spec(),
        compiler_params=params(),
        cost_estimate=cost(size=4 * ROWS * D),
        name="code",
    )(queries, positives.T)


def pack_kernel(*refs):
    out_ref = refs[-1]
    for i, ref in enumerate(refs[:-1]):
        out_ref[i * LINE : (i + 1) * LINE, :] = ref[:LINE, :]
    tails = [ref[LINE:, :] for ref in refs[:-1]]
    out_ref[NX * LINE :, :] = jnp.concatenate(tails, axis=0)


def pack(parts):
    return pl.pallas_call(
        pack_kernel,
        out_shape=jax.ShapeDtypeStruct((NX * (LINE + SLOTS), D), bf16),
        in_specs=[spec()] * 4,
        out_specs=spec(),
        compiler_params=params(),
        cost_estimate=cost(size=4 * NX * LINE * D),
        name="pack",
    )(*parts)


def beside():
    high, core = here_is()[:2]
    plane = (1 + 2 * core) ^ (2 * high)
    return [2 * plane, 2 * plane + 1]


def here():
    first = 4 * lax.axis_index("yhi")
    return [first, first + 1]


def remaining():
    return [block ^ 4 for block in beside() + here()]


def chosen(blocks, i):
    block = blocks[0]
    for k in range(1, len(blocks)):
        block = jnp.where(i == k, blocks[k], block)
    return pl.ds(pl.multiple_of(block * BLOCK, BLOCK), BLOCK)


def fill_block(q_ref, pos_ref, wb_ref, out_ref, half, at):
    q = q_ref[at, :]
    hits = [pos_ref[half, j : j + 1, at] for j in range(FAST)]
    for t in range(LAB // TILE):
        rows = slice(t * TILE, (t + 1) * TILE)
        out_ref[rows, at] = fill_tile(contract_last(wb_ref[rows, :], q), hits, t * TILE)


def finish(most, pos_ref, parts, blocks):
    count = jnp.max(most[...]).astype(i32)

    @pl.when(count > FAST)
    def _():
        @pl.loop(0, len(blocks))
        def _(i):
            for half, out_ref in parts:
                more_hits(count, pos_ref, half, out_ref, chosen(blocks, i))


def fill_terms(own_ref, other_ref, wb_own, wb_other, out_ref, blocks):
    @pl.loop(0, len(blocks))
    def _(i):
        at = chosen(blocks, i)
        first = contract_first(own_ref[:, at], wb_own[...])
        second = contract_first(other_ref[:, at], wb_other[...])
        rows = pl.ds(pl.multiple_of(i * BLOCK, BLOCK), BLOCK)
        out_ref[rows, :] = (first + second).astype(out_ref.dtype)


def plane_kernel(most, q_ref, pos_ref, wb_own, wb_other, *refs, blocks):
    own_ref, other_ref, out_ref = refs[-3:]
    blocks = blocks()

    @pl.loop(0, len(blocks))
    def _(i):
        at = chosen(blocks, i)
        fill_block(q_ref, pos_ref, wb_own, own_ref, 0, at)
        fill_block(q_ref, pos_ref, wb_other, other_ref, 1, at)

    finish(most, pos_ref, ((0, own_ref), (1, other_ref)), blocks)
    fill_terms(own_ref, other_ref, wb_own, wb_other, out_ref, blocks)


def plane_terms(most, q, pos, wb, wb_other, blocks, kind, into=()):
    size = 2 * LAB * 2 * BLOCK
    resid = jax.ShapeDtypeStruct((LAB, NQ), bf16)
    return pl.pallas_call(
        lambda *refs: plane_kernel(*refs, blocks=blocks),
        out_shape=(resid, resid, jax.ShapeDtypeStruct((2 * BLOCK, D), kind)),
        in_specs=[spec()] * (5 + len(into)),
        out_specs=(spec(),) * 3,
        input_output_aliases={5 + i: i for i in range(len(into))},
        compiler_params=params(),
        cost_estimate=cost(4 * size * D, 4 * size, 2 * size),
        name="plane",
    )(most, q, pos, wb, wb_other, *into)


def terms_kernel(own_ref, other_ref, wb_own, wb_other, out_ref, *, blocks):
    fill_terms(own_ref, other_ref, wb_own, wb_other, out_ref, blocks())


def terms(own, other, wb_own, wb_other, blocks, kind):
    return pl.pallas_call(
        lambda *refs: terms_kernel(*refs, blocks=blocks),
        out_shape=jax.ShapeDtypeStruct((2 * BLOCK, D), kind),
        in_specs=[spec()] * 4,
        out_specs=spec(),
        compiler_params=params(),
        cost_estimate=cost(8 * LAB * BLOCK * D, 4 * 2**20),
        name="terms",
    )(own, other, wb_own, wb_other)


def rest_kernel(most, q_ref, pos_ref, wb_ref, resid_ref, out_ref, *, half):
    blocks = remaining()

    @pl.loop(0, len(blocks) // 2)
    def _(i):
        for k in range(2):
            fill_block(q_ref, pos_ref, wb_ref, resid_ref, half, chosen(blocks, 2 * i + k))

    finish(most, pos_ref, ((half, resid_ref),), blocks)
    fill_grad(resid_ref, q_ref, out_ref)


def rest_gradient(most, q, pos, wb, resid, half):
    size = LAB * 4 * BLOCK
    return pl.pallas_call(
        lambda most, q, pos, wb, old, resid, out: rest_kernel(most, q, pos, wb, resid, out, half=half),
        out_shape=(jax.ShapeDtypeStruct((LAB, NQ), bf16), jax.ShapeDtypeStruct((LAB, D), f32)),
        in_specs=[spec()] * 5,
        out_specs=(spec(),) * 2,
        input_output_aliases={4: 0},
        compiler_params=params(),
        cost_estimate=cost(6 * size * D, 8 * size, 2 * size),
        name="rest",
    )(most, q, pos, wb, resid)[1]


def grad_kernel(resid_ref, q_ref, out_ref):
    fill_grad(resid_ref, q_ref, out_ref)


def gradient(resid, q):
    return pl.pallas_call(
        grad_kernel,
        out_shape=jax.ShapeDtypeStruct((LAB, D), f32),
        in_specs=[spec()] * 2,
        out_specs=spec(),
        compiler_params=params(),
        cost_estimate=cost(2 * LAB * NQ * D, 8 * 2**20),
        name="grad",
    )(resid, q)


def adamw(count, grad, weight, first, second):
    first = beta_one * first + (1.0 - beta_one) * grad
    second = beta_two * second + (1.0 - beta_two) * grad * grad
    first_hat = first * (1.0 / (1.0 - beta_one**count))
    second_hat = second * (1.0 / (1.0 - beta_two**count))
    weight = weight - rate * (first_hat / (jnp.sqrt(second_hat) + epsilon) + decay * weight)
    return weight, first, second


def fill_update(count, ins, outs, start, size):
    @pl.loop(0, size // 64)
    def _(t):
        rows = pl.ds(pl.multiple_of(start + t * 64, 64), 64)
        one, two, weight, first, second = (ref[rows, :] for ref in ins)
        new = adamw(count, one + two, weight, first, second)
        for ref, value in zip(outs, new + new[:1]):
            ref[rows, :] = value.astype(ref.dtype)


def adamw_kernel(count, *refs):
    fill_update(count, refs[:5], refs[5:], 0, LAB)


def last_adamw_kernel(count, *refs):
    ins, outs, held, sems = refs[:5], refs[5:8], refs[8:11], refs[11]
    copies = []
    for i in range(LAB // TILE):
        fill_update(count, ins, held, i * TILE, TILE)
        rows = slice(i * TILE, (i + 1) * TILE)
        for k in range(3):
            copies.append(pltpu.make_async_copy(held[k].at[rows], outs[k].at[rows], sems.at[i, k]))
            copies[-1].start()
    for copy in copies:
        copy.wait()


def update(count, last, *arrays):
    full = jax.ShapeDtypeStruct((LAB, D), f32)
    kernel = last_adamw_kernel if last else adamw_kernel
    held = [pltpu.VMEM((LAB, D), f32)] * 3 + [pltpu.SemaphoreType.DMA((LAB // TILE, 3))]
    return pl.pallas_call(
        lambda *refs: kernel(count, *refs),
        out_shape=(full, full, full) + (() if last else (jax.ShapeDtypeStruct((LAB, D), bf16),)),
        in_specs=[spec()] * 5,
        out_specs=(spec(space=pl.ANY),) * 3 if last else (spec(),) * 4,
        scratch_shapes=held if last else [],
        compiler_params=params(),
        cost_estimate=cost(20 * LAB * D, 12 * LAB * D, 2 * LAB * D),
        name="adamw",
    )(*arrays)


def moved(move):
    pairs = []
    for x in range(NX):
        for y in range(NY):
            for z in range(NZ):
                for core in range(NCORE):
                    tx, ty, tz, tcore = move(x, y, z, core)
                    name = lambda x, y, z, core: (
                        (((x % NX) * NLO + y % NLO) * NZ + z % NZ) * NCORE + core
                    ) * NHI + (y % NY) // NLO
                    pairs.append((name(x, y, z, core), name(tx, ty, tz, tcore)))
    return pairs


def send(array, move):
    return lax.ppermute(array, AXES, moved(move))


def along_x(by):
    return lambda x, y, z, core: (x ^ by, y, z, core)


def along_y(by):
    return lambda x, y, z, core: (x, y ^ by, z, core)


def by_core(zero, one):
    return lambda x, y, z, core: one(x, y, z, core) if core else zero(x, y, z, core)


def onward(by):
    def move(x, y, z, core):
        place = 2 * z + core + (by if core else -by)
        return x, y, place // 2, place % 2

    return move


def back(by):
    moves = {onward(by)(0, 0, z, core)[2] % NZ * 2 + onward(by)(0, 0, z, core)[3]: (z, core) for z in range(NZ) for core in range(2)}
    return lambda x, y, z, core: (x, y, *moves[2 * z + core])


def then(one, two):
    return lambda *at: two(*(i % n for i, n in zip(one(*at), (NX, NY, NZ, NCORE))))


def swap(array):
    return send(array, lambda x, y, z, core: (x, y, z, 1 - core))


def gather(queries, positives):
    line = code(queries, positives)
    line = jnp.concatenate([line] + [send(line, back(by)) for by in range(1, NZ)], axis=0)
    coded = line[:, D : D + 3 * SLOTS].T
    coded = jnp.concatenate([coded[i * SLOTS : (i + 1) * SLOTS] for i in range(3)], axis=1)
    coded = jnp.pad(coded, ((0, 0), (0, D - 3 * LINE)))
    chip = jnp.concatenate([line[:, :D], coded], axis=0)
    four = [chip] + [send(chip, by_core(along_x(by), along_y(by))) for by in (1, 3, 2)]
    four = pack(four)
    return four


def after(array, *others):
    return lax.optimization_barrier((array, *others))


def shards(queries, positives, weights, first_moment, second_moment):
    weight, first, second = weights, first_moment, second_moment
    over_y = by_core(along_y(1), along_y(3))
    first_x = by_core(along_x(1), along_x(3))
    second_x = by_core(along_x(3), along_x(1))

    wb = weight.astype(bf16)
    wb_other = swap(wb)
    four = gather(queries, positives)
    near = [send(four, by_core(along_y(by), along_x(by))) for by in (1, 3)]
    state = first_residuals(four, wb, wb_other, 0, ())
    far, *state = after(four, *state)
    far = send(far, by_core(along_y(LAST), along_x(LAST)))
    for late, part in zip((1, 3), near):
        state = first_residuals(part, wb, wb_other, late, state)
    q, pos, own, other, most, theirs = first_residuals(far, wb, wb_other, LAST, state)
    step0 = (own, other, wb, wb_other)

    part = swap(theirs)
    mine = gradient(own, q)
    out0 = terms(*step0, beside, bf16)
    part, mine, out0 = after(part, mine, out0)
    weight, first, second, wb = update(past_steps + 1, False, mine, part, weight, first, second)

    wb_other = swap(wb)
    wb, out0, *step0 = after(wb, out0, *step0)
    out0 = send(out0, over_y)
    part0 = terms(*step0, here, f32)
    wb_other, part0 = after(wb_other, part0)
    own, other, out1 = plane_terms(most, q, pos, wb, wb_other, beside, bf16)

    out1, own, other = after(out1, own, other)
    got = [send(out1[:BLOCK], over_y), send(out1[BLOCK:], then(over_y, first_x))]
    own, other, part1 = plane_terms(most, q, pos, wb, wb_other, here, f32, (own, other))
    out0, part1 = after(out0, part1)
    got.append(send(part1[BLOCK:].astype(bf16), first_x))
    part0 = part0 + out0.astype(f32)
    half0 = send(part0[BLOCK:].astype(bf16), first_x)

    part1, part0, other = after(part1, part0, other)
    theirs = rest_gradient(most, q, pos, wb_other, other, 1)
    *got, half0, theirs, own = after(*got, half0, theirs, own)
    part = swap(theirs)
    pair0 = part0[:BLOCK] + half0.astype(f32)
    pair1 = part1[:BLOCK] + got[0].astype(f32) + got[1].astype(f32) + got[2].astype(f32)

    lines = jnp.stack([pair.reshape(2, NZ, ROWS, D) for pair in (pair0, pair1)], axis=2)
    far = lines.astype(bf16)
    got = [send(far[1, :4], second_x), send(far[0, 4:], onward(4)), send(far[1, 4:], then(second_x, onward(4)))]
    lines, own = after(lines, own)
    mine = rest_gradient(most, q, pos, wb, own, 0)
    *got, mine = after(*got, mine)
    line = lines[0, :4] + got[0].astype(f32) + got[1].astype(f32) + got[2].astype(f32)

    got = [send(line[by], onward(by)) for by in (1, 2, 3)]
    line, mine = after(line, mine)
    weight, first, second = update(past_steps + 2, True, mine, part, weight, first, second)
    *got, weight, first, second = after(*got, weight, first, second)
    return weight, first, second, line[0] + got[0] + got[1] + got[2]


def solution(mesh):
    devices = mesh.devices.reshape(NX, NLO, NZ, NCORE, NHI)
    label = AXES[:4]
    in_specs = (P(AXES, None), P(AXES, None), P(label, None), P(label, None), P(label, None))
    out_specs = (P(label, None), P(label, None), P(label, None), P(None, AXES, None))
    return jax.shard_map(
        shards, mesh=Mesh(devices, AXES), in_specs=in_specs, out_specs=out_specs, check_vma=False
    )
```

```python
import jax
import jax.numpy as jnp
from jax import lax
from jax.experimental import pallas as pl
from jax.experimental.pallas import tpu as pltpu
from jax.sharding import Mesh, PartitionSpec as P

STEPS = 2

beta_one = 0.9
beta_two = 0.95
rate = 0.02
decay = 0.1
epsilon = 1e-08
past_steps = 1000

f32 = jnp.float32
bf16 = jnp.bfloat16
i32 = jnp.int32

NX, NLO, NZ, NCORE, NHI = 4, 2, 8, 2, 2
NY = NLO * NHI
AXES = ("x", "ylo", "z", "core", "yhi")
D = 512
ROWS = 16
SLOTS = 8
LINE = NZ * ROWS
NQ = NX * NY * LINE
BLOCK = 2 * LINE
LAB = 1024
TILE = 256
VMEM = 16 * 2**20
LOG2E = 1.4426950408889634


def spec(shape=None, index=None, space=pltpu.VMEM):
    if shape is None:
        return pl.BlockSpec(memory_space=space)
    return pl.BlockSpec(shape, index, memory_space=space)


def params():
    return pltpu.CompilerParams(vmem_limit_bytes=VMEM)


def cost(flops=0, size=0, exps=0):
    return pl.CostEstimate(flops=flops, bytes_accessed=size, transcendentals=exps)


def descending(rows):
    rows = list(rows)
    for a, b in (
        (0, 1), (2, 3), (4, 5), (6, 7), (0, 2), (1, 3), (4, 6), (5, 7), (1, 2), (5, 6),
        (0, 4), (1, 5), (2, 6), (3, 7), (2, 4), (3, 5), (1, 2), (3, 4), (5, 6),
    ):
        rows[a], rows[b] = jnp.maximum(rows[a], rows[b]), jnp.minimum(rows[a], rows[b])
    return rows


def here_is():
    high, core = lax.axis_index("yhi"), lax.axis_index("core")
    chip = (lax.axis_index("x") * NLO + lax.axis_index("ylo")) * NZ + lax.axis_index("z")
    base = chip * NCORE * LAB
    return high, core, base + core * LAB, base + (1 - core) * LAB


def gray(slot):
    return slot ^ (slot >> 1)


def place_of(late, early):
    high, core = here_is()[:2]
    y = late + core * (early - late)
    x = early + core * (late - early)
    return (y ^ (2 * high)) * NX + gray((x + (1 - core) * (4 - 2 * x)) & 3)


def span(late, early):
    return pl.ds(pl.multiple_of(place_of(late, early) * LINE, LINE), LINE)


FAST = 2


def contract_last(left, right):
    return lax.dot_general(left, right, (((1,), (1,)), ((), ())), preferred_element_type=f32)


def contract_first(left, right):
    return lax.dot_general(left, right, (((0,), (0,)), ((), ())), preferred_element_type=f32)


def fill_tile(logits, hits, first):
    share = pl.reciprocal(1.0 + jnp.exp2(logits * -LOG2E), approx=True)
    label = lax.broadcasted_iota(i32, logits.shape, 0) + first
    hit = hits[0] == label
    for row in hits[1:]:
        hit = hit | (row == label)
    return jnp.where(hit, share - 1.0, share).astype(bf16)


def more_hits(count, pos_ref, half, out_ref, at):
    @pl.loop(FAST, count)
    def _(j):
        slots = pos_ref[half, :, at]
        slots = jnp.where(lax.broadcasted_iota(i32, slots.shape, 0) == j, slots, -1)
        hit = jnp.max(slots, axis=0, keepdims=True)

        @pl.loop(0, LAB // TILE)
        def _(t):
            rows = pl.ds(pl.multiple_of(t * TILE, TILE), TILE)
            old = out_ref[rows, at].astype(f32)
            label = lax.broadcasted_iota(i32, old.shape, 0) + t * TILE
            out_ref[rows, at] = jnp.where(hit == label, old - 1.0, old).astype(bf16)


def fill_grad(resid_ref, q_ref, out_ref):
    for t in range(LAB // (2 * TILE)):
        rows = slice(2 * TILE * t, 2 * TILE * (t + 1))
        out_ref[rows, :] = jnp.dot(resid_ref[rows, :], q_ref[...], preferred_element_type=f32)


def part_kernel(part_ref, wb_own, wb_other, *refs, late):
    first_labels = here_is()[2:]
    grads = refs[-1:] if late == LAST else ()
    before = refs[4] if late else None
    q_ref, pos_ref, own_ref, other_ref, most_ref = refs[-5 - len(grads) : len(refs) - len(grads)]
    spans = [span(late, gray(early)) for early in range(4)]
    coded = part_ref[NX * LINE :, : 3 * LINE].astype(f32)
    ids = coded[:, :LINE] + 256.0 * coded[:, LINE : 2 * LINE] + 65536.0 * coded[:, 2 * LINE :]
    ids = ids.astype(i32)
    rows = []
    for j in range(SLOTS):
        row = jnp.concatenate([ids[SLOTS * early + j : SLOTS * early + j + 1] for early in range(4)], axis=0)
        local = jnp.concatenate([row - first for first in first_labels], axis=0)
        rows.append(jnp.where((local >= 0) & (local < LAB), local, -1))
    rows = descending(rows)
    count = sum((row >= 0).astype(f32) for row in rows)
    most = jnp.max(count).astype(i32)
    most_ref[...] = count if before is None else jnp.maximum(count, before[...])
    rows = rows[:1] + [jnp.where(row == last, -1, row) for last, row in zip(rows, rows[1:])]
    for half in range(2):
        for early, at in enumerate(spans):
            k = 4 * half + early
            for j in range(SLOTS):
                pos_ref[half, j : j + 1, at] = rows[j][k : k + 1]

    @pl.loop(0, 2)
    def _(pair):
        q = part_ref[pl.ds(pl.multiple_of(pair * BLOCK, BLOCK), BLOCK), :]
        ends = [span(late, 3 * pair), span(late, 1 + pair)]
        for half, wb_ref, out_ref in ((1, wb_other, other_ref), (0, wb_own, own_ref)):
            hits = [[pos_ref[half, j : j + 1, at] for j in range(FAST)] for at in ends]
            for t in range(LAB // TILE):
                tile = slice(t * TILE, (t + 1) * TILE)
                logits = contract_last(wb_ref[tile, :], q)
                for k, at in enumerate(ends):
                    out_ref[tile, at] = fill_tile(logits[:, k * LINE : (k + 1) * LINE], hits[k], t * TILE)

    for early, at in enumerate(spans):
        q_ref[at, :] = part_ref[early * LINE : (early + 1) * LINE, :]

    @pl.when(most > FAST)
    def _():
        @pl.loop(0, 4)
        def _(early):
            for half, out_ref in enumerate((own_ref, other_ref)):
                more_hits(most, pos_ref, half, out_ref, span(late, early))

    for out_ref in grads:
        fill_grad(other_ref, q_ref, out_ref)


LAST = 2


def first_residuals(part, wb, wb_other, late, into):
    shapes = (
        jax.ShapeDtypeStruct((NQ, D), bf16),
        jax.ShapeDtypeStruct((2, SLOTS, NQ), i32),
        jax.ShapeDtypeStruct((LAB, NQ), bf16),
        jax.ShapeDtypeStruct((LAB, NQ), bf16),
        jax.ShapeDtypeStruct((2 * NX, LINE), f32),
    )
    if late == LAST:
        shapes += (jax.ShapeDtypeStruct((LAB, D), f32),)
    size = LAB * NX * LINE
    return pl.pallas_call(
        lambda *refs: part_kernel(*refs, late=late),
        out_shape=shapes,
        in_specs=[spec()] * (3 + len(into)),
        out_specs=(spec(),) * len(shapes),
        input_output_aliases={3 + i: i for i in range(len(into))},
        compiler_params=params(),
        cost_estimate=cost((8 if late == LAST else 4) * size * D, 4 * size, 4 * size),
        name="part",
    )(part, wb, wb_other, *into)


def code_kernel(q_ref, pos_ref, out_ref):
    ids = pos_ref[...]
    out_ref[:, :D] = q_ref[...]
    digits = [ids & 255, (ids >> 8) & 255, ids >> 16]
    lane = lax.broadcasted_iota(i32, (SLOTS, LINE), 1) - lax.broadcasted_iota(i32, (SLOTS, LINE), 0)
    coded = jnp.zeros((ROWS, LINE), f32)
    for i, digit in enumerate(digits):
        put = (lane == i * SLOTS).astype(f32).astype(bf16)
        coded = coded + contract_first(digit.astype(f32).astype(bf16), put)
    out_ref[:, D:] = coded.astype(bf16)


def code(queries, positives):
    return pl.pallas_call(
        code_kernel,
        out_shape=jax.ShapeDtypeStruct((ROWS, D + LINE), bf16),
        in_specs=[spec()] * 2,
        out_specs=spec(),
        compiler_params=params(),
        cost_estimate=cost(size=4 * ROWS * D),
        name="code",
    )(queries, positives.T)


def pack_kernel(*refs):
    out_ref = refs[-1]
    for i, ref in enumerate(refs[:-1]):
        out_ref[i * LINE : (i + 1) * LINE, :] = ref[:LINE, :]
    tails = [ref[LINE:, :] for ref in refs[:-1]]
    out_ref[NX * LINE :, :] = jnp.concatenate(tails, axis=0)


def pack(parts):
    return pl.pallas_call(
        pack_kernel,
        out_shape=jax.ShapeDtypeStruct((NX * (LINE + SLOTS), D), bf16),
        in_specs=[spec()] * 4,
        out_specs=spec(),
        compiler_params=params(),
        cost_estimate=cost(size=4 * NX * LINE * D),
        name="pack",
    )(*parts)


def beside():
    high, core = here_is()[:2]
    plane = (1 + 2 * core) ^ (2 * high)
    return [2 * plane, 2 * plane + 1]


def here():
    first = 4 * lax.axis_index("yhi")
    return [first, first + 1]


def remaining():
    return [block ^ 4 for block in beside() + here()]


def chosen(blocks, i):
    block = blocks[0]
    for k in range(1, len(blocks)):
        block = jnp.where(i == k, blocks[k], block)
    return pl.ds(pl.multiple_of(block * BLOCK, BLOCK), BLOCK)


def fill_block(q_ref, pos_ref, wb_ref, out_ref, half, at):
    q = q_ref[at, :]
    hits = [pos_ref[half, j : j + 1, at] for j in range(FAST)]
    for t in range(LAB // TILE):
        rows = slice(t * TILE, (t + 1) * TILE)
        out_ref[rows, at] = fill_tile(contract_last(wb_ref[rows, :], q), hits, t * TILE)


def finish(most, pos_ref, parts, blocks):
    count = jnp.max(most[...]).astype(i32)

    @pl.when(count > FAST)
    def _():
        @pl.loop(0, len(blocks))
        def _(i):
            for half, out_ref in parts:
                more_hits(count, pos_ref, half, out_ref, chosen(blocks, i))


def fill_terms(own_ref, other_ref, wb_own, wb_other, out_ref, blocks):
    @pl.loop(0, len(blocks))
    def _(i):
        at = chosen(blocks, i)
        first = contract_first(own_ref[:, at], wb_own[...])
        second = contract_first(other_ref[:, at], wb_other[...])
        rows = pl.ds(pl.multiple_of(i * BLOCK, BLOCK), BLOCK)
        out_ref[rows, :] = (first + second).astype(out_ref.dtype)


def plane_kernel(most, q_ref, pos_ref, wb_own, wb_other, *refs, blocks):
    own_ref, other_ref, out_ref = refs[-3:]
    blocks = blocks()

    @pl.loop(0, len(blocks))
    def _(i):
        at = chosen(blocks, i)
        fill_block(q_ref, pos_ref, wb_own, own_ref, 0, at)
        fill_block(q_ref, pos_ref, wb_other, other_ref, 1, at)

    finish(most, pos_ref, ((0, own_ref), (1, other_ref)), blocks)
    fill_terms(own_ref, other_ref, wb_own, wb_other, out_ref, blocks)


def own_kernel(most, q_ref, pos_ref, wb_ref, own_ref):
    blocks = beside()
    for i in range(2):
        fill_block(q_ref, pos_ref, wb_ref, own_ref, 0, chosen(blocks, i))
    finish(most, pos_ref, ((0, own_ref),), blocks)


def own_beside(most, q, pos, wb):
    size = LAB * 2 * BLOCK
    return pl.pallas_call(
        own_kernel,
        out_shape=jax.ShapeDtypeStruct((LAB, NQ), bf16),
        in_specs=[spec()] * 4,
        out_specs=spec(),
        compiler_params=params(),
        cost_estimate=cost(2 * size * D, 4 * size, 2 * size),
        name="own",
    )(most, q, pos, wb)


def beside_kernel(most, q_ref, pos_ref, wb_own, wb_other, own_ref, other_ref, out_ref):
    blocks = beside()
    for i in range(2):
        fill_block(q_ref, pos_ref, wb_other, other_ref, 1, chosen(blocks, i))
    finish(most, pos_ref, ((1, other_ref),), blocks)
    fill_terms(own_ref, other_ref, wb_own, wb_other, out_ref, blocks)


def beside_terms(most, q, pos, wb, wb_other, own):
    size = LAB * 2 * BLOCK
    return pl.pallas_call(
        beside_kernel,
        out_shape=(jax.ShapeDtypeStruct((LAB, NQ), bf16), jax.ShapeDtypeStruct((2 * BLOCK, D), bf16)),
        in_specs=[spec()] * 6,
        out_specs=(spec(),) * 2,
        compiler_params=params(),
        cost_estimate=cost(6 * size * D, 4 * size, 2 * size),
        name="beside",
    )(most, q, pos, wb, wb_other, own)


def plane_terms(most, q, pos, wb, wb_other, blocks, kind, into=()):
    size = 2 * LAB * 2 * BLOCK
    resid = jax.ShapeDtypeStruct((LAB, NQ), bf16)
    return pl.pallas_call(
        lambda *refs: plane_kernel(*refs, blocks=blocks),
        out_shape=(resid, resid, jax.ShapeDtypeStruct((2 * BLOCK, D), kind)),
        in_specs=[spec()] * (5 + len(into)),
        out_specs=(spec(),) * 3,
        input_output_aliases={5 + i: i for i in range(len(into))},
        compiler_params=params(),
        cost_estimate=cost(4 * size * D, 4 * size, 2 * size),
        name="plane",
    )(most, q, pos, wb, wb_other, *into)


def terms_kernel(own_ref, other_ref, wb_own, wb_other, out_ref, *, blocks):
    fill_terms(own_ref, other_ref, wb_own, wb_other, out_ref, blocks())


def terms(own, other, wb_own, wb_other, blocks, kind):
    return pl.pallas_call(
        lambda *refs: terms_kernel(*refs, blocks=blocks),
        out_shape=jax.ShapeDtypeStruct((2 * BLOCK, D), kind),
        in_specs=[spec()] * 4,
        out_specs=spec(),
        compiler_params=params(),
        cost_estimate=cost(8 * LAB * BLOCK * D, 4 * 2**20),
        name="terms",
    )(own, other, wb_own, wb_other)


def rest_kernel(most, q_ref, pos_ref, wb_ref, resid_ref, out_ref, *, half):
    blocks = remaining()

    @pl.loop(0, len(blocks) // 2)
    def _(i):
        for k in range(2):
            fill_block(q_ref, pos_ref, wb_ref, resid_ref, half, chosen(blocks, 2 * i + k))

    finish(most, pos_ref, ((half, resid_ref),), blocks)
    fill_grad(resid_ref, q_ref, out_ref)


def rest_gradient(most, q, pos, wb, resid, half):
    size = LAB * 4 * BLOCK
    return pl.pallas_call(
        lambda most, q, pos, wb, old, resid, out: rest_kernel(most, q, pos, wb, resid, out, half=half),
        out_shape=(jax.ShapeDtypeStruct((LAB, NQ), bf16), jax.ShapeDtypeStruct((LAB, D), f32)),
        in_specs=[spec()] * 5,
        out_specs=(spec(),) * 2,
        input_output_aliases={4: 0},
        compiler_params=params(),
        cost_estimate=cost(6 * size * D, 8 * size, 2 * size),
        name="rest",
    )(most, q, pos, wb, resid)[1]


def grad_kernel(resid_ref, q_ref, out_ref):
    fill_grad(resid_ref, q_ref, out_ref)


def gradient(resid, q):
    return pl.pallas_call(
        grad_kernel,
        out_shape=jax.ShapeDtypeStruct((LAB, D), f32),
        in_specs=[spec()] * 2,
        out_specs=spec(),
        compiler_params=params(),
        cost_estimate=cost(2 * LAB * NQ * D, 8 * 2**20),
        name="grad",
    )(resid, q)


def adamw(count, grad, weight, first, second):
    first = beta_one * first + (1.0 - beta_one) * grad
    second = beta_two * second + (1.0 - beta_two) * grad * grad
    first_hat = first * (1.0 / (1.0 - beta_one**count))
    second_hat = second * (1.0 / (1.0 - beta_two**count))
    weight = weight - rate * (first_hat / (jnp.sqrt(second_hat) + epsilon) + decay * weight)
    return weight, first, second


def fill_update(count, ins, outs, start, size):
    @pl.loop(0, size // 64)
    def _(t):
        rows = pl.ds(pl.multiple_of(start + t * 64, 64), 64)
        one, two, weight, first, second = (ref[rows, :] for ref in ins)
        new = adamw(count, one + two, weight, first, second)
        for ref, value in zip(outs, new + new[:1]):
            ref[rows, :] = value.astype(ref.dtype)


def adamw_kernel(count, *refs):
    fill_update(count, refs[:5], refs[5:], 0, LAB)


def last_adamw_kernel(count, *refs):
    ins, outs, held, sems = refs[:5], refs[5:8], refs[8:11], refs[11]
    copies = []
    for i in range(LAB // TILE):
        fill_update(count, ins, held, i * TILE, TILE)
        rows = slice(i * TILE, (i + 1) * TILE)
        for k in range(3):
            copies.append(pltpu.make_async_copy(held[k].at[rows], outs[k].at[rows], sems.at[i, k]))
            copies[-1].start()
    for copy in copies:
        copy.wait()


def update(count, last, *arrays):
    full = jax.ShapeDtypeStruct((LAB, D), f32)
    kernel = last_adamw_kernel if last else adamw_kernel
    held = [pltpu.VMEM((LAB, D), f32)] * 3 + [pltpu.SemaphoreType.DMA((LAB // TILE, 3))]
    return pl.pallas_call(
        lambda *refs: kernel(count, *refs),
        out_shape=(full, full, full) + (() if last else (jax.ShapeDtypeStruct((LAB, D), bf16),)),
        in_specs=[spec()] * 5,
        out_specs=(spec(space=pl.ANY),) * 3 if last else (spec(),) * 4,
        scratch_shapes=held if last else [],
        compiler_params=params(),
        cost_estimate=cost(20 * LAB * D, 12 * LAB * D, 2 * LAB * D),
        name="adamw",
    )(*arrays)


def moved(move):
    pairs = []
    for x in range(NX):
        for y in range(NY):
            for z in range(NZ):
                for core in range(NCORE):
                    tx, ty, tz, tcore = move(x, y, z, core)
                    name = lambda x, y, z, core: (
                        (((x % NX) * NLO + y % NLO) * NZ + z % NZ) * NCORE + core
                    ) * NHI + (y % NY) // NLO
                    pairs.append((name(x, y, z, core), name(tx, ty, tz, tcore)))
    return pairs


def send(array, move):
    return lax.ppermute(array, AXES, moved(move))


def along_x(by):
    return lambda x, y, z, core: (x ^ by, y, z, core)


def along_y(by):
    return lambda x, y, z, core: (x, y ^ by, z, core)


def by_core(zero, one):
    return lambda x, y, z, core: one(x, y, z, core) if core else zero(x, y, z, core)


def onward(by):
    def move(x, y, z, core):
        place = 2 * z + core + (by if core else -by)
        return x, y, place // 2, place % 2

    return move


def back(by):
    moves = {onward(by)(0, 0, z, core)[2] % NZ * 2 + onward(by)(0, 0, z, core)[3]: (z, core) for z in range(NZ) for core in range(2)}
    return lambda x, y, z, core: (x, y, *moves[2 * z + core])


def then(one, two):
    return lambda *at: two(*(i % n for i, n in zip(one(*at), (NX, NY, NZ, NCORE))))


def swap(array):
    return send(array, lambda x, y, z, core: (x, y, z, 1 - core))


def gather(queries, positives):
    line = code(queries, positives)
    line = jnp.concatenate([line] + [send(line, back(by)) for by in (1, 2, 3)], axis=0)
    line = jnp.concatenate([line, send(line, back(4))], axis=0)
    coded = line[:, D : D + 3 * SLOTS].T
    coded = jnp.concatenate([coded[i * SLOTS : (i + 1) * SLOTS] for i in range(3)], axis=1)
    coded = jnp.pad(coded, ((0, 0), (0, D - 3 * LINE)))
    chip = jnp.concatenate([line[:, :D], coded], axis=0)
    four = [chip] + [send(chip, by_core(along_x(by), along_y(by))) for by in (1, 3, 2)]
    four = pack(four)
    return four


def after(array, *others):
    return lax.optimization_barrier((array, *others))


def shards(queries, positives, weights, first_moment, second_moment):
    weight, first, second = weights, first_moment, second_moment
    over_y = by_core(along_y(1), along_y(3))
    first_x = by_core(along_x(1), along_x(3))
    second_x = by_core(along_x(3), along_x(1))

    wb = weight.astype(bf16)
    wb_other = swap(wb)
    four = gather(queries, positives)
    near = [send(four, by_core(along_y(by), along_x(by))) for by in (1, 3)]
    state = first_residuals(four, wb, wb_other, 0, ())
    far, *state = after(four, *state)
    far = send(far, by_core(along_y(LAST), along_x(LAST)))
    for late, part in zip((1, 3), near):
        state = first_residuals(part, wb, wb_other, late, state)
    q, pos, own, other, most, theirs = first_residuals(far, wb, wb_other, LAST, state)
    step0 = (own, other, wb, wb_other)

    part = swap(theirs)
    mine = gradient(own, q)
    out0 = terms(*step0, beside, bf16)
    part, mine, out0 = after(part, mine, out0)
    weight, first, second, wb = update(past_steps + 1, False, mine, part, weight, first, second)

    wb_other = swap(wb)
    wb, out0 = after(wb, out0)
    out0 = send(out0, over_y)
    own = own_beside(most, q, pos, wb)
    wb_other, own = after(wb_other, own)
    other, out1 = beside_terms(most, q, pos, wb, wb_other, own)

    out1, own, other, *step0 = after(out1, own, other, *step0)
    got = [send(out1[:BLOCK], over_y), send(out1[BLOCK:], then(over_y, first_x))]
    part0 = terms(*step0, here, f32)
    out0, part0, own = after(out0, part0, own)
    part0 = part0 + out0.astype(f32)
    half0 = send(part0[BLOCK:].astype(bf16), first_x)
    own, other, part1 = plane_terms(most, q, pos, wb, wb_other, here, f32, (own, other))
    got.append(send(part1[BLOCK:].astype(bf16), first_x))

    part1, part0, other = after(part1, part0, other)
    theirs = rest_gradient(most, q, pos, wb_other, other, 1)
    *got, half0, theirs, own = after(*got, half0, theirs, own)
    part = swap(theirs)
    pair0 = part0[:BLOCK] + half0.astype(f32)
    pair1 = part1[:BLOCK] + got[0].astype(f32) + got[1].astype(f32) + got[2].astype(f32)

    lines = jnp.stack([pair.reshape(2, NZ, ROWS, D) for pair in (pair0, pair1)], axis=2)
    far = lines.astype(bf16)
    got = [send(far[1, :4], second_x), send(far[0, 4:], onward(4)), send(far[1, 4:], then(second_x, onward(4)))]
    lines, own = after(lines, own)
    mine = rest_gradient(most, q, pos, wb, own, 0)
    *got, mine = after(*got, mine)
    line = lines[0, :4] + got[0].astype(f32) + got[1].astype(f32) + got[2].astype(f32)

    got = [send(line[by], onward(by)) for by in (1, 2, 3)]
    line, mine = after(line, mine)
    weight, first, second = update(past_steps + 2, True, mine, part, weight, first, second)
    *got, weight, first, second = after(*got, weight, first, second)
    return weight, first, second, line[0] + got[0] + got[1] + got[2]


def solution(mesh):
    devices = mesh.devices.reshape(NX, NLO, NZ, NCORE, NHI)
    label = AXES[:4]
    in_specs = (P(AXES, None), P(AXES, None), P(label, None), P(label, None), P(label, None))
    out_specs = (P(label, None), P(label, None), P(label, None), P(None, AXES, None))
    return jax.shard_map(
        shards, mesh=Mesh(devices, AXES), in_specs=in_specs, out_specs=out_specs, check_vma=False
    )
```

```python
import jax
import jax.numpy as jnp
from jax import lax
from jax.experimental import pallas as pl
from jax.experimental.pallas import tpu as pltpu
from jax.sharding import Mesh, PartitionSpec as P

STEPS = 2

beta_one = 0.9
beta_two = 0.95
rate = 0.02
decay = 0.1
epsilon = 1e-08
past_steps = 1000

f32 = jnp.float32
bf16 = jnp.bfloat16
i32 = jnp.int32

NX, NLO, NZ, NCORE, NHI = 4, 2, 8, 2, 2
NY = NLO * NHI
AXES = ("x", "ylo", "z", "core", "yhi")
D = 512
ROWS = 16
SLOTS = 8
LINE = NZ * ROWS
NQ = NX * NY * LINE
BLOCK = 2 * LINE
LAB = 1024
TILE = 256
VMEM = 16 * 2**20
LOG2E = 1.4426950408889634


def spec(shape=None, index=None, space=pltpu.VMEM):
    if shape is None:
        return pl.BlockSpec(memory_space=space)
    return pl.BlockSpec(shape, index, memory_space=space)


def params():
    return pltpu.CompilerParams(vmem_limit_bytes=VMEM)


def cost(flops=0, size=0, exps=0):
    return pl.CostEstimate(flops=flops, bytes_accessed=size, transcendentals=exps)


def descending(rows):
    rows = list(rows)
    for a, b in (
        (0, 1), (2, 3), (4, 5), (6, 7), (0, 2), (1, 3), (4, 6), (5, 7), (1, 2), (5, 6),
        (0, 4), (1, 5), (2, 6), (3, 7), (2, 4), (3, 5), (1, 2), (3, 4), (5, 6),
    ):
        rows[a], rows[b] = jnp.maximum(rows[a], rows[b]), jnp.minimum(rows[a], rows[b])
    return rows


def here_is():
    high, core = lax.axis_index("yhi"), lax.axis_index("core")
    chip = (lax.axis_index("x") * NLO + lax.axis_index("ylo")) * NZ + lax.axis_index("z")
    base = chip * NCORE * LAB
    return high, core, base + core * LAB, base + (1 - core) * LAB


def gray(slot):
    return slot ^ (slot >> 1)


def place_of(late, early):
    high, core = here_is()[:2]
    y = late + core * (early - late)
    x = early + core * (late - early)
    return (y ^ (2 * high)) * NX + gray((x + (1 - core) * (4 - 2 * x)) & 3)


def span(late, early):
    return pl.ds(pl.multiple_of(place_of(late, early) * LINE, LINE), LINE)


FAST = 2


def contract_last(left, right):
    return lax.dot_general(left, right, (((1,), (1,)), ((), ())), preferred_element_type=f32)


def contract_first(left, right):
    return lax.dot_general(left, right, (((0,), (0,)), ((), ())), preferred_element_type=f32)


def fill_tile(logits, hits, first):
    share = pl.reciprocal(1.0 + jnp.exp2(logits * -LOG2E), approx=True)
    label = lax.broadcasted_iota(i32, logits.shape, 0) + first
    hit = hits[0] == label
    for row in hits[1:]:
        hit = hit | (row == label)
    return jnp.where(hit, share - 1.0, share).astype(bf16)


def more_hits(count, pos_ref, half, out_ref, at):
    @pl.loop(FAST, count)
    def _(j):
        slots = pos_ref[half, :, at]
        slots = jnp.where(lax.broadcasted_iota(i32, slots.shape, 0) == j, slots, -1)
        hit = jnp.max(slots, axis=0, keepdims=True)

        @pl.loop(0, LAB // TILE)
        def _(t):
            rows = pl.ds(pl.multiple_of(t * TILE, TILE), TILE)
            old = out_ref[rows, at].astype(f32)
            label = lax.broadcasted_iota(i32, old.shape, 0) + t * TILE
            out_ref[rows, at] = jnp.where(hit == label, old - 1.0, old).astype(bf16)


def fill_grad(resid_ref, q_ref, out_ref):
    for t in range(LAB // (2 * TILE)):
        rows = slice(2 * TILE * t, 2 * TILE * (t + 1))
        out_ref[rows, :] = jnp.dot(resid_ref[rows, :], q_ref[...], preferred_element_type=f32)


def part_kernel(part_ref, wb_own, wb_other, *refs, late):
    first_labels = here_is()[2:]
    grads = refs[-1:] if late == LAST else ()
    before = refs[4] if late else None
    q_ref, pos_ref, own_ref, other_ref, most_ref = refs[-5 - len(grads) : len(refs) - len(grads)]
    spans = [span(late, gray(early)) for early in range(4)]
    coded = part_ref[NX * LINE :, : 3 * LINE].astype(f32)
    ids = coded[:, :LINE] + 256.0 * coded[:, LINE : 2 * LINE] + 65536.0 * coded[:, 2 * LINE :]
    ids = ids.astype(i32)
    rows = []
    for j in range(SLOTS):
        row = jnp.concatenate([ids[SLOTS * early + j : SLOTS * early + j + 1] for early in range(4)], axis=0)
        local = jnp.concatenate([row - first for first in first_labels], axis=0)
        rows.append(jnp.where((local >= 0) & (local < LAB), local, -1))
    rows = descending(rows)
    count = sum((row >= 0).astype(f32) for row in rows)
    most = jnp.max(count).astype(i32)
    most_ref[...] = count if before is None else jnp.maximum(count, before[...])
    rows = rows[:1] + [jnp.where(row == last, -1, row) for last, row in zip(rows, rows[1:])]
    for half in range(2):
        for early, at in enumerate(spans):
            k = 4 * half + early
            for j in range(SLOTS):
                pos_ref[half, j : j + 1, at] = rows[j][k : k + 1]

    @pl.loop(0, 2, unroll=late == LAST)
    def _(pair):
        q = part_ref[pl.ds(pl.multiple_of(pair * BLOCK, BLOCK), BLOCK), :]
        ends = [span(late, 3 * pair), span(late, 1 + pair)]
        for half, wb_ref, out_ref in ((1, wb_other, other_ref), (0, wb_own, own_ref)):
            hits = [[pos_ref[half, j : j + 1, at] for j in range(FAST)] for at in ends]
            for t in range(LAB // TILE):
                tile = slice(t * TILE, (t + 1) * TILE)
                logits = contract_last(wb_ref[tile, :], q)
                for k, at in enumerate(ends):
                    out_ref[tile, at] = fill_tile(logits[:, k * LINE : (k + 1) * LINE], hits[k], t * TILE)

    for early, at in enumerate(spans):
        q_ref[at, :] = part_ref[early * LINE : (early + 1) * LINE, :]

    @pl.when(most > FAST)
    def _():
        @pl.loop(0, 4)
        def _(early):
            for half, out_ref in enumerate((own_ref, other_ref)):
                more_hits(most, pos_ref, half, out_ref, span(late, early))

    for out_ref in grads:
        fill_grad(other_ref, q_ref, out_ref)


LAST = 2


def first_residuals(part, wb, wb_other, late, into):
    shapes = (
        jax.ShapeDtypeStruct((NQ, D), bf16),
        jax.ShapeDtypeStruct((2, SLOTS, NQ), i32),
        jax.ShapeDtypeStruct((LAB, NQ), bf16),
        jax.ShapeDtypeStruct((LAB, NQ), bf16),
        jax.ShapeDtypeStruct((2 * NX, LINE), f32),
    )
    if late == LAST:
        shapes += (jax.ShapeDtypeStruct((LAB, D), f32),)
    size = LAB * NX * LINE
    return pl.pallas_call(
        lambda *refs: part_kernel(*refs, late=late),
        out_shape=shapes,
        in_specs=[spec()] * (3 + len(into)),
        out_specs=(spec(),) * len(shapes),
        input_output_aliases={3 + i: i for i in range(len(into))},
        compiler_params=params(),
        cost_estimate=cost((8 if late == LAST else 4) * size * D, 4 * size, 4 * size),
        name="part",
    )(part, wb, wb_other, *into)


def code_kernel(q_ref, pos_ref, out_ref):
    ids = pos_ref[...]
    out_ref[:, :D] = q_ref[...]
    digits = [ids & 255, (ids >> 8) & 255, ids >> 16]
    lane = lax.broadcasted_iota(i32, (SLOTS, LINE), 1) - lax.broadcasted_iota(i32, (SLOTS, LINE), 0)
    coded = jnp.zeros((ROWS, LINE), f32)
    for i, digit in enumerate(digits):
        put = (lane == i * SLOTS).astype(f32).astype(bf16)
        coded = coded + contract_first(digit.astype(f32).astype(bf16), put)
    out_ref[:, D:] = coded.astype(bf16)


def code(queries, positives):
    return pl.pallas_call(
        code_kernel,
        out_shape=jax.ShapeDtypeStruct((ROWS, D + LINE), bf16),
        in_specs=[spec()] * 2,
        out_specs=spec(),
        compiler_params=params(),
        cost_estimate=cost(size=4 * ROWS * D),
        name="code",
    )(queries, positives.T)


def pack_kernel(*refs):
    out_ref = refs[-1]
    for i, ref in enumerate(refs[:-1]):
        out_ref[i * LINE : (i + 1) * LINE, :] = ref[:LINE, :]
    tails = [ref[LINE:, :] for ref in refs[:-1]]
    out_ref[NX * LINE :, :] = jnp.concatenate(tails, axis=0)


def pack(parts):
    return pl.pallas_call(
        pack_kernel,
        out_shape=jax.ShapeDtypeStruct((NX * (LINE + SLOTS), D), bf16),
        in_specs=[spec()] * 4,
        out_specs=spec(),
        compiler_params=params(),
        cost_estimate=cost(size=4 * NX * LINE * D),
        name="pack",
    )(*parts)


def beside():
    high, core = here_is()[:2]
    plane = (1 + 2 * core) ^ (2 * high)
    return [2 * plane, 2 * plane + 1]


def here():
    first = 4 * lax.axis_index("yhi")
    return [first, first + 1]


def remaining():
    return [block ^ 4 for block in beside() + here()]


def chosen(blocks, i):
    block = blocks[0]
    for k in range(1, len(blocks)):
        block = jnp.where(i == k, blocks[k], block)
    return pl.ds(pl.multiple_of(block * BLOCK, BLOCK), BLOCK)


def fill_block(q_ref, pos_ref, wb_ref, out_ref, half, at):
    q = q_ref[at, :]
    hits = [pos_ref[half, j : j + 1, at] for j in range(FAST)]
    for t in range(LAB // TILE):
        rows = slice(t * TILE, (t + 1) * TILE)
        out_ref[rows, at] = fill_tile(contract_last(wb_ref[rows, :], q), hits, t * TILE)


def finish(most, pos_ref, parts, blocks):
    count = jnp.max(most[...]).astype(i32)

    @pl.when(count > FAST)
    def _():
        @pl.loop(0, len(blocks))
        def _(i):
            for half, out_ref in parts:
                more_hits(count, pos_ref, half, out_ref, chosen(blocks, i))


def fill_terms(own_ref, other_ref, wb_own, wb_other, out_ref, blocks):
    @pl.loop(0, len(blocks))
    def _(i):
        at = chosen(blocks, i)
        first = contract_first(own_ref[:, at], wb_own[...])
        second = contract_first(other_ref[:, at], wb_other[...])
        rows = pl.ds(pl.multiple_of(i * BLOCK, BLOCK), BLOCK)
        out_ref[rows, :] = (first + second).astype(out_ref.dtype)


def plane_kernel(most, q_ref, pos_ref, wb_own, wb_other, *refs, blocks):
    own_ref, other_ref, out_ref = refs[-3:]
    blocks = blocks()

    @pl.loop(0, len(blocks))
    def _(i):
        at = chosen(blocks, i)
        fill_block(q_ref, pos_ref, wb_own, own_ref, 0, at)
        fill_block(q_ref, pos_ref, wb_other, other_ref, 1, at)

    finish(most, pos_ref, ((0, own_ref), (1, other_ref)), blocks)
    fill_terms(own_ref, other_ref, wb_own, wb_other, out_ref, blocks)


def plane_terms(most, q, pos, wb, wb_other, blocks, kind, into=()):
    size = 2 * LAB * 2 * BLOCK
    resid = jax.ShapeDtypeStruct((LAB, NQ), bf16)
    return pl.pallas_call(
        lambda *refs: plane_kernel(*refs, blocks=blocks),
        out_shape=(resid, resid, jax.ShapeDtypeStruct((2 * BLOCK, D), kind)),
        in_specs=[spec()] * (5 + len(into)),
        out_specs=(spec(),) * 3,
        input_output_aliases={5 + i: i for i in range(len(into))},
        compiler_params=params(),
        cost_estimate=cost(4 * size * D, 4 * size, 2 * size),
        name="plane",
    )(most, q, pos, wb, wb_other, *into)


def terms_kernel(own_ref, other_ref, wb_own, wb_other, out_ref, *, blocks):
    fill_terms(own_ref, other_ref, wb_own, wb_other, out_ref, blocks())


def terms(own, other, wb_own, wb_other, blocks, kind):
    return pl.pallas_call(
        lambda *refs: terms_kernel(*refs, blocks=blocks),
        out_shape=jax.ShapeDtypeStruct((2 * BLOCK, D), kind),
        in_specs=[spec()] * 4,
        out_specs=spec(),
        compiler_params=params(),
        cost_estimate=cost(8 * LAB * BLOCK * D, 4 * 2**20),
        name="terms",
    )(own, other, wb_own, wb_other)


def rest_kernel(most, q_ref, pos_ref, wb_ref, resid_ref, out_ref, *, half):
    blocks = remaining()

    @pl.loop(0, len(blocks) // 2)
    def _(i):
        for k in range(2):
            fill_block(q_ref, pos_ref, wb_ref, resid_ref, half, chosen(blocks, 2 * i + k))

    finish(most, pos_ref, ((half, resid_ref),), blocks)
    fill_grad(resid_ref, q_ref, out_ref)


def rest_gradient(most, q, pos, wb, resid, half):
    size = LAB * 4 * BLOCK
    return pl.pallas_call(
        lambda most, q, pos, wb, old, resid, out: rest_kernel(most, q, pos, wb, resid, out, half=half),
        out_shape=(jax.ShapeDtypeStruct((LAB, NQ), bf16), jax.ShapeDtypeStruct((LAB, D), f32)),
        in_specs=[spec()] * 5,
        out_specs=(spec(),) * 2,
        input_output_aliases={4: 0},
        compiler_params=params(),
        cost_estimate=cost(6 * size * D, 8 * size, 2 * size),
        name="rest",
    )(most, q, pos, wb, resid)[1]


def grad_kernel(resid_ref, q_ref, out_ref):
    fill_grad(resid_ref, q_ref, out_ref)


def gradient(resid, q):
    return pl.pallas_call(
        grad_kernel,
        out_shape=jax.ShapeDtypeStruct((LAB, D), f32),
        in_specs=[spec()] * 2,
        out_specs=spec(),
        compiler_params=params(),
        cost_estimate=cost(2 * LAB * NQ * D, 8 * 2**20),
        name="grad",
    )(resid, q)


def adamw(count, grad, weight, first, second):
    first = beta_one * first + (1.0 - beta_one) * grad
    second = beta_two * second + (1.0 - beta_two) * grad * grad
    first_hat = first * (1.0 / (1.0 - beta_one**count))
    second_hat = second * (1.0 / (1.0 - beta_two**count))
    weight = weight - rate * (first_hat / (jnp.sqrt(second_hat) + epsilon) + decay * weight)
    return weight, first, second


def fill_update(count, ins, outs, start, size):
    @pl.loop(0, size // 64)
    def _(t):
        rows = pl.ds(pl.multiple_of(start + t * 64, 64), 64)
        one, two, weight, first, second = (ref[rows, :] for ref in ins)
        new = adamw(count, one + two, weight, first, second)
        for ref, value in zip(outs, new + new[:1]):
            ref[rows, :] = value.astype(ref.dtype)


def adamw_kernel(count, *refs):
    fill_update(count, refs[:5], refs[5:], 0, LAB)


def last_adamw_kernel(count, *refs):
    ins, outs, held, sems = refs[:5], refs[5:8], refs[8:11], refs[11]
    copies = []
    for i in range(LAB // TILE):
        fill_update(count, ins, held, i * TILE, TILE)
        rows = slice(i * TILE, (i + 1) * TILE)
        for k in range(3):
            copies.append(pltpu.make_async_copy(held[k].at[rows], outs[k].at[rows], sems.at[i, k]))
            copies[-1].start()
    for copy in copies:
        copy.wait()


def update(count, last, *arrays):
    full = jax.ShapeDtypeStruct((LAB, D), f32)
    kernel = last_adamw_kernel if last else adamw_kernel
    held = [pltpu.VMEM((LAB, D), f32)] * 3 + [pltpu.SemaphoreType.DMA((LAB // TILE, 3))]
    return pl.pallas_call(
        lambda *refs: kernel(count, *refs),
        out_shape=(full, full, full) + (() if last else (jax.ShapeDtypeStruct((LAB, D), bf16),)),
        in_specs=[spec()] * 5,
        out_specs=(spec(space=pl.ANY),) * 3 if last else (spec(),) * 4,
        scratch_shapes=held if last else [],
        compiler_params=params(),
        cost_estimate=cost(20 * LAB * D, 12 * LAB * D, 2 * LAB * D),
        name="adamw",
    )(*arrays)


def moved(move):
    pairs = []
    for x in range(NX):
        for y in range(NY):
            for z in range(NZ):
                for core in range(NCORE):
                    tx, ty, tz, tcore = move(x, y, z, core)
                    name = lambda x, y, z, core: (
                        (((x % NX) * NLO + y % NLO) * NZ + z % NZ) * NCORE + core
                    ) * NHI + (y % NY) // NLO
                    pairs.append((name(x, y, z, core), name(tx, ty, tz, tcore)))
    return pairs


def send(array, move):
    return lax.ppermute(array, AXES, moved(move))


def along_x(by):
    return lambda x, y, z, core: (x ^ by, y, z, core)


def along_y(by):
    return lambda x, y, z, core: (x, y ^ by, z, core)


def by_core(zero, one):
    return lambda x, y, z, core: one(x, y, z, core) if core else zero(x, y, z, core)


def onward(by):
    def move(x, y, z, core):
        place = 2 * z + core + (by if core else -by)
        return x, y, place // 2, place % 2

    return move


def back(by):
    moves = {onward(by)(0, 0, z, core)[2] % NZ * 2 + onward(by)(0, 0, z, core)[3]: (z, core) for z in range(NZ) for core in range(2)}
    return lambda x, y, z, core: (x, y, *moves[2 * z + core])


def then(one, two):
    return lambda *at: two(*(i % n for i, n in zip(one(*at), (NX, NY, NZ, NCORE))))


def swap(array):
    return send(array, lambda x, y, z, core: (x, y, z, 1 - core))


def gather(queries, positives):
    line = code(queries, positives)
    line = jnp.concatenate([line] + [send(line, back(by)) for by in (1, 2, 3)], axis=0)
    line = jnp.concatenate([line, send(line, back(4))], axis=0)
    coded = line[:, D : D + 3 * SLOTS].T
    coded = jnp.concatenate([coded[i * SLOTS : (i + 1) * SLOTS] for i in range(3)], axis=1)
    coded = jnp.pad(coded, ((0, 0), (0, D - 3 * LINE)))
    chip = jnp.concatenate([line[:, :D], coded], axis=0)
    four = [chip] + [send(chip, by_core(along_x(by), along_y(by))) for by in (1, 3, 2)]
    four = pack(four)
    return four


def after(array, *others):
    return lax.optimization_barrier((array, *others))


def shards(queries, positives, weights, first_moment, second_moment):
    weight, first, second = weights, first_moment, second_moment
    over_y = by_core(along_y(1), along_y(3))
    first_x = by_core(along_x(1), along_x(3))
    second_x = by_core(along_x(3), along_x(1))

    wb = weight.astype(bf16)
    wb_other = swap(wb)
    four = gather(queries, positives)
    near = [send(four, by_core(along_y(by), along_x(by))) for by in (1, 3)]
    state = first_residuals(four, wb, wb_other, 0, ())
    far, *state = after(four, *state)
    far = send(far, by_core(along_y(LAST), along_x(LAST)))
    for late, part in zip((1, 3), near):
        state = first_residuals(part, wb, wb_other, late, state)
    q, pos, own, other, most, theirs = first_residuals(far, wb, wb_other, LAST, state)
    step0 = (own, other, wb, wb_other)

    part = swap(theirs)
    mine = gradient(own, q)
    out0 = terms(*step0, beside, bf16)
    part, mine, out0 = after(part, mine, out0)
    weight, first, second, wb = update(past_steps + 1, False, mine, part, weight, first, second)

    wb_other = swap(wb)
    wb, out0, *step0 = after(wb, out0, *step0)
    out0 = send(out0, over_y)
    part0 = terms(*step0, here, f32)
    wb_other, part0 = after(wb_other, part0)
    own, other, out1 = plane_terms(most, q, pos, wb, wb_other, beside, bf16)

    out1, own, other = after(out1, own, other)
    got = [send(out1[:BLOCK], over_y), send(out1[BLOCK:], then(over_y, first_x))]
    own, other, part1 = plane_terms(most, q, pos, wb, wb_other, here, f32, (own, other))
    out0, part1 = after(out0, part1)
    got.append(send(part1[BLOCK:].astype(bf16), first_x))
    part0 = part0 + out0.astype(f32)
    half0 = send(part0[BLOCK:].astype(bf16), first_x)

    part1, part0, other = after(part1, part0, other)
    theirs = rest_gradient(most, q, pos, wb_other, other, 1)
    *got, half0, theirs, own = after(*got, half0, theirs, own)
    part = swap(theirs)
    pair0 = part0[:BLOCK] + half0.astype(f32)
    pair1 = part1[:BLOCK] + got[0].astype(f32) + got[1].astype(f32) + got[2].astype(f32)

    lines = jnp.stack([pair.reshape(2, NZ, ROWS, D) for pair in (pair0, pair1)], axis=2)
    far = lines.astype(bf16)
    got = [send(far[1, :4], second_x), send(far[0, 4:], onward(4)), send(far[1, 4:], then(second_x, onward(4)))]
    lines, own = after(lines, own)
    mine = rest_gradient(most, q, pos, wb, own, 0)
    *got, mine = after(*got, mine)
    line = lines[0, :4] + got[0].astype(f32) + got[1].astype(f32) + got[2].astype(f32)

    got = [send(line[by], onward(by)) for by in (1, 2, 3)]
    line, mine = after(line, mine)
    weight, first, second = update(past_steps + 2, True, mine, part, weight, first, second)
    *got, weight, first, second = after(*got, weight, first, second)
    return weight, first, second, line[0] + got[0] + got[1] + got[2]


def solution(mesh):
    devices = mesh.devices.reshape(NX, NLO, NZ, NCORE, NHI)
    label = AXES[:4]
    in_specs = (P(AXES, None), P(AXES, None), P(label, None), P(label, None), P(label, None))
    out_specs = (P(label, None), P(label, None), P(label, None), P(None, AXES, None))
    return jax.shard_map(
        shards, mesh=Mesh(devices, AXES), in_specs=in_specs, out_specs=out_specs, check_vma=False
    )
```
